32 devices in a mesh: dp: 16 (over z, y, core), qry: 2 (over x).
Axes of the slice: x: 2, y: 2, z: 4, core: 2. Of those that a mesh axis runs over, the one named last changes fastest.
Arguments:
- queries: bfloat16 [16, 128, 768], P('dp', 'qry'), may hold values from -6 to 6
- latents: bfloat16 [16, 128, 768], P('dp', 'qry'), may hold values from -6 to 6
- positions: int32 [16, 128], P('dp', 'qry'), may hold values from 0 to 195
- visible_valid: int32 [16, 128], P('dp'), may hold values from 0 to 1, as said below
- masked_valid: int32 [16, 128], P('dp'), may hold values from 0 to 1, as said below
- w_query: bfloat16 [768, 768], replicated, may hold values from -0.3125 to 0.3125
- b_query: float32 [768], replicated, may hold values from -3 to 3
- w_key: bfloat16 [768, 768], replicated, may hold values from -0.21875 to 0.21875
- w_value: bfloat16 [768, 768], replicated, may hold values from -0.21875 to 0.21875
- b_value: float32 [768], replicated, may hold values from -3 to 3
- w_out: bfloat16 [768, 768], replicated, may hold values from -0.875 to 0.875
- b_out: float32 [768], replicated, may hold values from -3 to 3
- w_fc1: bfloat16 [768, 3072], replicated, may hold values from -0.21875 to 0.21875
- b_fc1: float32 [3072], replicated, may hold values from -3 to 3
- w_fc2: bfloat16 [3072, 768], replicated, may hold values from -0.109375 to 0.109375
- b_fc2: float32 [768], replicated, may hold values from -3 to 3
- gain_query: float32 [768], replicated, may hold values from 0.25 to 1.75
- shift_query: float32 [768], replicated, may hold values from -2 to 2
- gain_keys: float32 [768], replicated, may hold values from 0.25 to 1.75
- shift_keys: float32 [768], replicated, may hold values from -2 to 2
- gain_mlp: float32 [768], replicated, may hold values from 0.25 to 1.75
- shift_mlp: float32 [768], replicated, may hold values from -2 to 2
- scale_attn: float32 [768], replicated, may hold values from 0.25 to 1.75
- scale_mlp: float32 [768], replicated, may hold values from 0.25 to 1.75
- out_grad: bfloat16 [16, 128, 768], P('dp', 'qry'), may hold values from -6 to 6
Outputs:
- block_out: bfloat16 [16, 128, 768], P('dp', 'qry')
- grad_queries: float32 [16, 128, 768], P('dp', 'qry')
- grad_latents: float32 [16, 128, 768], P('dp', 'qry')
- grad_w_query: float32 [768, 768], P('dp', 'qry')
- grad_b_query: float32 [768], replicated
- grad_w_key: float32 [768, 768], P('dp', 'qry')
- grad_w_value: float32 [768, 768], P('dp', 'qry')
- grad_b_value: float32 [768], replicated
- grad_w_out: float32 [768, 768], P('dp', 'qry')
- grad_b_out: float32 [768], replicated
- grad_w_fc1: float32 [768, 3072], P('dp', 'qry')
- grad_b_fc1: float32 [3072], replicated
- grad_w_fc2: float32 [3072, 768], P('dp', 'qry')
- grad_b_fc2: float32 [768], replicated
- grad_gain_query: float32 [768], replicated
- grad_shift_query: float32 [768], replicated
- grad_gain_keys: float32 [768], replicated
- grad_shift_keys: float32 [768], replicated
- grad_gain_mlp: float32 [768], replicated
- grad_shift_mlp: float32 [768], replicated
- grad_scale_attn: float32 [768], replicated
- grad_scale_mlp: float32 [768], replicated
The draws below stay inside these ranges and needn't reach their ends.
Inputs may be any that keep to these rules, and one draw needn't show every extreme that they name: `visible_valid`: in every image the valid visible slots form a leading run of more than 64 slots. `masked_valid`: in every image the valid masked slots form a leading run of more than 64 slots.
All inputs are finite; a program needn't handle non-finite values.
Results may differ from the reference program's by a relative error of at most 0.014.
The reference program's roundings to bfloat16 on the way count: a program that leaves them out, or rounds other values in their place, can miss the bound.
Values may be sent and summed in bfloat16 or wider, within the bound.
A program may use at most 128 MiB of HBM per device.

```python
import math
import jax
import jax.numpy as jnp
from jax import lax

D = 768
HEADS = 12
HEAD_DIM = 64
FF = 3072
VIS = 128
MSK = 128
PATCHES = 196
IMAGES = 16


def draw_visible_valid(key, part):
    key = jax.random.fold_in(key, 11)
    counts = jax.random.randint(key, (IMAGES, 1), VIS // 2 + 1, VIS + 1)
    slots = jnp.arange(VIS, dtype=jnp.int32)[None, :]
    return (slots < counts).astype(jnp.int32)


def draw_masked_valid(key, part):
    key = jax.random.fold_in(key, 23)
    counts = jax.random.randint(key, (IMAGES, 1), MSK // 2 + 1, MSK + 1)
    slots = jnp.arange(MSK, dtype=jnp.int32)[None, :]
    return (slots < counts).astype(jnp.int32)


def place_ends(drawn, own_key, smallest, high):
    index_at = [jax.random.randint(jax.random.fold_in(own_key, axis), (), 0, length) for axis, length in enumerate(drawn.shape)]
    widest = drawn.shape.index(max(drawn.shape))
    neighbour = index_at[:widest] + [(index_at[widest] + 1) % drawn.shape[widest]] + index_at[widest + 1:]
    return drawn.at[tuple(index_at)].set(smallest).at[tuple(neighbour)].set(high)


def shard_levels(own_key, dims, cuts, smallest, largest):
    def one(axis_at, parts):
        draws = jax.random.uniform(jax.random.fold_in(jax.random.fold_in(own_key, 6), axis_at), (parts,), jnp.float32, smallest / len(cuts), largest / len(cuts))
        return jnp.repeat(jnp.exp(draws), dims[axis_at] // parts).reshape((-1,) + (1,) * (len(dims) - axis_at - 1))

    level = one(*cuts[0])
    for cut in cuts[1:]:
        level = level * one(*cut)
    return level


def normal_values(stream_key, shape, scale, limit, shards=(), held_as=jnp.bfloat16):
    values = jax.random.normal(stream_key, shape, jnp.float32) * scale
    if len(shards) > 0:
        values = shard_levels(stream_key, shape, shards, -0.22, 0.18) * values
    return jnp.clip(values, min=-limit, max=limit).astype(held_as)


def setup_inputs(seed: int = 0) -> dict:
    splits = jax.random.split(jax.random.key(seed), 26)
    queries = normal_values(splits[0], (IMAGES, MSK, D), 1.0, 6.0, ((0, 16), (1, 2)))
    latents = normal_values(splits[1], (IMAGES, VIS, D), 1.0, 6.0, ((0, 16), (1, 2)))
    positions = place_ends(jax.random.randint(splits[2], (IMAGES, MSK), 0, PATCHES), jax.random.fold_in(splits[2], 1), 0, PATCHES - 1).astype(jnp.int32)
    visible_valid = draw_visible_valid(jax.random.fold_in(splits[25], 71), 0)
    masked_valid = draw_masked_valid(jax.random.fold_in(splits[25], 71), 0)
    w_query = normal_values(splits[5], (D, D), (D // 2) ** -0.5, 0.3125)
    b_query = normal_values(splits[6], (D,), 0.5, 3.0, (), jnp.float32)
    w_key = normal_values(splits[7], (D, D), D ** -0.5, 0.21875)
    w_value = normal_values(splits[8], (D, D), D ** -0.5, 0.21875)
    b_value = normal_values(splits[9], (D,), 0.5, 3.0, (), jnp.float32)
    w_out = normal_values(splits[10], (D, D), (D // 16) ** -0.5, 0.875)
    b_out = normal_values(splits[11], (D,), 0.5, 3.0, (), jnp.float32)
    w_fc1 = normal_values(splits[12], (D, FF), D ** -0.5, 0.21875)
    b_fc1 = normal_values(splits[13], (FF,), 0.5, 3.0, (), jnp.float32)
    w_fc2 = normal_values(splits[14], (FF, D), FF ** -0.5, 0.109375)
    b_fc2 = normal_values(splits[15], (D,), 0.5, 3.0, (), jnp.float32)
    gain_query = jnp.clip(1.0 + 0.15 * jax.random.normal(splits[16], (D,), jnp.float32), 0.25, 1.75)
    shift_query = normal_values(splits[17], (D,), 0.3, 2.0, (), jnp.float32)
    gain_keys = jnp.clip(1.0 + 0.15 * jax.random.normal(splits[18], (D,), jnp.float32), 0.25, 1.75)
    shift_keys = normal_values(splits[19], (D,), 0.3, 2.0, (), jnp.float32)
    gain_mlp = jnp.clip(1.0 + 0.15 * jax.random.normal(splits[20], (D,), jnp.float32), 0.25, 1.75)
    shift_mlp = normal_values(splits[21], (D,), 0.3, 2.0, (), jnp.float32)
    scale_attn = jnp.clip(1.0 + 0.15 * jax.random.normal(splits[22], (D,), jnp.float32), 0.25, 1.75)
    scale_mlp = jnp.clip(1.0 + 0.15 * jax.random.normal(splits[23], (D,), jnp.float32), 0.25, 1.75)
    out_grad = normal_values(splits[24], (IMAGES, MSK, D), 1.0, 6.0, ((0, 16), (1, 2)))
    return {"queries": queries, "latents": latents, "positions": positions, "visible_valid": visible_valid, "masked_valid": masked_valid, "w_query": w_query, "b_query": b_query, "w_key": w_key, "w_value": w_value, "b_value": b_value, "w_out": w_out, "b_out": b_out, "w_fc1": w_fc1, "b_fc1": b_fc1, "w_fc2": w_fc2, "b_fc2": b_fc2, "gain_query": gain_query, "shift_query": shift_query, "gain_keys": gain_keys, "shift_keys": shift_keys, "gain_mlp": gain_mlp, "shift_mlp": shift_mlp, "scale_attn": scale_attn, "scale_mlp": scale_mlp, "out_grad": out_grad}


@jax.custom_vjp
def low(v):
    return lax.optimization_barrier(v.astype(jnp.bfloat16)).astype(jnp.float32)

@jax.custom_vjp
def low_back(v):
    return v

def low_keep(v):
    return (low(v), None)

def low_pass(kept, grad):
    return (grad,)

def back_keep(v):
    return (v, None)

def back_low(kept, grad):
    return (low(grad),)
low.defvjp(low_keep, low_pass)
low_back.defvjp(back_keep, back_low)

def sinusoid(places, width):
    index = jnp.arange(width)
    freq = jnp.exp(-(2.0 * (index // 2).astype(jnp.float32) / width) * math.log(10000.0))
    angle = places.astype(jnp.float32)[..., None] * freq
    return jnp.where(index % 2 == 0, jnp.sin(angle), jnp.cos(angle))

def layer_norm(x, gain, shift):
    centre = x - lax.optimization_barrier(jnp.mean(x, axis=-1, keepdims=True))
    spread = lax.optimization_barrier(jnp.mean(centre * centre, axis=-1, keepdims=True))
    return centre * lax.rsqrt(spread + 1e-06) * gain + shift

def matmul(left, weight):
    return jnp.einsum('bnd,df->bnf', left, weight, precision=lax.Precision.HIGHEST)

def forward(queries, latents, places, vis_ok, msk_ok, params):
    w_query, b_query, w_key, w_value, b_value, w_out, b_out, w_fc1, b_fc1, w_fc2, b_fc2, gain_query, shift_query, gain_keys, shift_keys, gain_mlp, shift_mlp, scale_attn, scale_mlp = params
    batch = queries.shape[0]
    qin = queries + sinusoid(places, D)
    source = jnp.concatenate([latents, qin], axis=1)
    hq = low(layer_norm(qin, gain_query, shift_query))
    hk = low(layer_norm(source, gain_keys, shift_keys))
    query = low(low_back(matmul(hq, w_query) + b_query)).reshape(batch, MSK, HEADS, HEAD_DIM)
    keys = low(low_back(matmul(hk, w_key))).reshape(batch, VIS + MSK, HEADS, HEAD_DIM)
    values = low(low_back(matmul(hk, w_value) + b_value)).reshape(batch, VIS + MSK, HEADS, HEAD_DIM)
    raw = jnp.einsum('bmhe,bkhe->bhmk', query, keys, precision=lax.Precision.HIGHEST) * (1.0 / math.sqrt(HEAD_DIM))
    scores = low_back(raw)
    keymask = jnp.concatenate([vis_ok, msk_ok], axis=1) > 0
    scores = jnp.where(keymask[:, None, None, :], scores, -1e+30)
    probs = low(jax.nn.softmax(scores, axis=-1))
    attended = jnp.einsum('bhmk,bkhe->bmhe', probs, values, precision=lax.Precision.HIGHEST)
    attended = low(low_back(attended.reshape(batch, MSK, D)))
    branch = low_back(matmul(attended, w_out) + b_out)
    resid = qin + scale_attn * branch
    h_two = low(layer_norm(resid, gain_mlp, shift_mlp))
    pre_act = low_back(matmul(h_two, w_fc1) + b_fc1)
    act = low(jax.nn.gelu(pre_act, approximate=False))
    mlp_out = low_back(matmul(act, w_fc2) + b_fc2)
    return resid + scale_mlp * mlp_out

def reference(queries, latents, positions, visible_valid, masked_valid, w_query, b_query, w_key, w_value, b_value, w_out, b_out, w_fc1, b_fc1, w_fc2, b_fc2, gain_query, shift_query, gain_keys, shift_keys, gain_mlp, shift_mlp, scale_attn, scale_mlp, out_grad):
    params = tuple((p.astype(jnp.float32) for p in (w_query, b_query, w_key, w_value, b_value, w_out, b_out, w_fc1, b_fc1, w_fc2, b_fc2, gain_query, shift_query, gain_keys, shift_keys, gain_mlp, shift_mlp, scale_attn, scale_mlp)))
    group = math.gcd(IMAGES, 16)
    blocks = IMAGES // group

    def split(a):
        return a.reshape((blocks, group) + a.shape[1:])

    def step(total, item):
        q_blk, l_blk, p_blk, vis_blk, msk_blk, dy_blk = item

        def run(q_in, l_in, prm):
            return forward(q_in, l_in, p_blk, vis_blk, msk_blk, prm)
        result, pull = jax.vjp(run, q_blk.astype(jnp.float32), l_blk.astype(jnp.float32), params)
        d_q, d_l, d_p = pull(dy_blk.astype(jnp.float32))
        total = jax.tree.map(jnp.add, total, d_p)
        return (total, (result.astype(jnp.bfloat16), d_q, d_l))
    zeros = jax.tree.map(jnp.zeros_like, params)
    totals, (outs, d_queries, d_latents) = lax.scan(step, zeros, (split(queries), split(latents), split(positions), split(visible_valid), split(masked_valid), split(out_grad)))
    block_out = outs.reshape(IMAGES, MSK, D)
    return (block_out, d_queries.reshape(IMAGES, MSK, D), d_latents.reshape(IMAGES, VIS, D), totals[0], totals[1], totals[2], totals[3], totals[4], totals[5], totals[6], totals[7], totals[8], totals[9], totals[10], totals[11], totals[12], totals[13], totals[14], totals[15], totals[16], totals[17], totals[18])
```

```python
import functools
import math
import types

import jax
import jax.numpy as jnp
from jax import lax
from jax.experimental import pallas as pl
from jax.experimental.pallas import tpu as pltpu
from jax.sharding import PartitionSpec as P

HEAD_DIM = 64
MESH = pl.DeviceIdType.MESH
F32 = jnp.float32
BF16 = jnp.bfloat16
GROUPS = 16
Z_ORDER = (0, 2, 1, 3)


def dot(a, b):
    return lax.dot_general(a, b, (((1,), (0,)), ((), ())), preferred_element_type=F32)


def dot_t(a, b):
    return lax.dot_general(a, b, (((1,), (1,)), ((), ())), preferred_element_type=F32)


def col_sum(a):
    return jnp.sum(a, axis=0, keepdims=True)


def normalise(v):
    centre = v - jnp.mean(v, axis=-1, keepdims=True)
    spread = jnp.mean(centre * centre, axis=-1, keepdims=True)
    inv = lax.rsqrt(spread + 1e-06)
    return centre * inv, inv


def normalise_back(grad_hat, hat, inv):
    m1 = jnp.mean(grad_hat, axis=-1, keepdims=True)
    m2 = jnp.mean(grad_hat * hat, axis=-1, keepdims=True)
    return inv * (grad_hat - m1 - hat * m2)


def sinusoid(places, width):
    index = lax.broadcasted_iota(jnp.int32, (1, width), 1)
    half = index // 2
    freq = jnp.exp(-(2.0 * half.astype(F32) / width) * math.log(10000.0))
    odd = (index - 2 * half).astype(F32)
    angle = places * freq
    turns = jnp.floor(angle * (2.0 / math.pi) + 0.5)
    rest = angle - turns * 1.5703125
    rest = rest - turns * 4.8351287841796875e-4
    rest = rest - turns * 3.1385570764541626e-07
    sq = rest * rest
    sine = rest * (
        1.0 + sq * (-1.0 / 6 + sq * (1.0 / 120 + sq * (-1.0 / 5040 + sq * (1.0 / 362880))))
    )
    cosine = 1.0 + sq * (-0.5 + sq * (1.0 / 24 + sq * (-1.0 / 720 + sq * (1.0 / 40320))))
    quarter = turns + odd
    pairs = jnp.floor(quarter * 0.5)
    parity = quarter - 2.0 * pairs
    flips = pairs - 2.0 * jnp.floor(pairs * 0.5)
    value = jnp.where(parity > 0.5, cosine, sine)
    return jnp.where(flips > 0.5, -value, value)


def kernel(
    shape,
    queries, latents, positions, vis_ok, msk_ok, dy_in,
    w_query, w_key, w_value, w_out, w_fc1, w_fc2,
    b_query, b_value, b_out, b_fc1, b_fc2,
    gain_q, shift_q, gain_k, shift_k, gain_m, shift_m, scale_a, scale_m,
    out_block, out_dq, out_dl, out_wq, out_wk, out_wv, out_wo, out_w1, out_w2, out_vec,
    s,
):
    s = types.SimpleNamespace(**s)
    rows, width, ff, share = shape
    (b_query, b_value, b_out, b_fc1, b_fc2, gain_q, shift_q, gain_k, shift_k, gain_m, shift_m,
     scale_a, scale_m) = (
        ref[...].reshape(1, -1)
        for ref in (b_query, b_value, b_out, b_fc1, b_fc2, gain_q, shift_q, gain_k, shift_k, gain_m,
                    shift_m, scale_a, scale_m)
    )
    half = width // 2
    heads = half // HEAD_DIM
    blk = width // GROUPS
    fblk = ff // GROUPS
    nb = ff // half
    scale = 1.0 / math.sqrt(HEAD_DIM)

    x = lax.axis_index("qry")
    place = lax.axis_index("dp")
    n = place // share
    low = place - n * share
    z = n // 4
    y = (n // 2) % 2
    c = n % 2
    zs = (z, z + 1 - 2 * (z % 2), (z + 2) % 4, 3 - z)

    def dev(zz, yy, cc, xx):
        return (((zz * 2 + yy) * 2 + cc) * share + low, xx)

    PX = dev(z, y, c, 1 - x)
    PY = dev(z, 1 - y, c, x)
    PXY = dev(z, 1 - y, c, 1 - x)
    PC = dev(z, y, 1 - c, x)
    PZ = {t: dev(zs[t], y, c, x) for t in (1, 2, 3)}

    def remote(src, dst, i, peer):
        return pltpu.make_async_remote_copy(
            src_ref=src, dst_ref=dst, send_sem=s.send.at[i], recv_sem=s.recv.at[i],
            device_id=peer, device_id_type=MESH,
        )

    counter = [0]
    sent = []

    def new():
        counter[0] += 1
        return counter[0] - 1

    def push(src, dst, peer, landing=None):
        i = new()
        copy = remote(src, dst, i, peer)
        copy.start()
        sent.append(copy)
        arrival = copy if landing is None else remote(src, landing, i, peer)
        return arrival.wait_recv

    loads = []

    def load(src, dst):
        copy = pltpu.make_async_copy(src, dst, s.load.at[len(loads)])
        copy.start()
        loads.append(copy)
        return copy.wait

    own = pl.ds(pl.multiple_of(x * rows, rows), rows)
    other = pl.ds(pl.multiple_of((1 - x) * rows, rows), rows)
    mine = pl.ds(pl.multiple_of(x * half, half), half)
    theirs = pl.ds(pl.multiple_of((1 - x) * half, half), half)
    load_dy = load(dy_in.at[0], s.dy)
    load_q = load(queries.at[0], s.qraw.at[own])
    load_l = load(latents.at[0], s.lraw.at[own])
    load_w2 = load(w_fc2, s.w2)
    load_wk = load(w_key.at[:, mine], s.wk)
    load_wv = load(w_value.at[:, mine], s.wv)
    load_wq = load(w_query.at[:, mine], s.wq)
    load_wo = load(w_out, s.wo)
    load_w1 = load(w_fc1, s.w1)

    barrier = pltpu.get_barrier_semaphore()
    peers = [PX, PY, PXY, PC, PZ[1], PZ[2], PZ[3]]
    for peer in peers:
        pl.semaphore_signal(barrier, inc=1, device_id=peer, device_id_type=MESH)
    pl.semaphore_wait(barrier, len(peers))

    got_q = push(queries.at[0], s.qraw.at[own], PX, s.qraw.at[other])
    got_p = push(positions, s.ppos, PX)
    got_l = push(latents.at[0], s.lraw.at[own], PX, s.lraw.at[other])

    load_dy()
    dy = s.dy[...].astype(F32)
    d_mlp = (scale_m * dy).astype(BF16)
    s.vec[4:5, :] = col_sum(d_mlp.astype(F32))
    for xx in range(2):
        s.dm_s[xx] = d_mlp[:, xx * half:(xx + 1) * half]
    got_dm = [
        push(s.dm_s.at[x], s.dm_g.at[1], PY),
        push(s.dm_s.at[1 - x], s.dm_g.at[2], PX),
        push(s.dm_s.at[1 - x], s.dm_g.at[3], PXY),
    ]
    s.dm_g[0] = s.dm_s[x]

    eye = lax.broadcasted_iota(jnp.int32, (rows, rows), 0) == lax.broadcasted_iota(
        jnp.int32, (rows, rows), 1
    )

    def own_half(pos_ref, at, low_at):
        row = jnp.broadcast_to(pos_ref[...].astype(F32), (rows, rows))
        places = jnp.sum(jnp.where(eye, row, 0.0), axis=1, keepdims=True)
        qin = s.qraw[at, :].astype(F32) + sinusoid(places, width)
        hat, inv = normalise(qin)
        s.hat[low_at, :] = hat
        hq = (hat * gain_q + shift_q).astype(BF16)
        hkq = (hat * gain_k + shift_k).astype(BF16)
        s.hq[at, :] = hq
        s.hk[low_at, :] = hkq
        return qin, hat, inv, hq, hkq

    def lat_half(at):
        hat, inv = normalise(s.lraw[at, :].astype(F32))
        s.hat[at, :] = hat
        hkl = (hat * gain_k + shift_k).astype(BF16)
        s.hk[at, :] = hkl
        return hat, inv, hkl

    def project(hq, hkq, hkl, at, low_at):
        both = jnp.concatenate([hkl, hkq], axis=0)
        k = dot(both, s.wk[...]).astype(BF16)
        s.k[at, :] = k[:rows]
        s.k[low_at, :] = k[rows:]
        v = (dot(both, s.wv[...]) + jnp.where(x == 0, b_value[:, :half], b_value[:, half:])).astype(BF16)
        s.v[at, :] = v[:rows]
        s.v[low_at, :] = v[rows:]
        q = (dot(hq, s.wq[...]) + jnp.where(x == 0, b_query[:, :half], b_query[:, half:])).astype(BF16)
        s.q[at, :] = q

    low_own = pl.ds(pl.multiple_of((2 + x) * rows, rows), rows)
    low_other = pl.ds(pl.multiple_of((3 - x) * rows, rows), rows)
    load_q()
    load_l()
    qin, hat_q, inv_q, hq, hkq = own_half(positions, own, low_own)
    hat_l, inv_l, hkl = lat_half(own)

    load_w2()
    for b in range(nb):
        s.d_act[b] = dot_t(d_mlp, s.w2[b * half:(b + 1) * half, :])

    load_wk()
    load_wv()
    load_wq()
    project(hq, hkq, hkl, own, low_own)

    got_q()
    got_p()
    _, _, _, hq_o, hkq_o = own_half(s.ppos, other, low_other)
    got_l()
    _, _, hkl_o = lat_half(other)
    project(hq_o, hkq_o, hkl_o, other, low_other)

    ok = jnp.concatenate([vis_ok[...], msk_ok[...]], axis=1) > 0
    lane = lax.broadcasted_iota(jnp.int32, (2 * rows, 2 * HEAD_DIM), 1)
    first = lane < HEAD_DIM

    def stack(pair):
        zero = jnp.zeros_like(pair)
        return jnp.concatenate([jnp.where(first, pair, zero), jnp.where(first, zero, pair)], axis=0)

    def unstack(both):
        return jnp.where(first, both[:2 * rows], both[2 * rows:])

    def lanes(pair):
        return slice(pair * 2 * HEAD_DIM, (pair + 1) * 2 * HEAD_DIM)

    for pair in range(heads // 2):
        raw = dot_t(stack(s.q[:, lanes(pair)]), s.k[:, lanes(pair)]) * scale
        scores = jnp.where(ok, raw, -1e30)
        peak = jnp.max(scores, axis=-1, keepdims=True)
        weight = jnp.exp(scores - peak)
        prob = weight * (1.0 / jnp.sum(weight, axis=-1, keepdims=True))
        s.prob[pair] = prob
        s.att[x, :, lanes(pair)] = unstack(dot(prob.astype(BF16), s.v[:, lanes(pair)])).astype(
            BF16
        )
    got_att = push(s.att.at[x], s.att.at[x], PX, s.att.at[1 - x])

    s.hq_t[...] = s.hq[...].T
    s.hk_t[...] = s.hk[...].T
    load_wo()
    got_att()

    branch = (
        dot(s.att[0, own, :], s.wo[:half, :])
        + dot(s.att[1, own, :], s.wo[half:, :])
        + b_out
    )
    resid = qin + scale_a * branch
    hat_m, inv_m = normalise(resid)
    h_two = (hat_m * gain_m + shift_m).astype(BF16)
    s.h2_g[0] = h_two
    got_h2 = [
        push(s.h2_g.at[0], s.h2_g.at[1], PY),
        push(s.h2_g.at[0], s.h2_g.at[2], PX),
        push(s.h2_g.at[0], s.h2_g.at[3], PXY),
    ]
    load_w1()
    mlp = jnp.zeros((rows, width), F32)
    d_h2 = jnp.zeros((rows, width), F32)
    for b in range(nb):
        cols = slice(b * half, (b + 1) * half)
        pre = dot(h_two, s.w1[:, cols]) + b_fc1[:, cols]
        cdf = 0.5 * (1.0 + lax.erf(pre * math.sqrt(0.5)))
        act = (pre * cdf).astype(BF16)
        slope = cdf + pre * (jnp.exp(-0.5 * pre * pre) * (1.0 / math.sqrt(2 * math.pi)))
        d_pre = (s.d_act[b] * slope).astype(BF16)
        s.act_s[b % 2, b // 2] = act
        s.dp_s[b // (nb // 2), b % (nb // 2)] = d_pre
        s.vec[b // 2:b // 2 + 1, (b % 2) * half:(b % 2 + 1) * half] = col_sum(d_pre.astype(F32))
        mlp += dot(act, s.w2[cols, :])
        d_h2 += dot_t(d_pre, s.w1[:, cols])
    got_act = [push(s.act_s.at[1 - y], s.act_g.at[1], PY)]

    s.vec[6:7, :] = col_sum(d_h2 * hat_m)
    s.vec[7:8, :] = col_sum(d_h2)
    d_resid = dy + normalise_back(d_h2 * gain_m, hat_m, inv_m)
    d_branch = (scale_a * d_resid).astype(BF16)
    s.dbr[own, :] = d_branch
    got_dbr = push(s.dbr.at[own], s.dbr.at[own], PX, s.dbr.at[other])

    got_act += [
        push(s.act_s.at[y], s.act_g.at[2], PX),
        push(s.act_s.at[1 - y], s.act_g.at[3], PXY),
    ]
    got_dp = [
        push(s.dp_s.at[x], s.dp_g.at[1], PY),
        push(s.dp_s.at[1 - x], s.dp_g.at[2], PX),
        push(s.dp_s.at[1 - x], s.dp_g.at[3], PXY),
    ]
    s.act_g[0] = s.act_s[y]
    s.dp_g[0] = s.dp_s[x]
    mlp_out = mlp + b_fc2
    out_block[0] = (resid + scale_m * mlp_out).astype(BF16)
    s.vec[5:6, :] = col_sum(dy * mlp_out)
    s.vec2[0:1, :] = col_sum(d_branch.astype(F32))
    s.vec2[1:2, :] = col_sum(d_resid * branch)

    got_dbr()
    wo_mine = s.wo[mine, :]
    s.da[...] = dot_t(s.dbr[...], wo_mine).astype(BF16)
    for pair in range(heads // 2):
        q2 = stack(s.q[:, lanes(pair)])
        da2 = stack(s.da[:, lanes(pair)])
        prob = s.prob[pair]
        s.dv[:, lanes(pair)] = dot(prob.astype(BF16).T, da2).astype(BF16)
        d_prob = dot_t(da2, s.v[:, lanes(pair)])
        delta = jnp.sum(d_prob * prob, axis=-1, keepdims=True)
        ds = (prob * (d_prob - delta)).astype(BF16)
        s.dq[:, lanes(pair)] = (unstack(dot(ds, s.k[:, lanes(pair)])) * scale).astype(BF16)
        s.dk[:, lanes(pair)] = (dot(ds.T, q2) * scale).astype(BF16)

    def blocks(ref, cc, yy):
        return jnp.concatenate(
            [
                ref[pl.ds(pl.multiple_of(((zs[t] * 2 + yy) * 2 + cc) * blk, blk), blk), :]
                for t in Z_ORDER
            ],
            axis=0,
        )

    def square(i, left_t, right):
        for leave in (1, 0):
            cc = 1 - c if leave else c
            left = jnp.concatenate([blocks(left_t, cc, y), blocks(left_t, cc, 1 - y)], axis=0)
            total = dot(left, right)
            if leave:
                s.sq_cs[i] = total.astype(BF16)
                got = push(s.sq_cs.at[i], s.sq_cr.at[i], PC)
            else:
                s.sq[i] = total
        return got

    got_c = [None] * 4
    got_c[1] = square(1, s.hk_t, s.dv[...])
    got_c[2] = square(2, s.hk_t, s.dk[...])
    got_c[3] = square(3, s.hq_t, s.dq[...])

    dhk = dot_t(s.dk[...], s.wk[...]) + dot_t(s.dv[...], s.wv[...])
    dhq = dot_t(s.dq[...], s.wq[...])
    s.vec2[2:3, :] = jnp.zeros((1, width), F32)
    s.vec2[3:4, :] = jnp.zeros((1, width), F32)
    s.vec2[2:3, mine] = col_sum(s.dq[...].astype(F32))
    s.vec2[3:4, mine] = col_sum(s.dv[...].astype(F32))
    hat_low = s.hat[2 * rows:, :]
    s.vec2[4:5, :] = col_sum(dhq * hat_low)
    s.vec2[5:6, :] = col_sum(dhq)
    s.vec2[6:7, :] = col_sum(dhk * s.hat[...])
    s.vec2[7:8, :] = col_sum(dhk)
    s.dx[0] = dhk[:2 * rows] * gain_k
    s.dx[1] = dhk[2 * rows:] * gain_k + dhq * gain_q
    s.dx_s[...] = s.dx[:, other, :].astype(BF16)
    got_dx = push(s.dx_s, s.dx_r, PX)

    s.att_t[mine, :] = s.att[x].T
    s.att_t[theirs, :] = s.att[1 - x].T
    got_c[0] = square(0, s.att_t, s.dbr[:, mine])

    vectors = ((s.vec, s.vec_a, s.vec_b, s.vec_r), (s.vec2, s.vec2_a, s.vec2_b, s.vec2_r))
    got_vc = [push(s.vec, s.vec_r.at[0], PC), push(s.vec2, s.vec2_r.at[0], PC)]

    for got in got_dm:
        got()
    for got in got_act:
        got()
    d_mlp_all = s.dm_g[...].reshape(4 * rows, half)
    for k, t in enumerate(Z_ORDER):
        part = s.act_g[:, zs[t]].reshape(4 * rows, half)
        s.fc2[k] = dot(part.T, d_mlp_all)
        s.fc2_cs[k] = s.fc2[k, pl.ds(pl.multiple_of((1 - c) * fblk, fblk), fblk), :].astype(BF16)
    got_c2 = push(s.fc2_cs, s.fc2_cr, PC)

    for got in got_h2:
        got()
    s.h2_t[...] = s.h2_g[...].reshape(4 * rows, width).T
    for got in got_dp:
        got()
    leave = blocks(s.h2_t, 1 - c, y)
    stay = blocks(s.h2_t, c, y)
    for b in range(nb // 2):
        right = s.dp_g[:, b].reshape(4 * rows, half)
        s.fc1_cs[b] = dot(leave, right).astype(BF16)
        s.fc1[b] = dot(stay, right)
    got_c1 = push(s.fc1_cs, s.fc1_cr, PC)

    yrows = 4 * blk
    got_y = []
    for i in (1, 2, 3, 0):
        got_c[i]()
        s.sq_ys[i] = (s.sq[i, yrows:, :] + s.sq_cr[i, yrows:, :].astype(F32)).astype(BF16)
        got_y.append(push(s.sq_ys.at[i], s.sq_yr.at[i], PY))

    got_c2()
    keep = pl.ds(pl.multiple_of(c * fblk, fblk), fblk)
    s.fc2_zs[...] = (s.fc2[2:, keep, :] + s.fc2_cr[2:].astype(F32)).astype(BF16)
    got_z2 = push(s.fc2_zs, s.fc2_zr, PZ[1])
    got_c1()
    s.fc1_zs[...] = (s.fc1[:, 2 * blk:, :] + s.fc1_cr[:, 2 * blk:, :].astype(F32)).astype(BF16)
    got_z1 = push(s.fc1_zs, s.fc1_zr, PZ[1])

    got_vxy = []
    for group, got in enumerate(got_vc):
        got()
        ref, summed, _, landing = vectors[group]
        summed[...] = ref[...] + landing[0]
        got_vxy.append(
            [
                push(summed, landing.at[1], PX),
                push(summed, landing.at[2], PY),
                push(summed, landing.at[3], PXY),
            ]
        )

    for got in got_y:
        got()
    zrows = 2 * blk
    for i in range(4):
        s.sq[i, :yrows, :] = (
            s.sq[i, :yrows, :] + s.sq_cr[i, :yrows, :].astype(F32) + s.sq_yr[i].astype(F32)
        )
        s.sq_zs[i] = s.sq[i, zrows:yrows, :].astype(BF16)
    got_zsq = push(s.sq_zs, s.sq_zr, PZ[1])

    got_dx()
    dx_l = s.dx[0, own, :] + s.dx_r[0].astype(F32)
    dx_q = s.dx[1, own, :] + s.dx_r[1].astype(F32)
    out_dl[0] = normalise_back(dx_l, hat_l, inv_l)
    out_dq[0] = d_resid + normalise_back(dx_q, hat_q, inv_q)

    got_vz = []
    for group, gots in enumerate(got_vxy):
        for got in gots:
            got()
        _, summed, square_sum, landing = vectors[group]
        square_sum[...] = (summed[...] + landing[1]) + (landing[2] + landing[3])
        got_vz.append([push(square_sum, landing.at[3 + t], PZ[t]) for t in (1, 2, 3)])

    got_z2()
    s.fc2_ws[...] = (
        s.fc2[1, keep, :] + s.fc2_cr[1].astype(F32) + s.fc2_zr[1].astype(F32)
    ).astype(BF16)
    got_w2 = push(s.fc2_ws, s.fc2_wr, PZ[2])
    got_z1()
    s.fc1_ws[...] = (
        s.fc1[:, blk:2 * blk, :]
        + s.fc1_cr[:, blk:2 * blk, :].astype(F32)
        + s.fc1_zr[:, blk:, :].astype(F32)
    ).astype(BF16)
    got_w1 = push(s.fc1_ws, s.fc1_wr, PZ[2])
    got_zsq()
    s.sq_ws[...] = (s.sq[:, blk:zrows, :] + s.sq_zr[:, blk:, :].astype(F32)).astype(BF16)
    got_wsq = push(s.sq_ws, s.sq_wr, PZ[2])

    got_w2()
    out_w2[...] = (
        s.fc2[0, keep, :]
        + s.fc2_cr[0].astype(F32)
        + s.fc2_zr[0].astype(F32)
        + s.fc2_wr[...].astype(F32)
    )
    got_w1()
    for b in range(nb // 2):
        out_w1[:, b * half:(b + 1) * half] = (
            s.fc1[b, :blk, :]
            + s.fc1_cr[b, :blk, :].astype(F32)
            + s.fc1_zr[b, :blk, :].astype(F32)
            + s.fc1_wr[b].astype(F32)
        )
    for group, gots in enumerate(got_vz):
        for got in gots:
            got()
        _, _, square_sum, landing = vectors[group]
        out_vec[group * 8:group * 8 + 8, :] = (square_sum[...] + landing[4]) + (
            landing[5] + landing[6]
        )
    got_wsq()
    for i, out in enumerate((out_wo, out_wv, out_wk, out_wq)):
        out[...] = (
            s.sq[i, :blk, :] + s.sq_zr[i, :blk, :].astype(F32) + s.sq_wr[i].astype(F32)
        )
    for copy in sent:
        copy.wait_send()


def fused(share, args):
    (queries, latents, positions, vis_ok, msk_ok, dy, w_query, w_key, w_value, w_out, w_fc1, w_fc2) = args[:12]
    vectors = args[12:]
    _, rows, width = queries.shape
    ff = w_fc1.shape[1]
    half = width // 2
    blk, fblk, nb = width // GROUPS, ff // GROUPS, ff // half
    pairs = half // (2 * HEAD_DIM)
    vm = pltpu.VMEM
    scratch = dict(
        send=pltpu.SemaphoreType.DMA((64,)),
        recv=pltpu.SemaphoreType.DMA((64,)),
        load=pltpu.SemaphoreType.DMA((16,)),
        dy=vm((rows, width), BF16),
        qraw=vm((2 * rows, width), BF16),
        lraw=vm((2 * rows, width), BF16),
        ppos=vm((1, rows), jnp.int32),
        w2=vm((ff, width), BF16),
        w1=vm((width, ff), BF16),
        wo=vm((width, width), BF16),
        wk=vm((width, half), BF16),
        wv=vm((width, half), BF16),
        wq=vm((width, half), BF16),
        hat=vm((4 * rows, width), F32),
        hq=vm((2 * rows, width), BF16),
        hk=vm((4 * rows, width), BF16),
        hq_t=vm((width, 2 * rows), BF16),
        hk_t=vm((width, 4 * rows), BF16),
        att_t=vm((width, 2 * rows), BF16),
        h2_t=vm((width, 4 * rows), BF16),
        q=vm((2 * rows, half), BF16),
        k=vm((4 * rows, half), BF16),
        v=vm((4 * rows, half), BF16),
        prob=vm((pairs, 4 * rows, 4 * rows), F32),
        att=vm((2, 2 * rows, half), BF16),
        d_act=vm((nb, rows, half), F32),
        dm_s=vm((2, rows, half), BF16),
        dm_g=vm((4, rows, half), BF16),
        h2_g=vm((4, rows, width), BF16),
        act_s=vm((2, nb // 2, rows, half), BF16),
        act_g=vm((4, nb // 2, rows, half), BF16),
        dp_s=vm((2, nb // 2, rows, half), BF16),
        dp_g=vm((4, nb // 2, rows, half), BF16),
        dbr=vm((2 * rows, width), BF16),
        da=vm((2 * rows, half), BF16),
        dq=vm((2 * rows, half), BF16),
        dk=vm((4 * rows, half), BF16),
        dv=vm((4 * rows, half), BF16),
        dx=vm((2, 2 * rows, width), F32),
        dx_s=vm((2, rows, width), BF16),
        dx_r=vm((2, rows, width), BF16),
        sq=vm((4, 8 * blk, half), F32),
        sq_cs=vm((4, 8 * blk, half), BF16),
        sq_cr=vm((4, 8 * blk, half), BF16),
        sq_ys=vm((4, 4 * blk, half), BF16),
        sq_yr=vm((4, 4 * blk, half), BF16),
        sq_zs=vm((4, 2 * blk, half), BF16),
        sq_zr=vm((4, 2 * blk, half), BF16),
        sq_ws=vm((4, blk, half), BF16),
        sq_wr=vm((4, blk, half), BF16),
        fc2=vm((4, 2 * fblk, half), F32),
        fc2_cs=vm((4, fblk, half), BF16),
        fc2_cr=vm((4, fblk, half), BF16),
        fc2_zs=vm((2, fblk, half), BF16),
        fc2_zr=vm((2, fblk, half), BF16),
        fc2_ws=vm((fblk, half), BF16),
        fc2_wr=vm((fblk, half), BF16),
        fc1=vm((nb // 2, 4 * blk, half), F32),
        fc1_cs=vm((nb // 2, 4 * blk, half), BF16),
        fc1_cr=vm((nb // 2, 4 * blk, half), BF16),
        fc1_zs=vm((nb // 2, 2 * blk, half), BF16),
        fc1_zr=vm((nb // 2, 2 * blk, half), BF16),
        fc1_ws=vm((nb // 2, blk, half), BF16),
        fc1_wr=vm((nb // 2, blk, half), BF16),
        vec=vm((8, width), F32),
        vec_a=vm((8, width), F32),
        vec_b=vm((8, width), F32),
        vec_r=vm((7, 8, width), F32),
        vec2=vm((8, width), F32),
        vec2_a=vm((8, width), F32),
        vec2_b=vm((8, width), F32),
        vec2_r=vm((7, 8, width), F32),
    )
    ANY = pl.BlockSpec(memory_space=pl.ANY)
    VMEM = pl.BlockSpec(memory_space=pltpu.VMEM)
    sds = jax.ShapeDtypeStruct
    return pl.pallas_call(
        functools.partial(kernel, (rows, width, ff, share)),
        out_shape=(
            sds((1, rows, width), BF16),
            sds((1, rows, width), F32),
            sds((1, rows, width), F32),
            sds((blk, half), F32),
            sds((blk, half), F32),
            sds((blk, half), F32),
            sds((blk, half), F32),
            sds((blk, ff // 2), F32),
            sds((fblk, half), F32),
            sds((16, width), F32),
        ),
        in_specs=[ANY, ANY, VMEM, VMEM, VMEM, ANY] + [ANY] * 6 + [VMEM] * 13,
        out_specs=[VMEM] * 10,
        scratch_shapes=[scratch],
        compiler_params=pltpu.CompilerParams(
            collective_id=0, has_side_effects=True, vmem_limit_bytes=60 << 20
        ),
        cost_estimate=pl.CostEstimate(
            flops=6 * 10**9, bytes_accessed=16 * 10**6, transcendentals=10**6
        ),
    )(queries, latents, positions, vis_ok, msk_ok, dy, w_query, w_key, w_value, w_out, w_fc1, w_fc2, *vectors)


def finish_kernel(count, *refs):
    arrays, table = refs[:count], refs[count]
    outs, rows = refs[count + 1:2 * count + 1], refs[2 * count + 1:-1]
    sems = refs[-1]
    copies = [
        pltpu.make_async_copy(src, dst, sems.at[i]) for i, (src, dst) in enumerate(zip(arrays, outs))
    ]
    for copy in copies:
        copy.start()
    width = table.shape[1]
    parts = rows[0].shape[0] // width
    for k in range(parts):
        rows[0][k * width:(k + 1) * width] = table[k, :]
    for k, row in enumerate(rows[1:]):
        row[...] = table[parts + k, :]
    for copy in copies:
        copy.wait()


def finish(arrays, table, ff):
    count, width = len(arrays), table.shape[1]
    sds = jax.ShapeDtypeStruct
    vectors = table.shape[0] - ff // width
    ANY = pl.BlockSpec(memory_space=pl.ANY)
    VMEM = pl.BlockSpec(memory_space=pltpu.VMEM)
    return pl.pallas_call(
        functools.partial(finish_kernel, count),
        out_shape=tuple(sds(a.shape, a.dtype) for a in arrays)
        + (sds((ff,), F32),)
        + (sds((width,), F32),) * vectors,
        in_specs=[VMEM] * (count + 1),
        out_specs=[ANY] * count + [VMEM] * (1 + vectors),
        scratch_shapes=[pltpu.SemaphoreType.DMA((count,))],
    )(*arrays, table)


def per_device(
    queries, latents, positions, visible_valid, masked_valid,
    w_query, b_query, w_key, w_value, b_value, w_out, b_out, w_fc1, b_fc1, w_fc2, b_fc2,
    gain_query, shift_query, gain_keys, shift_keys, gain_mlp, shift_mlp, scale_attn, scale_mlp,
    out_grad,
):
    parts = lax.axis_size("dp")
    share = parts // GROUPS
    out = fused(
        share,
        (
            queries, latents, positions, visible_valid, masked_valid, out_grad,
            w_query, w_key, w_value, w_out, w_fc1, w_fc2,
            b_query, b_value, b_out, b_fc1, b_fc2,
            gain_query, shift_query, gain_keys, shift_keys, gain_mlp, shift_mlp, scale_attn, scale_mlp,
        ),
    )
    block_out, d_queries, d_latents, wq, wk, wv, wo, w1, w2, vec = out
    if share > 1:
        groups = [[n * share + i for i in range(share)] for n in range(GROUPS)]
        wq, wk, wv, wo, w1, w2 = (
            lax.psum_scatter(
                w, "dp", scatter_dimension=0, axis_index_groups=groups, tiled=True
            )
            for w in (wq, wk, wv, wo, w1, w2)
        )
        vec = lax.psum(vec, "dp", axis_index_groups=groups)
    arrays = (block_out, d_queries, d_latents, wq, wk, wv, wo, w1, w2)
    done = finish(arrays, vec, w_fc1.shape[1])
    block_out, d_queries, d_latents, wq, wk, wv, wo, w1, w2, b1 = done[:10]
    b2, sm, gm, hm, bo, sa, bq, bv, gq, hq, gk, hk = done[10:]
    return (
        block_out, d_queries, d_latents,
        wq, bq, wk, wv, bv, wo, bo, w1, b1, w2, b2,
        gq, hq, gk, hk, gm, hm, sa, sm,
    )


def solution(mesh):
    rows3 = P("dp", "qry", None)
    split = P("dp", "qry")
    full = P()
    return jax.shard_map(
        per_device,
        mesh=mesh,
        in_specs=(rows3, rows3, split, P("dp", None), P("dp", None)) + (full,) * 19 + (rows3,),
        out_specs=(
            rows3, rows3, rows3,
            split, full, split, split, full, split, full, split, full, split,
        ) + (full,) * 9,
        check_vma=False,
    )
```

```python
import functools
import math
import types

import jax
import jax.numpy as jnp
from jax import lax
from jax.experimental import pallas as pl
from jax.experimental.pallas import tpu as pltpu
from jax.sharding import PartitionSpec as P

HEAD_DIM = 64
MESH = pl.DeviceIdType.MESH
F32 = jnp.float32
BF16 = jnp.bfloat16
GROUPS = 16
Z_ORDER = (0, 2, 1, 3)


def dot(a, b):
    return lax.dot_general(a, b, (((1,), (0,)), ((), ())), preferred_element_type=F32)


def dot_t(a, b):
    return lax.dot_general(a, b, (((1,), (1,)), ((), ())), preferred_element_type=F32)


def col_sum(a):
    return jnp.sum(a, axis=0, keepdims=True)


def normalise(v):
    centre = v - jnp.mean(v, axis=-1, keepdims=True)
    spread = jnp.mean(centre * centre, axis=-1, keepdims=True)
    inv = lax.rsqrt(spread + 1e-06)
    return centre * inv, inv


def normalise_back(grad_hat, hat, inv):
    m1 = jnp.mean(grad_hat, axis=-1, keepdims=True)
    m2 = jnp.mean(grad_hat * hat, axis=-1, keepdims=True)
    return inv * (grad_hat - m1 - hat * m2)


def sinusoid(places, width):
    index = lax.broadcasted_iota(jnp.int32, (1, width), 1)
    half = index // 2
    freq = jnp.exp(-(2.0 * half.astype(F32) / width) * math.log(10000.0))
    odd = (index - 2 * half).astype(F32)
    angle = places * freq
    turns = jnp.floor(angle * (2.0 / math.pi) + 0.5)
    rest = angle - turns * 1.5703125
    rest = rest - turns * 4.8351287841796875e-4
    rest = rest - turns * 3.1385570764541626e-07
    sq = rest * rest
    sine = rest * (
        1.0 + sq * (-1.0 / 6 + sq * (1.0 / 120 + sq * (-1.0 / 5040 + sq * (1.0 / 362880))))
    )
    cosine = 1.0 + sq * (-0.5 + sq * (1.0 / 24 + sq * (-1.0 / 720 + sq * (1.0 / 40320))))
    quarter = turns + odd
    pairs = jnp.floor(quarter * 0.5)
    parity = quarter - 2.0 * pairs
    flips = pairs - 2.0 * jnp.floor(pairs * 0.5)
    value = jnp.where(parity > 0.5, cosine, sine)
    return jnp.where(flips > 0.5, -value, value)


def kernel(
    shape,
    queries, latents, positions, vis_ok, msk_ok, dy_in,
    w_query, w_key, w_value, w_out, w_fc1, w_fc2,
    b_query, b_value, b_out, b_fc1, b_fc2,
    gain_q, shift_q, gain_k, shift_k, gain_m, shift_m, scale_a, scale_m,
    out_block, out_dq, out_dl, out_wq, out_wk, out_wv, out_wo, out_w1, out_w2, out_vec,
    s,
):
    s = types.SimpleNamespace(**s)
    rows, width, ff, share = shape
    (b_query, b_value, b_out, b_fc1, b_fc2, gain_q, shift_q, gain_k, shift_k, gain_m, shift_m,
     scale_a, scale_m) = (
        ref[...].reshape(1, -1)
        for ref in (b_query, b_value, b_out, b_fc1, b_fc2, gain_q, shift_q, gain_k, shift_k, gain_m,
                    shift_m, scale_a, scale_m)
    )
    half = width // 2
    heads = half // HEAD_DIM
    blk = width // GROUPS
    fblk = ff // GROUPS
    hid = ff // 2
    nb = hid // half
    scale = 1.0 / math.sqrt(HEAD_DIM)

    x = lax.axis_index("qry")
    place = lax.axis_index("dp")
    n = place // share
    low = place - n * share
    z = n // 4
    y = (n // 2) % 2
    c = n % 2
    zs = (z, z + 1 - 2 * (z % 2), (z + 2) % 4, 3 - z)

    def dev(zz, yy, cc, xx):
        return (((zz * 2 + yy) * 2 + cc) * share + low, xx)

    PX = dev(z, y, c, 1 - x)
    PY = dev(z, 1 - y, c, x)
    PC = dev(z, y, 1 - c, x)
    PZ1 = dev(zs[1], y, c, x)
    PZ2 = dev(zs[2], y, c, x)

    counter = [0]
    sent = []

    def push(src, dst, peer, landing=None):
        i = counter[0]
        counter[0] += 1

        def describe(to):
            return pltpu.make_async_remote_copy(
                src_ref=src, dst_ref=to, send_sem=s.send.at[i], recv_sem=s.recv.at[i],
                device_id=peer, device_id_type=MESH,
            )

        copy = describe(dst)
        copy.start()
        sent.append(copy)
        arrival = copy if landing is None else describe(landing)
        return arrival.wait_recv

    loads = []

    def load(src, dst):
        copy = pltpu.make_async_copy(src, dst, s.load.at[len(loads)])
        copy.start()
        loads.append(copy)
        return copy.wait

    own = pl.ds(pl.multiple_of(x * rows, rows), rows)
    other = pl.ds(pl.multiple_of((1 - x) * rows, rows), rows)
    low_own = pl.ds(pl.multiple_of((2 + x) * rows, rows), rows)
    low_other = pl.ds(pl.multiple_of((3 - x) * rows, rows), rows)
    mine = pl.ds(pl.multiple_of(x * half, half), half)
    theirs = pl.ds(pl.multiple_of((1 - x) * half, half), half)
    units = pl.ds(pl.multiple_of(x * hid, hid), hid)
    load_q = load(queries.at[0], s.qraw.at[own])
    load_l = load(latents.at[0], s.lraw.at[own])
    load_dy = load(dy_in.at[0], s.dy.at[own])
    load_wk = load(w_key.at[:, mine], s.wk)
    load_wv = load(w_value.at[:, mine], s.wv)
    load_wq = load(w_query.at[:, mine], s.wq)
    load_w2 = load(w_fc2.at[units], s.w2)
    load_wo = load(w_out, s.wo)
    load_w1 = load(w_fc1.at[:, units], s.w1)

    barrier = pltpu.get_barrier_semaphore()
    peers = [PX, PY, PC, PZ1, PZ2]
    for peer in peers:
        pl.semaphore_signal(barrier, inc=1, device_id=peer, device_id_type=MESH)
    pl.semaphore_wait(barrier, len(peers))

    got_p = push(positions, s.ppos, PX)
    got_q = push(queries.at[0], s.qraw.at[own], PX, s.qraw.at[other])
    got_l = push(latents.at[0], s.lraw.at[own], PX, s.lraw.at[other])
    got_dy = push(dy_in.at[0], s.dy.at[own], PX, s.dy.at[other])

    eye = lax.broadcasted_iota(jnp.int32, (rows, rows), 0) == lax.broadcasted_iota(
        jnp.int32, (rows, rows), 1
    )

    def qry_half(pos_ref, at, low_at):
        row = jnp.broadcast_to(pos_ref[...].astype(F32), (rows, rows))
        places = jnp.sum(jnp.where(eye, row, 0.0), axis=1, keepdims=True)
        qin = s.qraw[at, :].astype(F32) + sinusoid(places, width)
        s.qin[at, :] = qin
        hat, inv = normalise(qin)
        s.hat[low_at, :] = hat
        hq = (hat * gain_q + shift_q).astype(BF16)
        hkq = (hat * gain_k + shift_k).astype(BF16)
        s.hq[at, :] = hq
        s.hk[low_at, :] = hkq
        return hat, inv, hq, hkq

    def lat_half(at):
        hat, inv = normalise(s.lraw[at, :].astype(F32))
        s.hat[at, :] = hat
        hkl = (hat * gain_k + shift_k).astype(BF16)
        s.hk[at, :] = hkl
        return hat, inv, hkl

    my_b_value = jnp.where(x == 0, b_value[:, :half], b_value[:, half:])
    my_b_query = jnp.where(x == 0, b_query[:, :half], b_query[:, half:])
    my_b_fc1 = jnp.where(x == 0, b_fc1[:, :hid], b_fc1[:, hid:])

    def project(hq, hkq, hkl, at, low_at):
        both = jnp.concatenate([hkl, hkq], axis=0)
        k = dot(both, s.wk[...]).astype(BF16)
        s.k[at, :] = k[:rows]
        s.k[low_at, :] = k[rows:]
        v = (dot(both, s.wv[...]) + my_b_value).astype(BF16)
        s.v[at, :] = v[:rows]
        s.v[low_at, :] = v[rows:]
        s.q[at, :] = (dot(hq, s.wq[...]) + my_b_query).astype(BF16)

    load_q()
    load_l()
    hat_q, inv_q, hq, hkq = qry_half(positions, own, low_own)
    hat_l, inv_l, hkl = lat_half(own)
    load_wk()
    load_wv()
    load_wq()
    project(hq, hkq, hkl, own, low_own)
    got_p()
    got_q()
    _, _, hq_o, hkq_o = qry_half(s.ppos, other, low_other)
    got_l()
    _, _, hkl_o = lat_half(other)
    project(hq_o, hkq_o, hkl_o, other, low_other)

    ok = jnp.concatenate([vis_ok[...], msk_ok[...]], axis=1) > 0
    lane = lax.broadcasted_iota(jnp.int32, (2 * rows, 2 * HEAD_DIM), 1)
    first = lane < HEAD_DIM

    def stack(pair):
        zero = jnp.zeros_like(pair)
        return jnp.concatenate([jnp.where(first, pair, zero), jnp.where(first, zero, pair)], axis=0)

    def unstack(both):
        return jnp.where(first, both[:2 * rows], both[2 * rows:])

    def lanes(pair):
        return slice(pair * 2 * HEAD_DIM, (pair + 1) * 2 * HEAD_DIM)

    for pair in range(heads // 2):
        raw = dot_t(stack(s.q[:, lanes(pair)]), s.k[:, lanes(pair)]) * scale
        scores = jnp.where(ok, raw, -1e30)
        peak = jnp.max(scores, axis=-1, keepdims=True)
        weight = jnp.exp(scores - peak)
        prob = weight * (1.0 / jnp.sum(weight, axis=-1, keepdims=True))
        s.prob[pair] = prob
        s.att[x, :, lanes(pair)] = unstack(dot(prob.astype(BF16), s.v[:, lanes(pair)])).astype(BF16)
    got_att = push(s.att.at[x], s.att.at[x], PX, s.att.at[1 - x])

    load_dy()
    got_dy()
    load_w2()
    dy = s.dy[...].astype(F32)
    d_mlp = (scale_m * dy).astype(BF16)
    s.dm[0] = d_mlp
    got_dm = push(s.dm.at[0], s.dm.at[1], PY)
    for b in range(nb):
        s.d_act[b] = dot_t(d_mlp, s.w2[b * half:(b + 1) * half, :])
    s.vec[0, 4:5, :] = col_sum((scale_m * s.dy[own, :].astype(F32)).astype(BF16).astype(F32))
    s.hq_t[...] = s.hq[...].T
    s.hk_t[...] = s.hk[...].T
    load_wo()
    got_att()

    branch = dot(s.att[0], s.wo[:half, :]) + dot(s.att[1], s.wo[half:, :]) + b_out
    s.branch[...] = branch
    resid = s.qin[...] + scale_a * branch
    s.resid[...] = resid
    hat_m, inv_m = normalise(resid)
    h_two = (hat_m * gain_m + shift_m).astype(BF16)

    def blocks(ref, cc, yy):
        return jnp.concatenate(
            [
                ref[pl.ds(pl.multiple_of(((zs[t] * 2 + yy) * 2 + cc) * blk, blk), blk), :]
                for t in Z_ORDER
            ],
            axis=0,
        )

    s.h2_t[...] = h_two.T
    for i, yy in enumerate((y, 1 - y)):
        s.h2_g[i, 0] = blocks(s.h2_t, c, yy)
        s.h2_g[i, 1] = blocks(s.h2_t, 1 - c, yy)
    got_h2 = push(s.h2_g.at[1], s.h2_r, PY)
    load_w1()
    mlp = jnp.zeros((2 * rows, width), F32)
    d_h2 = jnp.zeros((2 * rows, width), F32)
    s.vec[0, 0:4, :] = jnp.zeros((4, width), F32)
    got_dp = []
    for b in range(nb):
        cols = slice(b * half, (b + 1) * half)
        pre = dot(h_two, s.w1[:, cols]) + my_b_fc1[:, cols]
        cdf = 0.5 * (1.0 + lax.erf(pre * math.sqrt(0.5)))
        act = (pre * cdf).astype(BF16)
        slope = cdf + pre * (jnp.exp(-0.5 * pre * pre) * (1.0 / math.sqrt(2 * math.pi)))
        d_pre = (s.d_act[b] * slope).astype(BF16)
        s.act[b] = act
        s.dp[0, b] = d_pre
        got_dp.append(push(s.dp.at[0, b], s.dp.at[1, b], PY))
        d_h2 += dot_t(d_pre, s.w1[:, cols])
    s.dh2[0] = d_h2.astype(BF16)
    got_dh2 = push(s.dh2.at[0], s.dh2.at[1], PX)
    for b in range(nb):
        cols = slice(b * half, (b + 1) * half)
        mlp += dot(s.act[b], s.w2[cols, :])
        s.vec[0, pl.ds(2 * x + b // 2, 1), (b % 2) * half:(b % 2 + 1) * half] = col_sum(
            s.dp[0, b].astype(F32)
        )
        s.act_t[cols, :] = s.act[b].T
    for i, yy in enumerate((y, 1 - y)):
        for j, cc in enumerate((c, 1 - c)):
            for zz in range(2):
                at = pl.ds(pl.multiple_of((zz * 4 + yy * 2 + cc) * fblk, fblk), fblk)
                s.act_g[i, j, zz] = s.act_t[at, :]
    got_act = push(s.act_g.at[1], s.act_r, PY)
    s.mlp[...] = mlp
    s.mlp_s[...] = s.mlp[other, :].astype(BF16)
    got_mlp = push(s.mlp_s, s.mlp_r, PX)
    dy_own = s.dy[own, :].astype(F32)
    s.vec[0, 5:6, :] = col_sum(dy * mlp) + b_fc2 * col_sum(dy_own)
    s.vec[0, 6:7, :] = col_sum(d_h2 * hat_m)
    s.vec[0, 7:8, :] = col_sum(d_h2)

    got_c1, got_z1, got_w1 = [None] * nb, [None] * nb, [None] * nb

    def fc1_product(b):
        if b == 0:
            got_h2()
        got_dp[b]()
        right = s.dp[:, b].reshape(4 * rows, half)
        left = jnp.concatenate([s.h2_g[0], s.h2_r[...]], axis=-1)
        s.fc1_cs[b] = dot(left[1], right).astype(BF16)
        got_c1[b] = push(s.fc1_cs.at[b], s.fc1_cr.at[b], PC)
        s.fc1[b] = dot(left[0], right)

    def fc1_core(b):
        got_c1[b]()
        s.fc1[b] = s.fc1[b] + s.fc1_cr[b].astype(F32)
        s.fc1_zs[b] = s.fc1[b, 2 * blk:, :].astype(BF16)
        got_z1[b] = push(s.fc1_zs.at[b], s.fc1_zr.at[b], PZ1)

    def fc1_z(b):
        got_z1[b]()
        s.fc1_ws[b] = (s.fc1[b, blk:2 * blk, :] + s.fc1_zr[b, blk:, :].astype(F32)).astype(BF16)
        got_w1[b] = push(s.fc1_ws.at[b], s.fc1_wr.at[b], PZ2)

    def fc1_end(b):
        got_w1[b]()
        out_w1[:, b * half:(b + 1) * half] = (
            s.fc1[b, :blk, :] + s.fc1_zr[b, :blk, :].astype(F32) + s.fc1_wr[b].astype(F32)
        )

    got_c2, got_x2, got_z2, got_w2 = [None] * 2, [None] * 2, [None] * 2, [None]

    def fc2_product(zz):
        if zz == 0:
            got_dm()
            got_act()
        right = s.dm[...].reshape(4 * rows, width)
        for j in (1, 0):
            left = jnp.concatenate([s.act_g[0, j, zz], s.act_r[j, zz]], axis=-1)
            total = dot(left, right)
            if j:
                s.fc2_cs[zz] = total.astype(BF16)
                got_c2[zz] = push(s.fc2_cs.at[zz], s.fc2_cr.at[zz], PC)
            else:
                s.fc2[zz] = total

    def fc2_core(zz):
        got_c2[zz]()
        s.fc2[zz] = s.fc2[zz] + s.fc2_cr[zz].astype(F32)
        s.fc2_xs[zz] = s.fc2[zz, :, theirs].astype(BF16)
        got_x2[zz] = push(s.fc2_xs.at[zz], s.fc2_xr.at[zz], PX)
        s.fc2_all[2 * x + zz] = s.fc2[zz, :, mine]

    def fc2_swap():
        for zz in range(2):
            got_x2[zz]()
            s.fc2_all[2 * (1 - x) + zz] = s.fc2_xr[zz].astype(F32)
        for i, t in enumerate((3, 1)):
            s.fc2_zs[i] = s.fc2_all[zs[t]].astype(BF16)
            got_z2[i] = push(s.fc2_zs.at[i], s.fc2_zr.at[i], PZ1)

    def fc2_z():
        got_z2[0]()
        s.fc2_ws[...] = (s.fc2_all[zs[2]] + s.fc2_zr[0].astype(F32)).astype(BF16)
        got_w2[0] = push(s.fc2_ws, s.fc2_wr, PZ2)

    def fc2_end():
        got_z2[1]()
        got_w2[0]()
        out_w2[...] = s.fc2_all[zs[0]] + s.fc2_zr[1].astype(F32) + s.fc2_wr[...].astype(F32)

    yrows, zrows = 4 * blk, 2 * blk
    got_c, got_y, got_zsq, got_wsq = [None] * 4, [None] * 4, [None] * 4, [None] * 4

    def square(i, left_t, right):
        for leave in (1, 0):
            cc = 1 - c if leave else c
            left = jnp.concatenate([blocks(left_t, cc, y), blocks(left_t, cc, 1 - y)], axis=0)
            total = dot(left, right)
            if leave:
                s.sq_cs[i] = total.astype(BF16)
                got_c[i] = push(s.sq_cs.at[i], s.sq_cr.at[i], PC)
            else:
                s.sq[i] = total

    def square_core(i):
        got_c[i]()
        s.sq[i] = s.sq[i] + s.sq_cr[i].astype(F32)
        s.sq_ys[i] = s.sq[i, yrows:, :].astype(BF16)
        got_y[i] = push(s.sq_ys.at[i], s.sq_yr.at[i], PY)

    def square_y(i):
        got_y[i]()
        s.sq[i, :yrows, :] = s.sq[i, :yrows, :] + s.sq_yr[i].astype(F32)
        s.sq_zs[i] = s.sq[i, zrows:yrows, :].astype(BF16)
        got_zsq[i] = push(s.sq_zs.at[i], s.sq_zr.at[i], PZ1)

    def square_z(i):
        got_zsq[i]()
        s.sq_ws[i] = (s.sq[i, blk:zrows, :] + s.sq_zr[i, blk:, :].astype(F32)).astype(BF16)
        got_wsq[i] = push(s.sq_ws.at[i], s.sq_wr.at[i], PZ2)

    def square_end(i):
        got_wsq[i]()
        (out_wo, out_wv, out_wk, out_wq)[i][...] = (
            s.sq[i, :blk, :] + s.sq_zr[i, :blk, :].astype(F32) + s.sq_wr[i].astype(F32)
        )

    tables = (s.vec, s.vec2)
    landings = (s.vec_r, s.vec2_r)
    got_v = [None] * 2

    def vector_send(g, step, peer):
        got_v[g] = push(tables[g].at[step], landings[g].at[step], peer)

    def vector_add(g, step):
        got_v[g]()
        tables[g][step + 1] = tables[g][step] + landings[g][step]

    fc1_product(0)
    fc1_product(1)
    fc1_core(0)

    got_dh2()
    d_h2 = s.dh2[0].astype(F32) + s.dh2[1].astype(F32)
    d_resid = dy + normalise_back(d_h2 * gain_m, hat_m, inv_m)
    s.d_resid[...] = d_resid
    d_branch = (scale_a * d_resid).astype(BF16)
    s.dbr[...] = d_branch
    s.da[...] = dot_t(d_branch, s.wo[mine, :]).astype(BF16)

    for pair in range(heads // 2):
        q2 = stack(s.q[:, lanes(pair)])
        da2 = stack(s.da[:, lanes(pair)])
        prob = s.prob[pair]
        s.dv[:, lanes(pair)] = dot(prob.astype(BF16).T, da2).astype(BF16)
        d_prob = dot_t(da2, s.v[:, lanes(pair)])
        delta = jnp.sum(d_prob * prob, axis=-1, keepdims=True)
        ds = (prob * (d_prob - delta)).astype(BF16)
        s.dq[:, lanes(pair)] = (unstack(dot(ds, s.k[:, lanes(pair)])) * scale).astype(BF16)
        s.dk[:, lanes(pair)] = (dot(ds.T, q2) * scale).astype(BF16)
    fc1_core(1)

    square(1, s.hk_t, s.dv[...])
    square(2, s.hk_t, s.dk[...])
    square_core(1)
    square(3, s.hq_t, s.dq[...])
    square_core(2)
    s.att_t[mine, :] = s.att[x].T
    s.att_t[theirs, :] = s.att[1 - x].T
    square(0, s.att_t, s.dbr[:, mine])
    square_core(3)

    fc1_product(2)
    square_core(0)
    fc1_product(3)
    fc1_core(2)

    dhk = dot_t(s.dk[...], s.wk[...]) + dot_t(s.dv[...], s.wv[...])
    dhq = dot_t(s.dq[...], s.wq[...])
    s.dx[0] = dhk[:2 * rows] * gain_k
    s.dx[1] = dhk[2 * rows:] * gain_k + dhq * gain_q
    s.dx_s[...] = s.dx[:, other, :].astype(BF16)
    fc1_core(3)
    fc1_z(0)

    dbr_own = s.dbr[own, :].astype(F32)
    s.vec2[0, 0:1, :] = col_sum(dbr_own)
    s.vec2[0, 1:2, :] = col_sum(s.d_resid[own, :] * s.branch[own, :])
    s.vec2[0, 2:3, :] = jnp.zeros((1, width), F32)
    s.vec2[0, 3:4, :] = jnp.zeros((1, width), F32)
    s.vec2[0, 2:3, mine] = col_sum(s.dq[...].astype(F32))
    s.vec2[0, 3:4, mine] = col_sum(s.dv[...].astype(F32))
    hat_low = s.hat[2 * rows:, :]
    s.vec2[0, 4:5, :] = col_sum(dhq * hat_low)
    s.vec2[0, 5:6, :] = col_sum(dhq)
    s.vec2[0, 6:7, :] = col_sum(dhk * s.hat[...])
    s.vec2[0, 7:8, :] = col_sum(dhk)
    vector_send(0, 0, PC)
    vector_send(1, 0, PC)

    fc2_product(0)
    fc1_z(1)
    fc2_product(1)
    fc2_core(0)
    fc2_core(1)
    got_dx = push(s.dx_s, s.dx_r, PX)
    vector_add(0, 0)
    vector_send(0, 1, PX)
    vector_add(1, 0)
    vector_send(1, 1, PX)
    fc1_z(2)
    square_y(1)
    fc1_z(3)
    fc2_swap()

    got_mlp()
    mlp_own = s.mlp[own, :] + s.mlp_r[...].astype(F32) + b_fc2
    out_block[0] = (s.resid[own, :] + scale_m * mlp_own).astype(BF16)

    vector_add(0, 1)
    vector_send(0, 2, PY)
    vector_add(1, 1)
    vector_send(1, 2, PY)
    square_y(2)
    square_z(1)
    fc2_z()
    square_y(3)
    square_z(2)
    square_y(0)
    vector_add(0, 2)
    vector_send(0, 3, PZ1)
    vector_add(1, 2)
    vector_send(1, 3, PZ1)
    square_z(3)

    got_dx()
    dx_l = s.dx[0, own, :] + s.dx_r[0].astype(F32)
    dx_q = s.dx[1, own, :] + s.dx_r[1].astype(F32)
    out_dl[0] = normalise_back(dx_l, hat_l, inv_l)
    out_dq[0] = s.d_resid[own, :] + normalise_back(dx_q, hat_q, inv_q)

    for b in range(nb):
        fc1_end(b)
    square_z(0)
    vector_add(0, 3)
    vector_send(0, 4, PZ2)
    vector_add(1, 3)
    vector_send(1, 4, PZ2)
    fc2_end()
    square_end(1)
    square_end(2)
    square_end(3)
    square_end(0)
    for g in range(2):
        vector_add(g, 4)
        out_vec[g * 8:g * 8 + 8, :] = tables[g][5]
    for copy in sent:
        copy.wait_send()


def fused(share, args):
    (queries, latents, positions, vis_ok, msk_ok, dy, w_query, w_key, w_value, w_out, w_fc1, w_fc2) = args[:12]
    vectors = args[12:]
    _, rows, width = queries.shape
    ff = w_fc1.shape[1]
    half = width // 2
    blk, fblk, hid = width // GROUPS, ff // GROUPS, ff // 2
    nb = hid // half
    pairs = half // (2 * HEAD_DIM)
    vm = pltpu.VMEM
    scratch = dict(
        send=pltpu.SemaphoreType.DMA((96,)),
        recv=pltpu.SemaphoreType.DMA((96,)),
        load=pltpu.SemaphoreType.DMA((16,)),
        dy=vm((2 * rows, width), BF16),
        qraw=vm((2 * rows, width), BF16),
        lraw=vm((2 * rows, width), BF16),
        ppos=vm((1, rows), jnp.int32),
        w2=vm((hid, width), BF16),
        w1=vm((width, hid), BF16),
        wo=vm((width, width), BF16),
        wk=vm((width, half), BF16),
        wv=vm((width, half), BF16),
        wq=vm((width, half), BF16),
        qin=vm((2 * rows, width), F32),
        hat=vm((4 * rows, width), F32),
        hq=vm((2 * rows, width), BF16),
        hk=vm((4 * rows, width), BF16),
        hq_t=vm((width, 2 * rows), BF16),
        hk_t=vm((width, 4 * rows), BF16),
        att_t=vm((width, 2 * rows), BF16),
        h2_t=vm((width, 2 * rows), BF16),
        act_t=vm((hid, 2 * rows), BF16),
        q=vm((2 * rows, half), BF16),
        k=vm((4 * rows, half), BF16),
        v=vm((4 * rows, half), BF16),
        prob=vm((pairs, 4 * rows, 4 * rows), F32),
        att=vm((2, 2 * rows, half), BF16),
        branch=vm((2 * rows, width), F32),
        resid=vm((2 * rows, width), F32),
        d_resid=vm((2 * rows, width), F32),
        mlp=vm((2 * rows, width), F32),
        mlp_s=vm((rows, width), BF16),
        mlp_r=vm((rows, width), BF16),
        d_act=vm((nb, 2 * rows, half), F32),
        dm=vm((2, 2 * rows, width), BF16),
        h2_g=vm((2, 2, 4 * blk, 2 * rows), BF16),
        h2_r=vm((2, 4 * blk, 2 * rows), BF16),
        act=vm((nb, 2 * rows, half), BF16),
        act_g=vm((2, 2, 2, fblk, 2 * rows), BF16),
        act_r=vm((2, 2, fblk, 2 * rows), BF16),
        dp=vm((2, nb, 2 * rows, half), BF16),
        dh2=vm((2, 2 * rows, width), BF16),
        dbr=vm((2 * rows, width), BF16),
        da=vm((2 * rows, half), BF16),
        dq=vm((2 * rows, half), BF16),
        dk=vm((4 * rows, half), BF16),
        dv=vm((4 * rows, half), BF16),
        dx=vm((2, 2 * rows, width), F32),
        dx_s=vm((2, rows, width), BF16),
        dx_r=vm((2, rows, width), BF16),
        sq=vm((4, 8 * blk, half), F32),
        sq_cs=vm((4, 8 * blk, half), BF16),
        sq_cr=vm((4, 8 * blk, half), BF16),
        sq_ys=vm((4, 4 * blk, half), BF16),
        sq_yr=vm((4, 4 * blk, half), BF16),
        sq_zs=vm((4, 2 * blk, half), BF16),
        sq_zr=vm((4, 2 * blk, half), BF16),
        sq_ws=vm((4, blk, half), BF16),
        sq_wr=vm((4, blk, half), BF16),
        fc2=vm((2, fblk, width), F32),
        fc2_cs=vm((2, fblk, width), BF16),
        fc2_cr=vm((2, fblk, width), BF16),
        fc2_xs=vm((2, fblk, half), BF16),
        fc2_xr=vm((2, fblk, half), BF16),
        fc2_all=vm((4, fblk, half), F32),
        fc2_zs=vm((2, fblk, half), BF16),
        fc2_zr=vm((2, fblk, half), BF16),
        fc2_ws=vm((fblk, half), BF16),
        fc2_wr=vm((fblk, half), BF16),
        fc1=vm((nb, 4 * blk, half), F32),
        fc1_cs=vm((nb, 4 * blk, half), BF16),
        fc1_cr=vm((nb, 4 * blk, half), BF16),
        fc1_zs=vm((nb, 2 * blk, half), BF16),
        fc1_zr=vm((nb, 2 * blk, half), BF16),
        fc1_ws=vm((nb, blk, half), BF16),
        fc1_wr=vm((nb, blk, half), BF16),
        vec=vm((6, 8, width), F32),
        vec_r=vm((5, 8, width), F32),
        vec2=vm((6, 8, width), F32),
        vec2_r=vm((5, 8, width), F32),
    )
    ANY = pl.BlockSpec(memory_space=pl.ANY)
    VMEM = pl.BlockSpec(memory_space=pltpu.VMEM)
    sds = jax.ShapeDtypeStruct
    return pl.pallas_call(
        functools.partial(kernel, (rows, width, ff, share)),
        out_shape=(
            sds((1, rows, width), BF16),
            sds((1, rows, width), F32),
            sds((1, rows, width), F32),
            sds((blk, half), F32),
            sds((blk, half), F32),
            sds((blk, half), F32),
            sds((blk, half), F32),
            sds((blk, ff // 2), F32),
            sds((fblk, half), F32),
            sds((16, width), F32),
        ),
        in_specs=[ANY, ANY, VMEM, VMEM, VMEM, ANY] + [ANY] * 6 + [VMEM] * 13,
        out_specs=[VMEM] * 10,
        scratch_shapes=[scratch],
        compiler_params=pltpu.CompilerParams(
            collective_id=0, has_side_effects=True, vmem_limit_bytes=60 << 20
        ),
        cost_estimate=pl.CostEstimate(
            flops=6 * 10**9, bytes_accessed=16 * 10**6, transcendentals=10**6
        ),
    )(queries, latents, positions, vis_ok, msk_ok, dy, w_query, w_key, w_value, w_out, w_fc1, w_fc2, *vectors)


def finish_kernel(count, *refs):
    arrays, table = refs[:count], refs[count]
    outs, rows = refs[count + 1:2 * count + 1], refs[2 * count + 1:-1]
    sems = refs[-1]
    copies = [
        pltpu.make_async_copy(src, dst, sems.at[i]) for i, (src, dst) in enumerate(zip(arrays, outs))
    ]
    for copy in copies:
        copy.start()
    width = table.shape[1]
    parts = rows[0].shape[0] // width
    for k in range(parts):
        rows[0][k * width:(k + 1) * width] = table[k, :]
    for k, row in enumerate(rows[1:]):
        row[...] = table[parts + k, :]
    for copy in copies:
        copy.wait()


def finish(arrays, table, ff):
    count, width = len(arrays), table.shape[1]
    sds = jax.ShapeDtypeStruct
    vectors = table.shape[0] - ff // width
    ANY = pl.BlockSpec(memory_space=pl.ANY)
    VMEM = pl.BlockSpec(memory_space=pltpu.VMEM)
    return pl.pallas_call(
        functools.partial(finish_kernel, count),
        out_shape=tuple(sds(a.shape, a.dtype) for a in arrays)
        + (sds((ff,), F32),)
        + (sds((width,), F32),) * vectors,
        in_specs=[VMEM] * (count + 1),
        out_specs=[ANY] * count + [VMEM] * (1 + vectors),
        scratch_shapes=[pltpu.SemaphoreType.DMA((count,))],
    )(*arrays, table)


def per_device(
    queries, latents, positions, visible_valid, masked_valid,
    w_query, b_query, w_key, w_value, b_value, w_out, b_out, w_fc1, b_fc1, w_fc2, b_fc2,
    gain_query, shift_query, gain_keys, shift_keys, gain_mlp, shift_mlp, scale_attn, scale_mlp,
    out_grad,
):
    parts = lax.axis_size("dp")
    share = parts // GROUPS
    out = fused(
        share,
        (
            queries, latents, positions, visible_valid, masked_valid, out_grad,
            w_query, w_key, w_value, w_out, w_fc1, w_fc2,
            b_query, b_value, b_out, b_fc1, b_fc2,
            gain_query, shift_query, gain_keys, shift_keys, gain_mlp, shift_mlp, scale_attn, scale_mlp,
        ),
    )
    block_out, d_queries, d_latents, wq, wk, wv, wo, w1, w2, vec = out
    if share > 1:
        groups = [[n * share + i for i in range(share)] for n in range(GROUPS)]
        wq, wk, wv, wo, w1, w2 = (
            lax.psum_scatter(
                w, "dp", scatter_dimension=0, axis_index_groups=groups, tiled=True
            )
            for w in (wq, wk, wv, wo, w1, w2)
        )
        vec = lax.psum(vec, "dp", axis_index_groups=groups)
    arrays = (block_out, d_queries, d_latents, wq, wk, wv, wo, w1, w2)
    done = finish(arrays, vec, w_fc1.shape[1])
    block_out, d_queries, d_latents, wq, wk, wv, wo, w1, w2, b1 = done[:10]
    b2, sm, gm, hm, bo, sa, bq, bv, gq, hq, gk, hk = done[10:]
    return (
        block_out, d_queries, d_latents,
        wq, bq, wk, wv, bv, wo, bo, w1, b1, w2, b2,
        gq, hq, gk, hk, gm, hm, sa, sm,
    )


def solution(mesh):
    rows3 = P("dp", "qry", None)
    split = P("dp", "qry")
    full = P()
    return jax.shard_map(
        per_device,
        mesh=mesh,
        in_specs=(rows3, rows3, split, P("dp", None), P("dp", None)) + (full,) * 19 + (rows3,),
        out_specs=(
            rows3, rows3, rows3,
            split, full, split, split, full, split, full, split, full, split,
        ) + (full,) * 9,
        check_vma=False,
    )
```

```python
import functools
import math
import types

import jax
import jax.numpy as jnp
from jax import lax
from jax.experimental import pallas as pl
from jax.experimental.pallas import tpu as pltpu
from jax.sharding import PartitionSpec as P

HEAD_DIM = 64
MESH = pl.DeviceIdType.MESH
F32 = jnp.float32
BF16 = jnp.bfloat16
GROUPS = 16
Z_ORDER = (0, 2, 1, 3)


def dot(a, b):
    return lax.dot_general(a, b, (((1,), (0,)), ((), ())), preferred_element_type=F32)


def dot_t(a, b):
    return lax.dot_general(a, b, (((1,), (1,)), ((), ())), preferred_element_type=F32)


def col_sum(a):
    return jnp.sum(a, axis=0, keepdims=True)


def normalise(v):
    centre = v - jnp.mean(v, axis=-1, keepdims=True)
    spread = jnp.mean(centre * centre, axis=-1, keepdims=True)
    inv = lax.rsqrt(spread + 1e-06)
    return centre * inv, inv


def normalise_back(grad_hat, hat, inv):
    m1 = jnp.mean(grad_hat, axis=-1, keepdims=True)
    m2 = jnp.mean(grad_hat * hat, axis=-1, keepdims=True)
    return inv * (grad_hat - m1 - hat * m2)


def sinusoid(places, width):
    index = lax.broadcasted_iota(jnp.int32, (1, width), 1)
    half = index // 2
    freq = jnp.exp(-(2.0 * half.astype(F32) / width) * math.log(10000.0))
    odd = (index - 2 * half).astype(F32)
    angle = places * freq
    turns = jnp.floor(angle * (2.0 / math.pi) + 0.5)
    rest = angle - turns * 1.5703125
    rest = rest - turns * 4.8351287841796875e-4
    rest = rest - turns * 3.1385570764541626e-07
    sq = rest * rest
    sine = rest * (
        1.0 + sq * (-1.0 / 6 + sq * (1.0 / 120 + sq * (-1.0 / 5040 + sq * (1.0 / 362880))))
    )
    cosine = 1.0 + sq * (-0.5 + sq * (1.0 / 24 + sq * (-1.0 / 720 + sq * (1.0 / 40320))))
    quarter = turns + odd
    pairs = jnp.floor(quarter * 0.5)
    parity = quarter - 2.0 * pairs
    flips = pairs - 2.0 * jnp.floor(pairs * 0.5)
    value = jnp.where(parity > 0.5, cosine, sine)
    return jnp.where(flips > 0.5, -value, value)


def kernel(
    shape,
    queries, latents, positions, vis_ok, msk_ok, dy_in,
    w_query, w_key, w_value, w_out, w_fc1, w_fc2,
    b_query, b_value, b_out, b_fc1, b_fc2,
    gain_q, shift_q, gain_k, shift_k, gain_m, shift_m, scale_a, scale_m,
    out_block, out_dq, out_dl, out_wq, out_wk, out_wv, out_wo, out_w1, out_w2, out_vec,
    s,
):
    s = types.SimpleNamespace(**s)
    rows, width, ff, share = shape
    half = width // 2
    heads = half // HEAD_DIM
    blk = width // GROUPS
    fblk = ff // GROUPS
    hid = ff // 2
    nb = hid // half
    scale = 1.0 / math.sqrt(HEAD_DIM)

    x = lax.axis_index("qry")
    place = lax.axis_index("dp")
    n = place // share
    low = place - n * share
    z = n // 4
    y = (n // 2) % 2
    c = n % 2
    zs = (z, z + 1 - 2 * (z % 2), (z + 2) % 4, 3 - z)

    def dev(zz, yy, cc, xx):
        return (((zz * 2 + yy) * 2 + cc) * share + low, xx)

    PX = dev(z, y, c, 1 - x)
    PY = dev(z, 1 - y, c, x)
    PC = dev(z, y, 1 - c, x)
    PZ1 = dev(zs[1], y, c, x)
    PZ2 = dev(zs[2], y, c, x)
    PYZ1 = dev(zs[1], 1 - y, c, x)
    z_low = z % 2
    z_high = z // 2

    counter = [0]
    sent = []

    def push(src, dst, peer, landing=None):
        i = counter[0]
        counter[0] += 1

        def describe(to):
            return pltpu.make_async_remote_copy(
                src_ref=src, dst_ref=to, send_sem=s.send.at[i], recv_sem=s.recv.at[i],
                device_id=peer, device_id_type=MESH,
            )

        copy = describe(dst)
        copy.start()
        sent.append(copy)
        arrival = copy if landing is None else describe(landing)
        return arrival.wait_recv

    barrier = pltpu.get_barrier_semaphore()

    def tell(sem, peer):
        pl.semaphore_signal(sem, inc=1, device_id=peer, device_id_type=MESH)

    def tell_z(sem):
        @pl.when(z > 0)
        def _():
            tell(sem, dev(z - 1, y, c, x))

        @pl.when(z < 3)
        def _():
            tell(sem, dev(z + 1, y, c, x))

    z_links = 2 - (z + 3) // 3 + (z + 1) // 2 - z // 3
    for peer in (PX, PY, PC):
        tell(barrier, peer)
    tell_z(barrier)

    loads = []

    def load(src, dst):
        copy = pltpu.make_async_copy(src, dst, s.load.at[len(loads)])
        copy.start()
        loads.append(copy)
        return copy.wait

    own = pl.ds(pl.multiple_of(x * rows, rows), rows)
    other = pl.ds(pl.multiple_of((1 - x) * rows, rows), rows)
    low_own = pl.ds(pl.multiple_of((2 + x) * rows, rows), rows)
    low_other = pl.ds(pl.multiple_of((3 - x) * rows, rows), rows)
    mine = pl.ds(pl.multiple_of(x * half, half), half)
    theirs = pl.ds(pl.multiple_of((1 - x) * half, half), half)
    units = pl.ds(pl.multiple_of(x * hid, hid), hid)

    def row_of(ref, i):
        wait = load(ref, s.rows.at[i])

        def value():
            wait()
            return s.rows[i].reshape(1, width)

        return value

    load_q = load(queries.at[0], s.qraw.at[own])
    load_p = load(positions, s.pos)
    load_l = load(latents.at[0], s.lraw.at[own])
    gain_q, shift_q, gain_k, shift_k = (
        row_of(ref, i) for i, ref in enumerate((gain_q, shift_q, gain_k, shift_k))
    )
    load_wk = load(w_key.at[:, mine], s.wk)
    load_wv = load(w_value.at[:, mine], s.wv)
    load_wq = load(w_query.at[:, mine], s.wq)
    b_query, b_value, b_out, b_fc2, gain_m, shift_m, scale_a, scale_m = (
        row_of(ref, 4 + i)
        for i, ref in enumerate((b_query, b_value, b_out, b_fc2, gain_m, shift_m, scale_a, scale_m))
    )
    load_b1 = load(b_fc1, s.b_fc1)
    load_ok = [load(vis_ok, s.ok.at[0]), load(msk_ok, s.ok.at[1])]
    load_dy = load(dy_in.at[0], s.dy.at[0, own])
    load_w2 = load(w_fc2.at[units], s.w2)
    load_wo = load(w_out, s.wo)
    load_w1 = load(w_fc1.at[:, units], s.w1)

    eye = lax.broadcasted_iota(jnp.int32, (rows, rows), 0) == lax.broadcasted_iota(
        jnp.int32, (rows, rows), 1
    )

    gain_q, shift_q, gain_k, shift_k = gain_q(), shift_q(), gain_k(), shift_k()

    def qry_half(pos_ref, at, low_at):
        row = jnp.broadcast_to(pos_ref[...].astype(F32), (rows, rows))
        places = jnp.sum(jnp.where(eye, row, 0.0), axis=1, keepdims=True)
        qin = s.qraw[at, :].astype(F32) + sinusoid(places, width)
        s.qin[at, :] = qin
        hat, inv = normalise(qin)
        s.hat[low_at, :] = hat
        hq = (hat * gain_q + shift_q).astype(BF16)
        hkq = (hat * gain_k + shift_k).astype(BF16)
        s.hq[at, :] = hq
        s.hk[low_at, :] = hkq
        return hat, inv, hq, hkq

    def lat_half(at):
        hat, inv = normalise(s.lraw[at, :].astype(F32))
        s.hat[at, :] = hat
        hkl = (hat * gain_k + shift_k).astype(BF16)
        s.hk[at, :] = hkl
        return hat, inv, hkl

    def project(hq, hkq, hkl, at, low_at):
        both = jnp.concatenate([hkl, hkq], axis=0)
        k = dot(both, s.wk[...]).astype(BF16)
        s.k[at, :] = k[:rows]
        s.k[low_at, :] = k[rows:]
        v = (dot(both, s.wv[...]) + my_b_value).astype(BF16)
        s.v[at, :] = v[:rows]
        s.v[low_at, :] = v[rows:]
        s.q[at, :] = (dot(hq, s.wq[...]) + my_b_query).astype(BF16)

    load_q()
    load_p()
    hat_q, inv_q, hq, hkq = qry_half(s.pos, own, low_own)
    load_l()
    hat_l, inv_l, hkl = lat_half(own)

    pl.semaphore_wait(barrier, 3 + z_links)
    got_p = push(positions, s.ppos, PX)
    got_q = push(queries.at[0], s.qraw.at[own], PX, s.qraw.at[other])
    got_l = push(latents.at[0], s.lraw.at[own], PX, s.lraw.at[other])
    got_dy = push(dy_in.at[0], s.dy.at[0, own], PX, s.dy.at[0, other])
    got_dy_y = push(dy_in.at[0], s.dy.at[1, own], PY)
    got_dy_z = push(dy_in.at[0], s.dy.at[2, own], PZ1)
    tell_z(s.ready)

    load_wk()
    load_wv()
    load_wq()
    b_query, b_value, b_out, b_fc2, gain_m, shift_m, scale_a, scale_m = (
        value() for value in (b_query, b_value, b_out, b_fc2, gain_m, shift_m, scale_a, scale_m)
    )
    load_b1()
    my_b_value = jnp.where(x == 0, b_value[:, :half], b_value[:, half:])
    my_b_query = jnp.where(x == 0, b_query[:, :half], b_query[:, half:])
    b_fc1 = s.b_fc1[...].reshape(1, ff)
    my_b_fc1 = jnp.where(x == 0, b_fc1[:, :hid], b_fc1[:, hid:])
    project(hq, hkq, hkl, own, low_own)
    got_p()
    got_q()
    _, _, hq_o, hkq_o = qry_half(s.ppos, other, low_other)
    pl.semaphore_wait(s.ready, z_links)
    got_dy_yz = push(dy_in.at[0], s.dy.at[3, own], PYZ1)
    got_l()
    _, _, hkl_o = lat_half(other)
    project(hq_o, hkq_o, hkl_o, other, low_other)
    for wait in load_ok:
        wait()

    ok = jnp.concatenate([s.ok[0], s.ok[1]], axis=1) > 0
    lane = lax.broadcasted_iota(jnp.int32, (2 * rows, 2 * HEAD_DIM), 1)
    first = lane < HEAD_DIM

    def stack(pair):
        zero = jnp.zeros_like(pair)
        return jnp.concatenate([jnp.where(first, pair, zero), jnp.where(first, zero, pair)], axis=0)

    def unstack(both):
        return jnp.where(first, both[:2 * rows], both[2 * rows:])

    def lanes(pair):
        return slice(pair * 2 * HEAD_DIM, (pair + 1) * 2 * HEAD_DIM)

    for pair in range(heads // 2):
        raw = dot_t(stack(s.q[:, lanes(pair)]), s.k[:, lanes(pair)]) * scale
        scores = jnp.where(ok, raw, -1e30)
        peak = jnp.max(scores, axis=-1, keepdims=True)
        weight = jnp.exp(scores - peak)
        prob = weight * (1.0 / jnp.sum(weight, axis=-1, keepdims=True))
        s.prob[pair] = prob
        s.att[x, :, lanes(pair)] = unstack(dot(prob.astype(BF16), s.v[:, lanes(pair)])).astype(BF16)
    got_att = push(s.att.at[x], s.att.at[x], PX, s.att.at[1 - x])

    got_dy()
    got_dy_y2 = push(s.dy.at[0, other], s.dy.at[1, other], PY)
    got_dy_z2 = push(s.dy.at[0, other], s.dy.at[2, other], PZ1)
    got_dy_yz2 = push(s.dy.at[0, other], s.dy.at[3, other], PYZ1)
    s.hq_t[...] = s.hq[...].T
    s.hk_t[...] = s.hk[...].T
    load_dy()
    load_w2()
    dy = s.dy[0].astype(F32)
    d_mlp = (scale_m * dy).astype(BF16)
    s.dm[0] = d_mlp
    for b in range(nb):
        s.d_act[b] = dot_t(d_mlp, s.w2[b * half:(b + 1) * half, :])
    load_wo()
    s.branch[...] = dot(s.att[x], s.wo[mine, :]) + b_out
    got_att()

    branch = s.branch[...] + dot(s.att[1 - x], s.wo[theirs, :])
    resid = s.qin[...] + scale_a * branch
    hat_m, inv_m = normalise(resid)
    h_two = (hat_m * gain_m + shift_m).astype(BF16)

    def blocks(ref, cc, yy):
        return jnp.concatenate(
            [
                ref[pl.ds(pl.multiple_of(((zs[t] * 2 + yy) * 2 + cc) * blk, blk), blk), :]
                for t in Z_ORDER
            ],
            axis=0,
        )

    s.h2_t[...] = h_two.T
    s.h2_g[1, 0] = blocks(s.h2_t, c, 1 - y)
    s.h2_g[1, 1] = blocks(s.h2_t, 1 - c, 1 - y)
    got_h2 = push(s.h2_g.at[1], s.h2_r, PY)
    load_w1()
    d_h2 = jnp.zeros((2 * rows, width), F32)
    got_dp = []
    for b in range(nb):
        cols = slice(b * half, (b + 1) * half)
        pre = dot(h_two, s.w1[:, cols]) + my_b_fc1[:, cols]
        cdf = 0.5 * (1.0 + lax.erf(pre * math.sqrt(0.5)))
        act = (pre * cdf).astype(BF16)
        slope = cdf + pre * (jnp.exp(-0.5 * pre * pre) * (1.0 / math.sqrt(2 * math.pi)))
        d_pre = (s.d_act[b] * slope).astype(BF16)
        s.act[b] = act
        s.dp[0, b] = d_pre
        got_dp.append(push(s.dp.at[0, b], s.dp.at[1, b], PY))
        d_h2 += dot_t(d_pre, s.w1[:, cols])
    s.dh2[0] = d_h2.astype(BF16)
    got_dh2 = push(s.dh2.at[0], s.dh2.at[1], PX)

    for b in range(nb):
        s.act_t[b * half:(b + 1) * half, :] = s.act[b].T
    got_act = []
    for i, (zz, yy) in enumerate(
        ((z_low, y), (z_low, 1 - y), (1 - z_low, y), (1 - z_low, 1 - y))
    ):
        for j, cc in enumerate((c, 1 - c)):
            at = pl.ds(pl.multiple_of((zz * 4 + yy * 2 + cc) * fblk, fblk), fblk)
            s.act_s[i, j] = s.act_t[at, :]
        if i:
            got_act.append(push(s.act_s.at[i], s.act_r.at[i - 1], (PY, PZ1, PYZ1)[i - 1]))

    s.branch[...] = branch
    s.resid[...] = resid
    s.h2_g[0, 0] = blocks(s.h2_t, c, y)
    s.h2_g[0, 1] = blocks(s.h2_t, 1 - c, y)
    mlp = jnp.zeros((2 * rows, width), F32)
    s.vec[0, 0:4, :] = jnp.zeros((4, width), F32)
    for b in range(nb):
        cols = slice(b * half, (b + 1) * half)
        mlp += dot(s.act[b], s.w2[cols, :])
        s.vec[0, pl.ds(2 * x + b // 2, 1), (b % 2) * half:(b % 2 + 1) * half] = col_sum(
            s.dp[0, b].astype(F32)
        )
    s.mlp[...] = mlp
    s.mlp_s[...] = s.mlp[other, :].astype(BF16)
    got_mlp = push(s.mlp_s, s.mlp_r, PX)
    dy_own = s.dy[0, own, :].astype(F32)
    s.vec[0, 4:5, :] = col_sum(s.dm[0, own, :].astype(F32))
    s.vec[0, 5:6, :] = col_sum(dy * mlp) + b_fc2 * col_sum(dy_own)
    s.vec[0, 6:7, :] = col_sum(d_h2 * hat_m)
    s.vec[0, 7:8, :] = col_sum(d_h2)

    got_c1, got_z1, got_w1 = [None] * nb, [None] * nb, [None] * nb

    def fc1_product(b):
        if b == 0:
            got_h2()
        got_dp[b]()
        right = s.dp[:, b].reshape(4 * rows, half)
        left = jnp.concatenate([s.h2_g[0], s.h2_r[...]], axis=-1)
        s.fc1_cs[b] = dot(left[1], right).astype(BF16)
        got_c1[b] = push(s.fc1_cs.at[b], s.fc1_cr.at[b], PC)
        s.fc1[b] = dot(left[0], right)

    def fc1_core(b):
        got_c1[b]()
        s.fc1[b] = s.fc1[b] + s.fc1_cr[b].astype(F32)
        s.fc1_zs[b] = s.fc1[b, 2 * blk:, :].astype(BF16)
        got_z1[b] = push(s.fc1_zs.at[b], s.fc1_zr.at[b], PZ1)

    def fc1_z(b):
        got_z1[b]()
        s.fc1_ws[b] = (s.fc1[b, blk:2 * blk, :] + s.fc1_zr[b, blk:, :].astype(F32)).astype(BF16)
        got_w1[b] = push(s.fc1_ws.at[b], s.fc1_wr.at[b], PZ2)

    def fc1_end(b):
        got_w1[b]()
        out_w1[:, b * half:(b + 1) * half] = (
            s.fc1[b, :blk, :] + s.fc1_zr[b, :blk, :].astype(F32) + s.fc1_wr[b].astype(F32)
        )

    got_c2, got_x2, got_w2 = [None], [None], [None]

    def fc2_product():
        for got in [got_dy_y, got_dy_z, got_dy_yz, got_dy_y2, got_dy_z2, got_dy_yz2] + got_act:
            got()
        for g in range(1, 4):
            s.dm[g] = (scale_m * s.dy[g].astype(F32)).astype(BF16)
        right = s.dm[...].reshape(8 * rows, width)
        for j in (1, 0):
            left = jnp.concatenate([s.act_s[0, j]] + [s.act_r[g, j] for g in range(3)], axis=-1)
            total = dot(left, right)
            if j:
                s.fc2_cs[...] = total.astype(BF16)
                got_c2[0] = push(s.fc2_cs, s.fc2_cr, PC)
            else:
                s.fc2[...] = total

    def fc2_core():
        got_c2[0]()
        s.fc2[...] = s.fc2[...] + s.fc2_cr[...].astype(F32)
        s.fc2_xs[...] = s.fc2[:, theirs].astype(BF16)
        got_x2[0] = push(s.fc2_xs, s.fc2_xr, PX)
        s.fc2_all[x] = s.fc2[:, mine]

    def fc2_swap():
        got_x2[0]()
        s.fc2_all[1 - x] = s.fc2_xr[...].astype(F32)
        s.fc2_ws[...] = s.fc2_all[1 - z_high].astype(BF16)
        got_w2[0] = push(s.fc2_ws, s.fc2_wr, PZ2)

    def fc2_end():
        got_w2[0]()
        out_w2[...] = s.fc2_all[z_high] + s.fc2_wr[...].astype(F32)

    yrows, zrows = 4 * blk, 2 * blk
    got_c, got_y, got_yr, got_zsq, got_wsq = ([None] * 4 for _ in range(5))

    def square(i, left_t, right):
        for leave in (1, 0):
            cc = 1 - c if leave else c
            left = jnp.concatenate([blocks(left_t, cc, y), blocks(left_t, cc, 1 - y)], axis=0)
            total = dot(left, right)
            if leave:
                s.sq_cs[i] = total.astype(BF16)
                got_c[i] = push(s.sq_cs.at[i], s.sq_cr.at[i], PC)
            else:
                s.sq[i] = total

    def square_core(i):
        got_c[i]()
        s.sq[i] = s.sq[i] + s.sq_cr[i].astype(F32)
        s.sq_ys[i, 1] = s.sq[i, yrows + zrows:, :].astype(BF16)
        got_y[i] = push(s.sq_ys.at[i, 1], s.sq_yr.at[i, 1], PY)

    def square_core_rest(i):
        s.sq_ys[i, 0] = s.sq[i, yrows:yrows + zrows, :].astype(BF16)
        got_yr[i] = push(s.sq_ys.at[i, 0], s.sq_yr.at[i, 0], PY)

    def square_y(i):
        got_y[i]()
        s.sq_zs[i] = (s.sq[i, zrows:yrows, :] + s.sq_yr[i, 1].astype(F32)).astype(BF16)
        got_zsq[i] = push(s.sq_zs.at[i], s.sq_zr.at[i], PZ1)

    def square_z(i):
        got_yr[i]()
        got_zsq[i]()
        s.sq[i, :zrows, :] = (
            s.sq[i, :zrows, :] + s.sq_yr[i, 0].astype(F32) + s.sq_zr[i].astype(F32)
        )
        s.sq_ws[i] = s.sq[i, blk:zrows, :].astype(BF16)
        got_wsq[i] = push(s.sq_ws.at[i], s.sq_wr.at[i], PZ2)

    def square_end(i):
        got_wsq[i]()
        (out_wo, out_wv, out_wk, out_wq)[i][...] = (
            s.sq[i, :blk, :] + s.sq_wr[i].astype(F32)
        )

    tables = (s.vec, s.vec2)
    landings = (s.vec_r, s.vec2_r)
    got_v = [None] * 2

    def vector_send(g, step, peer):
        got_v[g] = push(tables[g].at[step], landings[g].at[step], peer)

    def vector_add(g, step):
        got_v[g]()
        tables[g][step + 1] = tables[g][step] + landings[g][step]

    live = types.SimpleNamespace()

    def d_resid():
        got_dh2()
        d_h2 = s.dh2[0].astype(F32) + s.dh2[1].astype(F32)
        d_resid = dy + normalise_back(d_h2 * gain_m, hat_m, inv_m)
        s.d_resid[...] = d_resid
        d_branch = (scale_a * d_resid).astype(BF16)
        s.dbr[...] = d_branch
        s.da[...] = dot_t(d_branch, s.wo[mine, :]).astype(BF16)

    def attention_back():
        for pair in range(heads // 2):
            q2 = stack(s.q[:, lanes(pair)])
            da2 = stack(s.da[:, lanes(pair)])
            prob = s.prob[pair]
            s.dv[:, lanes(pair)] = dot(prob.astype(BF16).T, da2).astype(BF16)
            d_prob = dot_t(da2, s.v[:, lanes(pair)])
            delta = jnp.sum(d_prob * prob, axis=-1, keepdims=True)
            ds = (prob * (d_prob - delta)).astype(BF16)
            s.dq[:, lanes(pair)] = (unstack(dot(ds, s.k[:, lanes(pair)])) * scale).astype(BF16)
            s.dk[:, lanes(pair)] = (dot(ds.T, q2) * scale).astype(BF16)

    def square_product(i):
        if i == 0:
            s.att_t[mine, :] = s.att[x].T
            s.att_t[theirs, :] = s.att[1 - x].T
            square(0, s.att_t, s.dbr[:, mine])
        elif i < 3:
            square(i, s.hk_t, (s.dv, s.dk)[i - 1][...])
        else:
            square(3, s.hq_t, s.dq[...])

    def norms_back():
        dhk = dot_t(s.dk[...], s.wk[...]) + dot_t(s.dv[...], s.wv[...])
        dhq = dot_t(s.dq[...], s.wq[...])
        s.dx[0] = dhk[:2 * rows] * gain_k
        s.dx[1] = dhk[2 * rows:] * gain_k + dhq * gain_q
        s.dx_s[...] = s.dx[:, other, :].astype(BF16)
        s.vec2[0, 0:1, :] = col_sum(s.dbr[own, :].astype(F32))
        s.vec2[0, 1:2, :] = col_sum(s.d_resid[own, :] * s.branch[own, :])
        s.vec2[0, 2:3, :] = jnp.zeros((1, width), F32)
        s.vec2[0, 3:4, :] = jnp.zeros((1, width), F32)
        s.vec2[0, 2:3, mine] = col_sum(s.dq[...].astype(F32))
        s.vec2[0, 3:4, mine] = col_sum(s.dv[...].astype(F32))
        s.vec2[0, 4:5, :] = col_sum(dhq * s.hat[2 * rows:, :])
        s.vec2[0, 5:6, :] = col_sum(dhq)
        s.vec2[0, 6:7, :] = col_sum(dhk * s.hat[...])
        s.vec2[0, 7:8, :] = col_sum(dhk)

    def norms_send():
        live.got_dx = push(s.dx_s, s.dx_r, PX)

    def norms_end():
        live.got_dx()
        dx_l = s.dx[0, own, :] + s.dx_r[0].astype(F32)
        dx_q = s.dx[1, own, :] + s.dx_r[1].astype(F32)
        out_dl[0] = normalise_back(dx_l, hat_l, inv_l)
        out_dq[0] = s.d_resid[own, :] + normalise_back(dx_q, hat_q, inv_q)

    def block_end():
        got_mlp()
        mlp_own = s.mlp[own, :] + s.mlp_r[...].astype(F32) + b_fc2
        out_block[0] = (s.resid[own, :] + scale_m * mlp_own).astype(BF16)

    routes = (PZ2, PZ1, PY, PX, PC)

    def vector(g, step):
        if step:
            vector_add(g, step - 1)
        if step < 5:
            vector_send(g, step, routes[step])
        else:
            out_vec[g * 8:g * 8 + 8, :] = tables[g][5]

    V, K, Q, O = 1, 2, 3, 0
    vector(0, 0)
    fc1_product(0)
    d_resid()
    fc1_core(0)
    attention_back()
    fc1_product(1)
    norms_back()
    vector(0, 1)
    fc1_product(2)
    square_product(V)
    fc1_core(1)
    square_product(O)
    fc1_core(2)
    block_end()
    square_core(V)
    vector(1, 0)
    fc1_product(3)
    square_product(K)
    square_core(O)
    fc1_core(3)
    square_product(Q)
    fc1_z(0)
    square_core_rest(V)
    square_core_rest(O)
    fc1_z(1)
    fc1_z(2)
    fc2_product()
    square_y(V)
    square_core(K)
    square_y(O)
    fc2_core()
    square_core(Q)
    square_core_rest(K)
    vector(1, 1)
    fc1_z(3)
    square_z(V)
    square_z(O)
    vector(1, 2)
    square_y(K)
    fc2_swap()
    square_core_rest(Q)
    norms_send()
    vector(0, 2)
    vector(1, 3)
    fc1_end(3)
    square_y(Q)
    vector(0, 3)
    fc1_end(2)
    square_z(K)
    norms_end()
    vector(1, 4)
    square_z(Q)
    vector(1, 5)
    square_end(V)
    fc1_end(1)
    square_end(K)
    fc2_end()
    square_end(O)
    fc1_end(0)
    vector(0, 4)
    vector(0, 5)
    square_end(Q)
    for copy in sent:
        copy.wait_send()


def fused(share, args):
    (queries, latents, positions, vis_ok, msk_ok, dy, w_query, w_key, w_value, w_out, w_fc1, w_fc2) = args[:12]
    vectors = args[12:]
    _, rows, width = queries.shape
    ff = w_fc1.shape[1]
    half = width // 2
    blk, fblk, hid = width // GROUPS, ff // GROUPS, ff // 2
    nb = hid // half
    pairs = half // (2 * HEAD_DIM)
    vm = pltpu.VMEM
    scratch = dict(
        send=pltpu.SemaphoreType.DMA((96,)),
        recv=pltpu.SemaphoreType.DMA((96,)),
        load=pltpu.SemaphoreType.DMA((32,)),
        ready=pltpu.SemaphoreType.REGULAR,
        rows=vm((12, width), F32),
        b_fc1=vm((ff,), F32),
        ok=vm((2, 1, 2 * rows), jnp.int32),
        pos=vm((1, rows), jnp.int32),
        dy=vm((4, 2 * rows, width), BF16),
        qraw=vm((2 * rows, width), BF16),
        lraw=vm((2 * rows, width), BF16),
        ppos=vm((1, rows), jnp.int32),
        w2=vm((hid, width), BF16),
        w1=vm((width, hid), BF16),
        wo=vm((width, width), BF16),
        wk=vm((width, half), BF16),
        wv=vm((width, half), BF16),
        wq=vm((width, half), BF16),
        qin=vm((2 * rows, width), F32),
        hat=vm((4 * rows, width), F32),
        hq=vm((2 * rows, width), BF16),
        hk=vm((4 * rows, width), BF16),
        hq_t=vm((width, 2 * rows), BF16),
        hk_t=vm((width, 4 * rows), BF16),
        att_t=vm((width, 2 * rows), BF16),
        h2_t=vm((width, 2 * rows), BF16),
        act_t=vm((hid, 2 * rows), BF16),
        q=vm((2 * rows, half), BF16),
        k=vm((4 * rows, half), BF16),
        v=vm((4 * rows, half), BF16),
        prob=vm((pairs, 4 * rows, 4 * rows), F32),
        att=vm((2, 2 * rows, half), BF16),
        branch=vm((2 * rows, width), F32),
        resid=vm((2 * rows, width), F32),
        d_resid=vm((2 * rows, width), F32),
        mlp=vm((2 * rows, width), F32),
        mlp_s=vm((rows, width), BF16),
        mlp_r=vm((rows, width), BF16),
        d_act=vm((nb, 2 * rows, half), F32),
        dm=vm((4, 2 * rows, width), BF16),
        h2_g=vm((2, 2, 4 * blk, 2 * rows), BF16),
        h2_r=vm((2, 4 * blk, 2 * rows), BF16),
        act=vm((nb, 2 * rows, half), BF16),
        act_s=vm((4, 2, fblk, 2 * rows), BF16),
        act_r=vm((3, 2, fblk, 2 * rows), BF16),
        dp=vm((2, nb, 2 * rows, half), BF16),
        dh2=vm((2, 2 * rows, width), BF16),
        dbr=vm((2 * rows, width), BF16),
        da=vm((2 * rows, half), BF16),
        dq=vm((2 * rows, half), BF16),
        dk=vm((4 * rows, half), BF16),
        dv=vm((4 * rows, half), BF16),
        dx=vm((2, 2 * rows, width), F32),
        dx_s=vm((2, rows, width), BF16),
        dx_r=vm((2, rows, width), BF16),
        sq=vm((4, 8 * blk, half), F32),
        sq_cs=vm((4, 8 * blk, half), BF16),
        sq_cr=vm((4, 8 * blk, half), BF16),
        sq_ys=vm((4, 2, 2 * blk, half), BF16),
        sq_yr=vm((4, 2, 2 * blk, half), BF16),
        sq_zs=vm((4, 2 * blk, half), BF16),
        sq_zr=vm((4, 2 * blk, half), BF16),
        sq_ws=vm((4, blk, half), BF16),
        sq_wr=vm((4, blk, half), BF16),
        fc2=vm((fblk, width), F32),
        fc2_cs=vm((fblk, width), BF16),
        fc2_cr=vm((fblk, width), BF16),
        fc2_xs=vm((fblk, half), BF16),
        fc2_xr=vm((fblk, half), BF16),
        fc2_all=vm((2, fblk, half), F32),
        fc2_ws=vm((fblk, half), BF16),
        fc2_wr=vm((fblk, half), BF16),
        fc1=vm((nb, 4 * blk, half), F32),
        fc1_cs=vm((nb, 4 * blk, half), BF16),
        fc1_cr=vm((nb, 4 * blk, half), BF16),
        fc1_zs=vm((nb, 2 * blk, half), BF16),
        fc1_zr=vm((nb, 2 * blk, half), BF16),
        fc1_ws=vm((nb, blk, half), BF16),
        fc1_wr=vm((nb, blk, half), BF16),
        vec=vm((6, 8, width), F32),
        vec_r=vm((5, 8, width), F32),
        vec2=vm((6, 8, width), F32),
        vec2_r=vm((5, 8, width), F32),
    )
    ANY = pl.BlockSpec(memory_space=pl.ANY)
    VMEM = pl.BlockSpec(memory_space=pltpu.VMEM)
    sds = jax.ShapeDtypeStruct
    return pl.pallas_call(
        functools.partial(kernel, (rows, width, ff, share)),
        out_shape=(
            vm((1, rows, width), BF16),
            vm((1, rows, width), F32),
            vm((1, rows, width), F32),
            vm((blk, half), F32),
            vm((blk, half), F32),
            vm((blk, half), F32),
            vm((blk, half), F32),
            vm((blk, ff // 2), F32),
            vm((fblk, half), F32),
            vm((16, width), F32),
        ),
        in_specs=[ANY] * 25,
        out_specs=[VMEM] * 10,
        scratch_shapes=[scratch],
        compiler_params=pltpu.CompilerParams(
            collective_id=0, has_side_effects=True, vmem_limit_bytes=60 << 20
        ),
        cost_estimate=pl.CostEstimate(
            flops=6 * 10**9, bytes_accessed=16 * 10**6, transcendentals=10**6
        ),
    )(queries, latents, positions, vis_ok, msk_ok, dy, w_query, w_key, w_value, w_out, w_fc1, w_fc2, *vectors)


def finish_kernel(count, *refs):
    arrays, table = refs[:count], refs[count]
    outs, rows = refs[count + 1:2 * count + 1], refs[2 * count + 1:-1]
    sems = refs[-1]
    copies = [
        pltpu.make_async_copy(src, dst, sems.at[i]) for i, (src, dst) in enumerate(zip(arrays, outs))
    ]
    for copy in copies:
        copy.start()
    width = table.shape[1]
    parts = rows[0].shape[0] // width
    for k in range(parts):
        rows[0][k * width:(k + 1) * width] = table[k, :]
    for k, row in enumerate(rows[1:]):
        row[...] = table[parts + k, :]
    for copy in copies:
        copy.wait()


def finish(arrays, table, ff, share):
    if share == 1:
        arrays = tuple(pltpu.with_memory_space_constraint(a, pltpu.VMEM) for a in arrays)
        table = pltpu.with_memory_space_constraint(table, pltpu.VMEM)
    count, width = len(arrays), table.shape[1]
    sds = jax.ShapeDtypeStruct
    vectors = table.shape[0] - ff // width
    ANY = pl.BlockSpec(memory_space=pl.ANY)
    VMEM = pl.BlockSpec(memory_space=pltpu.VMEM)
    return pl.pallas_call(
        functools.partial(finish_kernel, count),
        out_shape=tuple(sds(a.shape, a.dtype) for a in arrays)
        + (sds((ff,), F32),)
        + (sds((width,), F32),) * vectors,
        in_specs=[VMEM] * (count + 1),
        out_specs=[ANY] * count + [VMEM] * (1 + vectors),
        scratch_shapes=[pltpu.SemaphoreType.DMA((count,))],
    )(*arrays, table)


def per_device(
    queries, latents, positions, visible_valid, masked_valid,
    w_query, b_query, w_key, w_value, b_value, w_out, b_out, w_fc1, b_fc1, w_fc2, b_fc2,
    gain_query, shift_query, gain_keys, shift_keys, gain_mlp, shift_mlp, scale_attn, scale_mlp,
    out_grad,
):
    parts = lax.axis_size("dp")
    share = parts // GROUPS
    out = fused(
        share,
        (
            queries, latents, positions, visible_valid, masked_valid, out_grad,
            w_query, w_key, w_value, w_out, w_fc1, w_fc2,
            b_query, b_value, b_out, b_fc1, b_fc2,
            gain_query, shift_query, gain_keys, shift_keys, gain_mlp, shift_mlp, scale_attn, scale_mlp,
        ),
    )
    block_out, d_queries, d_latents, wq, wk, wv, wo, w1, w2, vec = out
    if share > 1:
        groups = [[n * share + i for i in range(share)] for n in range(GROUPS)]
        wq, wk, wv, wo, w1, w2 = (
            lax.psum_scatter(
                w, "dp", scatter_dimension=0, axis_index_groups=groups, tiled=True
            )
            for w in (wq, wk, wv, wo, w1, w2)
        )
        vec = lax.psum(vec, "dp", axis_index_groups=groups)
    arrays = (block_out, d_queries, d_latents, wq, wk, wv, wo, w1, w2)
    done = finish(arrays, vec, w_fc1.shape[1], share)
    block_out, d_queries, d_latents, wq, wk, wv, wo, w1, w2, b1 = done[:10]
    b2, sm, gm, hm, bo, sa, bq, bv, gq, hq, gk, hk = done[10:]
    return (
        block_out, d_queries, d_latents,
        wq, bq, wk, wv, bv, wo, bo, w1, b1, w2, b2,
        gq, hq, gk, hk, gm, hm, sa, sm,
    )


def solution(mesh):
    rows3 = P("dp", "qry", None)
    split = P("dp", "qry")
    full = P()
    return jax.shard_map(
        per_device,
        mesh=mesh,
        in_specs=(rows3, rows3, split, P("dp", None), P("dp", None)) + (full,) * 19 + (rows3,),
        out_specs=(
            rows3, rows3, rows3,
            split, full, split, split, full, split, full, split, full, split,
        ) + (full,) * 9,
        check_vma=False,
    )
```

```python
import functools
import math
import types

import jax
import jax.numpy as jnp
from jax import lax
from jax.experimental import pallas as pl
from jax.experimental.pallas import tpu as pltpu
from jax.sharding import PartitionSpec as P

HEAD_DIM = 64
MESH = pl.DeviceIdType.MESH
F32 = jnp.float32
BF16 = jnp.bfloat16
GROUPS = 16
Z_ORDER = (0, 2, 1, 3)
Z2_FIRST = (0, 1)
Z_FIRST = (3, 0)


def dot(a, b):
    return lax.dot_general(a, b, (((1,), (0,)), ((), ())), preferred_element_type=F32)


def dot_t(a, b):
    return lax.dot_general(a, b, (((1,), (1,)), ((), ())), preferred_element_type=F32)


def col_sum(a):
    return jnp.sum(a, axis=0, keepdims=True)


def normalise(v):
    centre = v - jnp.mean(v, axis=-1, keepdims=True)
    spread = jnp.mean(centre * centre, axis=-1, keepdims=True)
    inv = lax.rsqrt(spread + 1e-06)
    return centre * inv, inv


def normalise_back(grad_hat, hat, inv):
    m1 = jnp.mean(grad_hat, axis=-1, keepdims=True)
    m2 = jnp.mean(grad_hat * hat, axis=-1, keepdims=True)
    return inv * (grad_hat - m1 - hat * m2)


def sinusoid(places, width):
    index = lax.broadcasted_iota(jnp.int32, (1, width), 1)
    half = index // 2
    freq = jnp.exp(-(2.0 * half.astype(F32) / width) * math.log(10000.0))
    odd = (index - 2 * half).astype(F32)
    angle = places * freq
    turns = jnp.floor(angle * (2.0 / math.pi) + 0.5)
    rest = angle - turns * 1.5703125
    rest = rest - turns * 4.8351287841796875e-4
    rest = rest - turns * 3.1385570764541626e-07
    sq = rest * rest
    sine = rest * (
        1.0 + sq * (-1.0 / 6 + sq * (1.0 / 120 + sq * (-1.0 / 5040 + sq * (1.0 / 362880))))
    )
    cosine = 1.0 + sq * (-0.5 + sq * (1.0 / 24 + sq * (-1.0 / 720 + sq * (1.0 / 40320))))
    quarter = turns + odd
    pairs = jnp.floor(quarter * 0.5)
    parity = quarter - 2.0 * pairs
    flips = pairs - 2.0 * jnp.floor(pairs * 0.5)
    value = jnp.where(parity > 0.5, cosine, sine)
    return jnp.where(flips > 0.5, -value, value)


def kernel(
    shape,
    queries, latents, positions, vis_ok, msk_ok, dy_in,
    w_query, w_key, w_value, w_out, w_fc1, w_fc2,
    b_query, b_value, b_out, b_fc1, b_fc2,
    gain_q, shift_q, gain_k, shift_k, gain_m, shift_m, scale_a, scale_m,
    out_block, out_dq, out_dl, out_wq, out_wk, out_wv, out_wo, out_w1, out_w2, out_vec,
    s,
):
    s = types.SimpleNamespace(**s)
    rows, width, ff, share = shape
    half = width // 2
    pairs = half // (2 * HEAD_DIM)
    blk = width // GROUPS
    fblk = ff // GROUPS
    hid = ff // 2
    nb = hid // half
    scale = 1.0 / math.sqrt(HEAD_DIM)

    x = lax.axis_index("qry")
    place = lax.axis_index("dp")
    n = place // share
    low = place - n * share
    z = n // 4
    y = (n // 2) % 2
    c = n % 2
    zs = (z, z + 1 - 2 * (z % 2), (z + 2) % 4, 3 - z)

    def dev(zz, yy, cc, xx):
        return (((zz * 2 + yy) * 2 + cc) * share + low, xx)

    PX = dev(z, y, c, 1 - x)
    PY = dev(z, 1 - y, c, x)
    PC = dev(z, y, 1 - c, x)
    PZ1 = dev(zs[1], y, c, x)
    PZ2 = dev(zs[2], y, c, x)
    z_low = z % 2
    z_high = z // 2

    counter = [0]
    sent = []

    def push(src, dst, peer, landing=None):
        i = counter[0]
        counter[0] += 1

        def describe(to):
            return pltpu.make_async_remote_copy(
                src_ref=src, dst_ref=to, send_sem=s.send.at[i], recv_sem=s.recv.at[i],
                device_id=peer, device_id_type=MESH,
            )

        copy = describe(dst)
        copy.start()
        sent.append(copy)
        arrival = copy if landing is None else describe(landing)
        return arrival.wait_recv

    barrier = pltpu.get_barrier_semaphore()

    def tell(sem, peer):
        pl.semaphore_signal(sem, inc=1, device_id=peer, device_id_type=MESH)

    def tell_z(sem):
        @pl.when(z > 0)
        def _():
            tell(sem, dev(z - 1, y, c, x))

        @pl.when(z < 3)
        def _():
            tell(sem, dev(z + 1, y, c, x))

    z_links = 2 - (z + 3) // 3 + (z + 1) // 2 - z // 3
    for peer in (PX, PY, PC):
        tell(barrier, peer)
    tell_z(barrier)

    loads = []

    def load(src, dst):
        copy = pltpu.make_async_copy(src, dst, s.load.at[len(loads)])
        copy.start()
        loads.append(copy)
        return copy.wait

    own = pl.ds(pl.multiple_of(x * rows, rows), rows)
    other = pl.ds(pl.multiple_of((1 - x) * rows, rows), rows)
    low_own = pl.ds(pl.multiple_of((2 + x) * rows, rows), rows)
    low_other = pl.ds(pl.multiple_of((3 - x) * rows, rows), rows)
    mine = pl.ds(pl.multiple_of(x * half, half), half)
    theirs = pl.ds(pl.multiple_of((1 - x) * half, half), half)

    def row_of(ref, i):
        wait = load(ref, s.rows.at[i])

        def value():
            wait()
            return s.rows[i].reshape(1, width)

        return value

    load_q = load(queries.at[0], s.qraw.at[own])
    load_p = load(positions, s.pos)
    load_l = load(latents.at[0], s.lraw.at[own])
    gain_q, shift_q, gain_k, shift_k = (
        row_of(ref, i) for i, ref in enumerate((gain_q, shift_q, gain_k, shift_k))
    )
    load_wk = load(w_key, s.wk)
    load_wv = load(w_value, s.wv)
    load_wq = load(w_query, s.wq)
    b_query, b_value, b_out, b_fc2, gain_m, shift_m, scale_a, scale_m = (
        row_of(ref, 4 + i)
        for i, ref in enumerate((b_query, b_value, b_out, b_fc2, gain_m, shift_m, scale_a, scale_m))
    )
    load_b1 = load(b_fc1, s.b_fc1)
    load_ok = [load(vis_ok, s.ok.at[0]), load(msk_ok, s.ok.at[1])]
    load_dy = load(dy_in.at[0], s.dy.at[0, own])
    load_w2 = load(w_fc2, s.w2)
    load_wo = load(w_out, s.wo)
    load_w1 = load(w_fc1, s.w1)

    eye = lax.broadcasted_iota(jnp.int32, (rows, rows), 0) == lax.broadcasted_iota(
        jnp.int32, (rows, rows), 1
    )

    gain_q, shift_q, gain_k, shift_k = gain_q(), shift_q(), gain_k(), shift_k()

    def qry_half(pos_ref, at, low_at):
        row = jnp.broadcast_to(pos_ref[...].astype(F32), (rows, rows))
        places = jnp.sum(jnp.where(eye, row, 0.0), axis=1, keepdims=True)
        qin = s.qraw[at, :].astype(F32) + sinusoid(places, width)
        s.qin[at, :] = qin
        hat, inv = normalise(qin)
        s.hat[low_at, :] = hat
        hq = (hat * gain_q + shift_q).astype(BF16)
        hkq = (hat * gain_k + shift_k).astype(BF16)
        s.hq[at, :] = hq
        s.hk[low_at, :] = hkq
        return hat, inv, hq, hkq

    def lat_half(at):
        hat, inv = normalise(s.lraw[at, :].astype(F32))
        s.hat[at, :] = hat
        hkl = (hat * gain_k + shift_k).astype(BF16)
        s.hk[at, :] = hkl
        return hat, inv, hkl

    def project(hq, hkq, hkl, at, low_at):
        both = jnp.concatenate([hkl, hkq], axis=0)
        k = dot(both, s.wk[...]).astype(BF16)
        s.k[at, :] = k[:rows]
        s.k[low_at, :] = k[rows:]
        v = (dot(both, s.wv[...]) + b_value).astype(BF16)
        s.v[at, :] = v[:rows]
        s.v[low_at, :] = v[rows:]
        s.q[at, :] = (dot(hq, s.wq[...]) + b_query).astype(BF16)

    load_q()
    load_p()
    hat_q, inv_q, hq, hkq = qry_half(s.pos, own, low_own)
    load_l()
    hat_l, inv_l, hkl = lat_half(own)

    pl.semaphore_wait(barrier, 3 + z_links)
    got_p = push(positions, s.ppos, PX)
    got_q = push(queries.at[0], s.qraw.at[own], PX, s.qraw.at[other])
    got_l = push(latents.at[0], s.lraw.at[own], PX, s.lraw.at[other])
    got_dy = push(dy_in.at[0], s.dy.at[0, own], PX, s.dy.at[0, other])
    got_dy_z = push(dy_in.at[0], s.dy.at[1, own], PZ1)
    tell_z(s.ready)

    load_wk()
    load_wv()
    load_wq()
    b_query, b_value, b_out, b_fc2, gain_m, shift_m, scale_a, scale_m = (
        value() for value in (b_query, b_value, b_out, b_fc2, gain_m, shift_m, scale_a, scale_m)
    )
    load_b1()
    b_fc1 = s.b_fc1[...].reshape(1, ff)
    halves_b_fc1 = [
        jnp.where(x == k, b_fc1[:, :hid], b_fc1[:, hid:]) for k in range(2)
    ]
    project(hq, hkq, hkl, own, low_own)

    def act_back(at):
        d_mlp = (scale_m * s.dy[0, at, :].astype(F32)).astype(BF16)
        s.dm[0, at, :] = d_mlp
        for b in range(2 * nb):
            s.d_act[b, at, :] = dot_t(d_mlp, s.w2[b * half:(b + 1) * half, :])

    load_dy()
    load_w2()
    act_back(own)
    got_p()
    got_q()
    _, _, hq_o, hkq_o = qry_half(s.ppos, other, low_other)
    got_l()
    _, _, hkl_o = lat_half(other)
    project(hq_o, hkq_o, hkl_o, other, low_other)
    for wait in load_ok:
        wait()

    ok = jnp.concatenate([s.ok[0], s.ok[1]], axis=1) > 0
    lane = lax.broadcasted_iota(jnp.int32, (2 * rows, 2 * HEAD_DIM), 1)
    first = lane < HEAD_DIM

    def stack(pair):
        zero = jnp.zeros_like(pair)
        return jnp.concatenate([jnp.where(first, pair, zero), jnp.where(first, zero, pair)], axis=0)

    def unstack(both):
        return jnp.where(first, both[:2 * rows], both[2 * rows:])

    for pair in range(2 * pairs):
        at = slice(pair * 2 * HEAD_DIM, (pair + 1) * 2 * HEAD_DIM)
        raw = dot_t(stack(s.q[:, at]), s.k[:, at]) * scale
        scores = jnp.where(ok, raw, -1e30)
        peak = jnp.max(scores, axis=-1, keepdims=True)
        weight = jnp.exp(scores - peak)
        prob = weight * (1.0 / jnp.sum(weight, axis=-1, keepdims=True))
        s.prob[pair] = prob
        s.att[:, at] = unstack(dot(prob.astype(BF16), s.v[:, at])).astype(BF16)

    got_dy()
    got_dy_z2 = push(s.dy.at[0, other], s.dy.at[1, other], PZ1)
    load_wo()
    branch = dot(s.att[...], s.wo[...]) + b_out
    resid = s.qin[...] + scale_a * branch
    hat_m, inv_m = normalise(resid)
    h_two = (hat_m * gain_m + shift_m).astype(BF16)

    def blocks(ref, cc, yy):
        return jnp.concatenate(
            [
                ref[pl.ds(pl.multiple_of(((zs[t] * 2 + yy) * 2 + cc) * blk, blk), blk), :]
                for t in Z_ORDER
            ],
            axis=0,
        )

    s.h2_t[...] = h_two.T
    s.h2_g[1, 0] = blocks(s.h2_t, c, 1 - y)
    s.h2_g[1, 1] = blocks(s.h2_t, 1 - c, 1 - y)
    got_h2 = push(s.h2_g.at[1], s.h2_r, PY)
    act_back(other)
    load_w1()

    def hidden(first_block, b, bias):
        at = pl.ds(pl.multiple_of((first_block + b) * half, half), half)
        pre = dot(h_two, s.w1[:, at]) + bias[:, b * half:(b + 1) * half]
        cdf = 0.5 * (1.0 + lax.erf(pre * math.sqrt(0.5)))
        slope = cdf + pre * (jnp.exp(-0.5 * pre * pre) * (1.0 / math.sqrt(2 * math.pi)))
        s.act[first_block + b] = (pre * cdf).astype(BF16)
        s.dp[first_block + b] = (s.d_act[first_block + b] * slope).astype(BF16)

    got_dp = []
    for b in range(nb):
        hidden(x * nb, b, halves_b_fc1[0])
        got_dp.append(push(s.dp.at[x * nb + b], s.dp_r.at[b], PY))

    for b in range(nb):
        zz, at = divmod(b * half, hid // 2)
        s.act_t[zz, at:at + half, :] = s.act[x * nb + b].T
    got_act = push(s.act_t.at[1 - z_low], s.act_r, PZ1)
    s.h2_g[0, 0] = blocks(s.h2_t, c, y)
    s.h2_g[0, 1] = blocks(s.h2_t, 1 - c, y)
    s.hq_t[...] = s.hq[...].T
    s.hk_t[...] = s.hk[...].T
    s.att_t[...] = s.att[...].T

    got_c1, got_z1, got_w1 = [None] * nb, [None] * nb, [None] * nb

    def fc1_product(b):
        if b == 0:
            got_h2()
        got_dp[b]()
        right = jnp.concatenate([s.dp[x * nb + b], s.dp_r[b]], axis=0)
        left = jnp.concatenate([s.h2_g[0], s.h2_r[...]], axis=-1)
        s.fc1_cs[b] = dot(left[1], right).astype(BF16)
        got_c1[b] = push(s.fc1_cs.at[b], s.fc1_cr.at[b], PC)
        s.fc1[b] = dot(left[0], right)

    def fc1_rows(b):
        kept, leaving = ((0, 2), (1, 3)) if b in Z2_FIRST else ((0, 1), (2, 3))
        return [[slice(k * blk, (k + 1) * blk) for k in side] for side in (kept, leaving)]

    def fc1_core(b):
        got_c1[b]()
        s.fc1[b] = s.fc1[b] + s.fc1_cr[b].astype(F32)
        for k, at in enumerate(fc1_rows(b)[1]):
            s.fc1_zs[b, k * blk:(k + 1) * blk, :] = s.fc1[b, at, :].astype(BF16)
        got_z1[b] = push(s.fc1_zs.at[b], s.fc1_zr.at[b], PZ2 if b in Z2_FIRST else PZ1)

    def fc1_z(b):
        got_z1[b]()
        s.fc1_ws[b] = (
            s.fc1[b, fc1_rows(b)[0][1], :] + s.fc1_zr[b, blk:, :].astype(F32)
        ).astype(BF16)
        got_w1[b] = push(s.fc1_ws.at[b], s.fc1_wr.at[b], PZ1 if b in Z2_FIRST else PZ2)

    def fc1_end(b):
        got_w1[b]()
        out_w1[:, b * half:(b + 1) * half] = (
            s.fc1[b, :blk, :] + s.fc1_zr[b, :blk, :].astype(F32) + s.fc1_wr[b].astype(F32)
        )

    live = types.SimpleNamespace()
    hb = fblk // 2
    got_c2, got_x2, got_y2, got_w2 = ([None] * 2 for _ in range(4))

    def fc2_side(cc, k):
        left = jnp.concatenate(
            [
                jnp.concatenate([s.act_t[z_low, at, :], s.act_r[at, :]], axis=-1)
                for at in (
                    pl.ds(pl.multiple_of((yy * 2 + cc) * fblk + k * hb, hb), hb)
                    for yy in (y, 1 - y)
                )
            ],
            axis=0,
        )
        return dot(left, s.dm[...].reshape(4 * rows, width))

    def fc2_product(k):
        if got_c2 == [None, None]:
            for got in (got_dy_z, got_dy_z2, got_act):
                got()
            s.dm[1] = (scale_m * s.dy[1].astype(F32)).astype(BF16)
        s.fc2_cs[k] = fc2_side(1 - c, k).astype(BF16)
        got_c2[k] = push(s.fc2_cs.at[k], s.fc2_cr.at[k], PC)

    def fc2_rest(k):
        s.fc2[k] = fc2_side(c, k)

    def fc2_core(k):
        got_c2[k]()
        s.fc2[k] = s.fc2[k] + s.fc2_cr[k].astype(F32)
        s.fc2_xs[k] = s.fc2[k, :, theirs].astype(BF16)
        got_x2[k] = push(s.fc2_xs.at[k], s.fc2_xr.at[k], PX)
        s.fc2_all[k, x] = s.fc2[k, :, mine]

    def fc2_swap(k):
        got_x2[k]()
        s.fc2_all[k, 1 - x] = s.fc2_xr[k].astype(F32)
        s.fc2_ys[k] = s.fc2_all[k, :, hb:, :].astype(BF16)
        got_y2[k] = push(s.fc2_ys.at[k], s.fc2_yr.at[k], PY)

    def fc2_y(k):
        got_y2[k]()
        s.fc2_ws[k] = (
            s.fc2_all[k, 1 - z_high, :hb, :] + s.fc2_yr[k, 1 - z_high].astype(F32)
        ).astype(BF16)
        got_w2[k] = push(s.fc2_ws.at[k], s.fc2_wr.at[k], PZ2)

    def fc2_end(k):
        got_w2[k]()
        out_w2[k * hb:(k + 1) * hb, :] = (
            s.fc2_all[k, z_high, :hb, :]
            + s.fc2_yr[k, z_high].astype(F32)
            + s.fc2_wr[k].astype(F32)
        )

    yrows, zrows = 4 * blk, 2 * blk
    got_c, got_y, got_yr, got_zsq, got_wsq = ([None] * 4 for _ in range(5))

    def square(i, left_t, right):
        for leave in (1, 0):
            cc = 1 - c if leave else c
            left = jnp.concatenate([blocks(left_t, cc, y), blocks(left_t, cc, 1 - y)], axis=0)
            total = dot(left, right)
            if leave:
                s.sq_cs[i] = total.astype(BF16)
                got_c[i] = push(s.sq_cs.at[i], s.sq_cr.at[i], PC)
            else:
                s.sq[i] = total

    def square_core(i):
        got_c[i]()
        s.sq[i] = s.sq[i] + s.sq_cr[i].astype(F32)
        if i in Z_FIRST:
            for k in range(2):
                s.sq_zs[i, k] = s.sq[i, k * yrows + zrows:(k + 1) * yrows, :].astype(BF16)
            got_zsq[i] = push(s.sq_zs.at[i], s.sq_zr.at[i], PZ1)
        else:
            s.sq_ys[i, 1] = s.sq[i, yrows + zrows:, :].astype(BF16)
            got_y[i] = push(s.sq_ys.at[i, 1], s.sq_yr.at[i, 1], PY)

    def square_core_rest(i):
        s.sq_ys[i, 0] = s.sq[i, yrows:yrows + zrows, :].astype(BF16)
        got_yr[i] = push(s.sq_ys.at[i, 0], s.sq_yr.at[i, 0], PY)

    def square_y(i):
        if i in Z_FIRST:
            got_zsq[i]()
            s.sq_ys[i, 0] = (
                s.sq[i, yrows:yrows + zrows, :] + s.sq_zr[i, 1].astype(F32)
            ).astype(BF16)
            got_yr[i] = push(s.sq_ys.at[i, 0], s.sq_yr.at[i, 0], PY)
        else:
            got_y[i]()
            s.sq_zs[i, 0] = (s.sq[i, zrows:yrows, :] + s.sq_yr[i, 1].astype(F32)).astype(BF16)
            got_zsq[i] = push(s.sq_zs.at[i, 0], s.sq_zr.at[i, 0], PZ1)

    def square_z(i):
        got_yr[i]()
        if i not in Z_FIRST:
            got_zsq[i]()
        s.sq[i, :zrows, :] = (
            s.sq[i, :zrows, :] + s.sq_yr[i, 0].astype(F32) + s.sq_zr[i, 0].astype(F32)
        )
        s.sq_ws[i] = s.sq[i, blk:zrows, :].astype(BF16)
        got_wsq[i] = push(s.sq_ws.at[i], s.sq_wr.at[i], PZ2)

    def square_end(i):
        got_wsq[i]()
        (out_wo, out_wv, out_wk, out_wq)[i][...] = (
            s.sq[i, :blk, :] + s.sq_wr[i].astype(F32)
        )

    tables = (s.vec, s.vec2)
    landings = (s.vec_r, s.vec2_r)
    got_v = [None] * 2

    def vector_send(g, step, peer):
        got_v[g] = push(tables[g].at[step], landings[g].at[step], peer)

    def vector_add(g, step):
        got_v[g]()
        tables[g][step + 1] = tables[g][step] + landings[g][step]

    def hidden_others():
        for b in range(nb):
            hidden((1 - x) * nb, b, halves_b_fc1[1])
        s.branch[...] = branch
        s.resid[...] = resid

    def d_resid():
        d_h2 = jnp.zeros((width, 2 * rows), F32)
        for b in range(2 * nb):
            d_h2 += dot(s.w1[:, b * half:(b + 1) * half], s.dp[b].T)
        d_h2 = d_h2.T
        s.vec[0, 6:7, :] = col_sum(d_h2 * hat_m)
        s.vec[0, 7:8, :] = col_sum(d_h2)
        d_resid = s.dy[0].astype(F32) + normalise_back(d_h2 * gain_m, hat_m, inv_m)
        s.d_resid[...] = d_resid
        s.dbr[...] = (scale_a * d_resid).astype(BF16)

    def mlp_sums():
        mlp = jnp.zeros((2 * rows, width), F32) + b_fc2
        for b in range(2 * nb):
            mlp += dot(s.act[b], s.w2[b * half:(b + 1) * half, :])
            s.vec[0, b // 2:b // 2 + 1, (b % 2) * half:(b % 2 + 1) * half] = col_sum(
                s.dp[b].astype(F32)
            )
        s.mlp[...] = mlp
        s.vec[0, 4:5, :] = col_sum(s.dm[0].astype(F32))
        s.vec[0, 5:6, :] = col_sum(s.dy[0].astype(F32) * mlp)

    def block_end():
        out_block[0] = (s.resid[own, :] + scale_m * s.mlp[own, :]).astype(BF16)

    def heads_back(xx, cols):
        s.da[:, cols] = dot(s.wo[cols, :], s.dbr[...].T).T.astype(BF16)
        for p in range(pairs):
            pair = xx * pairs + p
            at = pl.ds(pl.multiple_of(pair * 2 * HEAD_DIM, 2 * HEAD_DIM), 2 * HEAD_DIM)
            q2 = stack(s.q[:, at])
            da2 = stack(s.da[:, at])
            prob = s.prob[pair]
            s.dv[:, at] = dot(prob.astype(BF16).T, da2).astype(BF16)
            d_prob = dot_t(da2, s.v[:, at])
            delta = jnp.sum(d_prob * prob, axis=-1, keepdims=True)
            ds = (prob * (d_prob - delta)).astype(BF16)
            s.dq[:, at] = (unstack(dot(ds, s.k[:, at])) * scale).astype(BF16)
            s.dk[:, at] = (dot(ds.T, q2) * scale).astype(BF16)

    def attention_back():
        heads_back(x, mine)

    def attention_back_others():
        heads_back(1 - x, theirs)

    def square_product(i):
        square(
            i,
            (s.att_t, s.hk_t, s.hk_t, s.hq_t)[i],
            (s.dbr, s.dv, s.dk, s.dq)[i][:, mine],
        )

    def norms_back():
        dhk = dot_t(s.dk[...], s.wk[...]) + dot_t(s.dv[...], s.wv[...])
        dhq = dot_t(s.dq[...], s.wq[...])
        s.dx[0] = dhk[:2 * rows] * gain_k
        s.dx[1] = dhk[2 * rows:] * gain_k + dhq * gain_q
        s.vec2[0, 0:1, :] = col_sum(s.dbr[...].astype(F32))
        s.vec2[0, 1:2, :] = col_sum(s.d_resid[...] * s.branch[...])
        s.vec2[0, 2:3, :] = col_sum(s.dq[...].astype(F32))
        s.vec2[0, 3:4, :] = col_sum(s.dv[...].astype(F32))
        s.vec2[0, 4:5, :] = col_sum(dhq * s.hat[2 * rows:, :])
        s.vec2[0, 5:6, :] = col_sum(dhq)
        s.vec2[0, 6:7, :] = col_sum(dhk * s.hat[...])
        s.vec2[0, 7:8, :] = col_sum(dhk)

    def norms_end():
        out_dl[0] = normalise_back(s.dx[0, own, :], hat_l, inv_l)
        out_dq[0] = s.d_resid[own, :] + normalise_back(s.dx[1, own, :], hat_q, inv_q)

    routes = (PZ2, PZ1, PY, PC)

    def vector(g, step):
        if step:
            vector_add(g, step - 1)
        if step < 4:
            vector_send(g, step, routes[step])
        else:
            out_vec[g * 8:g * 8 + 8, :] = tables[g][4]

    pl.semaphore_wait(s.ready, z_links)
    V, K, Q, O = 1, 2, 3, 0
    hidden_others()
    d_resid()
    square_product(O)
    attention_back()
    fc1_product(0)
    square_core(O)
    square_product(V)
    attention_back_others()
    fc1_core(0)
    fc1_product(1)
    square_product(K)
    fc2_product(1)
    square_core(V)
    fc1_core(1)
    norms_back()
    fc1_product(2)
    square_core(K)
    fc2_product(0)
    fc2_rest(1)
    fc2_core(1)
    fc2_rest(0)
    square_y(O)
    fc1_core(2)
    norms_end()
    mlp_sums()
    vector(0, 0)
    square_core_rest(V)
    square_y(V)
    fc1_product(3)
    square_core_rest(K)
    fc2_core(0)
    square_y(K)
    vector(1, 0)
    fc1_z(2)
    fc2_swap(1)
    square_product(Q)
    square_z(O)
    square_z(V)
    vector(0, 1)
    fc2_swap(0)
    square_core(Q)
    square_z(K)
    fc1_core(3)
    fc2_y(1)
    vector(1, 1)
    fc2_y(0)
    square_y(Q)
    fc1_z(3)
    square_end(O)
    square_z(Q)
    fc1_z(1)
    vector(0, 2)
    vector(1, 2)
    fc1_end(2)
    fc1_z(0)
    fc2_end(0)
    block_end()
    square_end(K)
    square_end(V)
    vector(0, 3)
    fc1_end(3)
    vector(1, 3)
    fc2_end(1)
    fc1_end(1)
    vector(0, 4)
    vector(1, 4)
    square_end(Q)
    fc1_end(0)
    for copy in sent:
        copy.wait_send()


def fused(share, args):
    (queries, latents, positions, vis_ok, msk_ok, dy, w_query, w_key, w_value, w_out, w_fc1, w_fc2) = args[:12]
    vectors = args[12:]
    _, rows, width = queries.shape
    ff = w_fc1.shape[1]
    half = width // 2
    blk, fblk, hid = width // GROUPS, ff // GROUPS, ff // 2
    nb = hid // half
    pairs = half // (2 * HEAD_DIM)
    vm = pltpu.VMEM
    scratch = dict(
        send=pltpu.SemaphoreType.DMA((96,)),
        recv=pltpu.SemaphoreType.DMA((96,)),
        load=pltpu.SemaphoreType.DMA((32,)),
        ready=pltpu.SemaphoreType.REGULAR,
        rows=vm((12, width), F32),
        b_fc1=vm((ff,), F32),
        ok=vm((2, 1, 2 * rows), jnp.int32),
        pos=vm((1, rows), jnp.int32),
        dy=vm((2, 2 * rows, width), BF16),
        qraw=vm((2 * rows, width), BF16),
        lraw=vm((2 * rows, width), BF16),
        ppos=vm((1, rows), jnp.int32),
        w2=vm((ff, width), BF16),
        w1=vm((width, ff), BF16),
        wo=vm((width, width), BF16),
        wk=vm((width, width), BF16),
        wv=vm((width, width), BF16),
        wq=vm((width, width), BF16),
        qin=vm((2 * rows, width), F32),
        hat=vm((4 * rows, width), F32),
        hq=vm((2 * rows, width), BF16),
        hk=vm((4 * rows, width), BF16),
        hq_t=vm((width, 2 * rows), BF16),
        hk_t=vm((width, 4 * rows), BF16),
        att_t=vm((width, 2 * rows), BF16),
        h2_t=vm((width, 2 * rows), BF16),
        act_t=vm((2, hid // 2, 2 * rows), BF16),
        q=vm((2 * rows, width), BF16),
        k=vm((4 * rows, width), BF16),
        v=vm((4 * rows, width), BF16),
        prob=vm((2 * pairs, 4 * rows, 4 * rows), F32),
        att=vm((2 * rows, width), BF16),
        branch=vm((2 * rows, width), F32),
        resid=vm((2 * rows, width), F32),
        d_resid=vm((2 * rows, width), F32),
        mlp=vm((2 * rows, width), F32),
        d_act=vm((2 * nb, 2 * rows, half), F32),
        dm=vm((2, 2 * rows, width), BF16),
        h2_g=vm((2, 2, 4 * blk, 2 * rows), BF16),
        h2_r=vm((2, 4 * blk, 2 * rows), BF16),
        act=vm((2 * nb, 2 * rows, half), BF16),
        act_r=vm((hid // 2, 2 * rows), BF16),
        dp=vm((2 * nb, 2 * rows, half), BF16),
        dp_r=vm((nb, 2 * rows, half), BF16),
        dbr=vm((2 * rows, width), BF16),
        da=vm((2 * rows, width), BF16),
        dq=vm((2 * rows, width), BF16),
        dk=vm((4 * rows, width), BF16),
        dv=vm((4 * rows, width), BF16),
        dx=vm((2, 2 * rows, width), F32),
        sq=vm((4, 8 * blk, half), F32),
        sq_cs=vm((4, 8 * blk, half), BF16),
        sq_cr=vm((4, 8 * blk, half), BF16),
        sq_ys=vm((4, 2, 2 * blk, half), BF16),
        sq_yr=vm((4, 2, 2 * blk, half), BF16),
        sq_zs=vm((4, 2, 2 * blk, half), BF16),
        sq_zr=vm((4, 2, 2 * blk, half), BF16),
        sq_ws=vm((4, blk, half), BF16),
        sq_wr=vm((4, blk, half), BF16),
        fc2=vm((2, fblk, width), F32),
        fc2_cs=vm((2, fblk, width), BF16),
        fc2_cr=vm((2, fblk, width), BF16),
        fc2_xs=vm((2, fblk, half), BF16),
        fc2_xr=vm((2, fblk, half), BF16),
        fc2_all=vm((2, 2, fblk, half), F32),
        fc2_ys=vm((2, 2, fblk // 2, half), BF16),
        fc2_yr=vm((2, 2, fblk // 2, half), BF16),
        fc2_ws=vm((2, fblk // 2, half), BF16),
        fc2_wr=vm((2, fblk // 2, half), BF16),
        fc1=vm((nb, 4 * blk, half), F32),
        fc1_cs=vm((nb, 4 * blk, half), BF16),
        fc1_cr=vm((nb, 4 * blk, half), BF16),
        fc1_zs=vm((nb, 2 * blk, half), BF16),
        fc1_zr=vm((nb, 2 * blk, half), BF16),
        fc1_ws=vm((nb, blk, half), BF16),
        fc1_wr=vm((nb, blk, half), BF16),
        vec=vm((5, 8, width), F32),
        vec_r=vm((4, 8, width), F32),
        vec2=vm((5, 8, width), F32),
        vec2_r=vm((4, 8, width), F32),
    )
    ANY = pl.BlockSpec(memory_space=pl.ANY)
    VMEM = pl.BlockSpec(memory_space=pltpu.VMEM)
    sds = jax.ShapeDtypeStruct
    return pl.pallas_call(
        functools.partial(kernel, (rows, width, ff, share)),
        out_shape=(
            vm((1, rows, width), BF16),
            vm((1, rows, width), F32),
            vm((1, rows, width), F32),
            vm((blk, half), F32),
            vm((blk, half), F32),
            vm((blk, half), F32),
            vm((blk, half), F32),
            vm((blk, ff // 2), F32),
            vm((fblk, half), F32),
            vm((16, width), F32),
        ),
        in_specs=[ANY] * 25,
        out_specs=[VMEM] * 10,
        scratch_shapes=[scratch],
        compiler_params=pltpu.CompilerParams(
            collective_id=0, has_side_effects=True, vmem_limit_bytes=60 << 20
        ),
        cost_estimate=pl.CostEstimate(
            flops=6 * 10**9, bytes_accessed=16 * 10**6, transcendentals=10**6
        ),
    )(queries, latents, positions, vis_ok, msk_ok, dy, w_query, w_key, w_value, w_out, w_fc1, w_fc2, *vectors)


def finish_kernel(count, *refs):
    arrays, table = refs[:count], refs[count]
    outs, rows = refs[count + 1:2 * count + 1], refs[2 * count + 1:-1]
    sems = refs[-1]
    copies = [
        pltpu.make_async_copy(src, dst, sems.at[i]) for i, (src, dst) in enumerate(zip(arrays, outs))
    ]
    for copy in copies:
        copy.start()
    width = table.shape[1]
    parts = rows[0].shape[0] // width
    for k in range(parts):
        rows[0][k * width:(k + 1) * width] = table[k, :]
    for k, row in enumerate(rows[1:]):
        row[...] = table[parts + k, :]
    for copy in copies:
        copy.wait()


def finish(arrays, table, ff, share):
    if share == 1:
        arrays = tuple(pltpu.with_memory_space_constraint(a, pltpu.VMEM) for a in arrays)
        table = pltpu.with_memory_space_constraint(table, pltpu.VMEM)
    count, width = len(arrays), table.shape[1]
    sds = jax.ShapeDtypeStruct
    vectors = table.shape[0] - ff // width
    ANY = pl.BlockSpec(memory_space=pl.ANY)
    VMEM = pl.BlockSpec(memory_space=pltpu.VMEM)
    return pl.pallas_call(
        functools.partial(finish_kernel, count),
        out_shape=tuple(sds(a.shape, a.dtype) for a in arrays)
        + (sds((ff,), F32),)
        + (sds((width,), F32),) * vectors,
        in_specs=[VMEM] * (count + 1),
        out_specs=[ANY] * count + [VMEM] * (1 + vectors),
        scratch_shapes=[pltpu.SemaphoreType.DMA((count,))],
    )(*arrays, table)


def per_device(
    queries, latents, positions, visible_valid, masked_valid,
    w_query, b_query, w_key, w_value, b_value, w_out, b_out, w_fc1, b_fc1, w_fc2, b_fc2,
    gain_query, shift_query, gain_keys, shift_keys, gain_mlp, shift_mlp, scale_attn, scale_mlp,
    out_grad,
):
    parts = lax.axis_size("dp")
    share = parts // GROUPS
    out = fused(
        share,
        (
            queries, latents, positions, visible_valid, masked_valid, out_grad,
            w_query, w_key, w_value, w_out, w_fc1, w_fc2,
            b_query, b_value, b_out, b_fc1, b_fc2,
            gain_query, shift_query, gain_keys, shift_keys, gain_mlp, shift_mlp, scale_attn, scale_mlp,
        ),
    )
    block_out, d_queries, d_latents, wq, wk, wv, wo, w1, w2, vec = out
    if share > 1:
        groups = [[n * share + i for i in range(share)] for n in range(GROUPS)]
        wq, wk, wv, wo, w1, w2 = (
            lax.psum_scatter(
                w, "dp", scatter_dimension=0, axis_index_groups=groups, tiled=True
            )
            for w in (wq, wk, wv, wo, w1, w2)
        )
        vec = lax.psum(vec, "dp", axis_index_groups=groups)
    arrays = (block_out, d_queries, d_latents, wq, wk, wv, wo, w1, w2)
    done = finish(arrays, vec, w_fc1.shape[1], share)
    block_out, d_queries, d_latents, wq, wk, wv, wo, w1, w2, b1 = done[:10]
    b2, sm, gm, hm, bo, sa, bq, bv, gq, hq, gk, hk = done[10:]
    return (
        block_out, d_queries, d_latents,
        wq, bq, wk, wv, bv, wo, bo, w1, b1, w2, b2,
        gq, hq, gk, hk, gm, hm, sa, sm,
    )


def solution(mesh):
    rows3 = P("dp", "qry", None)
    split = P("dp", "qry")
    full = P()
    return jax.shard_map(
        per_device,
        mesh=mesh,
        in_specs=(rows3, rows3, split, P("dp", None), P("dp", None)) + (full,) * 19 + (rows3,),
        out_specs=(
            rows3, rows3, rows3,
            split, full, split, split, full, split, full, split, full, split,
        ) + (full,) * 9,
        check_vma=False,
    )
```

```python
import functools
import math
import types

import jax
import jax.numpy as jnp
from jax import lax
from jax.experimental import pallas as pl
from jax.experimental.pallas import tpu as pltpu
from jax.sharding import PartitionSpec as P

HEAD_DIM = 64
MESH = pl.DeviceIdType.MESH
F32 = jnp.float32
BF16 = jnp.bfloat16
GROUPS = 16
Z_ORDER = (0, 2, 1, 3)
Z2_FIRST = (0, 1)
Z_FIRST = (3, 0)


def dot(a, b):
    return lax.dot_general(a, b, (((1,), (0,)), ((), ())), preferred_element_type=F32)


def dot_t(a, b):
    return lax.dot_general(a, b, (((1,), (1,)), ((), ())), preferred_element_type=F32)


def col_sum(a):
    return jnp.sum(a, axis=0, keepdims=True)


def normalise(v):
    centre = v - jnp.mean(v, axis=-1, keepdims=True)
    spread = jnp.mean(centre * centre, axis=-1, keepdims=True)
    inv = lax.rsqrt(spread + 1e-06)
    return centre * inv, inv


def normalise_back(grad_hat, hat, inv):
    m1 = jnp.mean(grad_hat, axis=-1, keepdims=True)
    m2 = jnp.mean(grad_hat * hat, axis=-1, keepdims=True)
    return inv * (grad_hat - m1 - hat * m2)


def sinusoid(places, width):
    index = lax.broadcasted_iota(jnp.int32, (1, width), 1)
    half = index // 2
    freq = jnp.exp(-(2.0 * half.astype(F32) / width) * math.log(10000.0))
    odd = (index - 2 * half).astype(F32)
    angle = places * freq
    turns = jnp.floor(angle * (2.0 / math.pi) + 0.5)
    rest = angle - turns * 1.5703125
    rest = rest - turns * 4.8351287841796875e-4
    rest = rest - turns * 3.1385570764541626e-07
    sq = rest * rest
    sine = rest * (
        1.0 + sq * (-1.0 / 6 + sq * (1.0 / 120 + sq * (-1.0 / 5040 + sq * (1.0 / 362880))))
    )
    cosine = 1.0 + sq * (-0.5 + sq * (1.0 / 24 + sq * (-1.0 / 720 + sq * (1.0 / 40320))))
    quarter = turns + odd
    pairs = jnp.floor(quarter * 0.5)
    parity = quarter - 2.0 * pairs
    flips = pairs - 2.0 * jnp.floor(pairs * 0.5)
    value = jnp.where(parity > 0.5, cosine, sine)
    return jnp.where(flips > 0.5, -value, value)


def kernel(
    shape,
    queries, latents, positions, vis_ok, msk_ok, dy_in,
    w_query, w_key, w_value, w_out, w_fc1, w_fc2,
    b_query, b_value, b_out, b_fc1, b_fc2,
    gain_q, shift_q, gain_k, shift_k, gain_m, shift_m, scale_a, scale_m,
    out_block, out_dq, out_dl, out_wq, out_wk, out_wv, out_wo, out_w1, out_w2, out_vec,
    s,
):
    s = types.SimpleNamespace(**s)
    rows, width, ff, share = shape
    half = width // 2
    pairs = half // (2 * HEAD_DIM)
    blk = width // GROUPS
    fblk = ff // GROUPS
    hid = ff // 2
    nb = hid // half
    scale = 1.0 / math.sqrt(HEAD_DIM)

    x = lax.axis_index("qry")
    place = lax.axis_index("dp")
    n = place // share
    low = place - n * share
    z = n // 4
    y = (n // 2) % 2
    c = n % 2
    zs = (z, z + 1 - 2 * (z % 2), (z + 2) % 4, 3 - z)

    def dev(zz, yy, cc, xx):
        return (((zz * 2 + yy) * 2 + cc) * share + low, xx)

    PX = dev(z, y, c, 1 - x)
    PY = dev(z, 1 - y, c, x)
    PC = dev(z, y, 1 - c, x)
    PZ1 = dev(zs[1], y, c, x)
    PZ2 = dev(zs[2], y, c, x)
    z_low = z % 2
    z_high = z // 2

    counter = [0]
    sent = []

    def push(src, dst, peer, landing=None):
        i = counter[0]
        counter[0] += 1

        def describe(to):
            return pltpu.make_async_remote_copy(
                src_ref=src, dst_ref=to, send_sem=s.send.at[i], recv_sem=s.recv.at[i],
                device_id=peer, device_id_type=MESH,
            )

        copy = describe(dst)
        copy.start()
        sent.append(copy)
        arrival = copy if landing is None else describe(landing)
        return arrival.wait_recv

    barrier = pltpu.get_barrier_semaphore()

    def tell(sem, peer):
        pl.semaphore_signal(sem, inc=1, device_id=peer, device_id_type=MESH)

    def tell_z(sem):
        @pl.when(z > 0)
        def _():
            tell(sem, dev(z - 1, y, c, x))

        @pl.when(z < 3)
        def _():
            tell(sem, dev(z + 1, y, c, x))

    z_links = 2 - (z + 3) // 3 + (z + 1) // 2 - z // 3
    for peer in (PX, PY, PC):
        tell(barrier, peer)
    tell_z(barrier)

    loads = []

    def load(src, dst):
        copy = pltpu.make_async_copy(src, dst, s.load.at[len(loads)])
        copy.start()
        loads.append(copy)
        return copy.wait

    own = pl.ds(pl.multiple_of(x * rows, rows), rows)
    other = pl.ds(pl.multiple_of((1 - x) * rows, rows), rows)
    low_own = pl.ds(pl.multiple_of((2 + x) * rows, rows), rows)
    low_other = pl.ds(pl.multiple_of((3 - x) * rows, rows), rows)
    mine = pl.ds(pl.multiple_of(x * half, half), half)
    theirs = pl.ds(pl.multiple_of((1 - x) * half, half), half)

    def row_of(ref, i):
        wait = load(ref, s.rows.at[i])

        def value():
            wait()
            return s.rows[i].reshape(1, width)

        return value

    load_q = load(queries.at[0], s.qraw.at[own])
    load_p = load(positions, s.pos)
    load_l = load(latents.at[0], s.lraw.at[own])
    gain_q, shift_q, gain_k, shift_k = (
        row_of(ref, i) for i, ref in enumerate((gain_q, shift_q, gain_k, shift_k))
    )
    load_wk = load(w_key, s.wk)
    load_wv = load(w_value, s.wv)
    load_wq = load(w_query, s.wq)
    b_query, b_value, b_out, b_fc2, gain_m, shift_m, scale_a, scale_m = (
        row_of(ref, 4 + i)
        for i, ref in enumerate((b_query, b_value, b_out, b_fc2, gain_m, shift_m, scale_a, scale_m))
    )
    load_b1 = load(b_fc1, s.b_fc1)
    load_ok = [load(vis_ok, s.ok.at[0]), load(msk_ok, s.ok.at[1])]
    load_dy = load(dy_in.at[0], s.dy.at[0, own])
    load_w2 = load(w_fc2, s.w2)
    load_wo = load(w_out, s.wo)
    load_w1 = load(w_fc1, s.w1)

    eye = lax.broadcasted_iota(jnp.int32, (rows, rows), 0) == lax.broadcasted_iota(
        jnp.int32, (rows, rows), 1
    )

    gain_q, shift_q, gain_k, shift_k = gain_q(), shift_q(), gain_k(), shift_k()

    def qry_half(pos_ref, at, low_at):
        row = jnp.broadcast_to(pos_ref[...].astype(F32), (rows, rows))
        places = jnp.sum(jnp.where(eye, row, 0.0), axis=1, keepdims=True)
        qin = s.qraw[at, :].astype(F32) + sinusoid(places, width)
        s.qin[at, :] = qin
        hat, inv = normalise(qin)
        s.hat[low_at, :] = hat
        hq = (hat * gain_q + shift_q).astype(BF16)
        hkq = (hat * gain_k + shift_k).astype(BF16)
        s.hq[at, :] = hq
        s.hk[low_at, :] = hkq
        return hat, inv, hq, hkq

    def lat_half(at):
        hat, inv = normalise(s.lraw[at, :].astype(F32))
        s.hat[at, :] = hat
        hkl = (hat * gain_k + shift_k).astype(BF16)
        s.hk[at, :] = hkl
        return hat, inv, hkl

    def project(hk, at):
        s.k[at, :] = dot(hk, s.wk[...]).astype(BF16)
        s.v[at, :] = (dot(hk, s.wv[...]) + b_value).astype(BF16)

    def project_query(hq, at):
        s.q[at, :] = (dot(hq, s.wq[...]) + b_query).astype(BF16)

    load_q()
    load_p()
    hat_q, inv_q, hq, hkq = qry_half(s.pos, own, low_own)
    load_l()
    hat_l, inv_l, hkl = lat_half(own)

    pl.semaphore_wait(barrier, 3 + z_links)
    got_p = push(positions, s.ppos, PX)
    got_q = push(queries.at[0], s.qraw.at[own], PX, s.qraw.at[other])
    got_l = push(latents.at[0], s.lraw.at[own], PX, s.lraw.at[other])
    got_dy = push(dy_in.at[0], s.dy.at[0, own], PX, s.dy.at[0, other])
    got_dy_z = push(dy_in.at[0], s.dy.at[1, own], PZ1)
    tell_z(s.ready)

    load_wk()
    load_wv()
    load_wq()
    b_query, b_value, b_out, b_fc2, gain_m, shift_m, scale_a, scale_m = (
        value() for value in (b_query, b_value, b_out, b_fc2, gain_m, shift_m, scale_a, scale_m)
    )
    load_b1()
    b_fc1 = s.b_fc1[...].reshape(1, ff)
    halves_b_fc1 = [
        jnp.where(x == k, b_fc1[:, :hid], b_fc1[:, hid:]) for k in range(2)
    ]
    project(hkl, own)
    project(hkq, low_own)
    project_query(hq, own)

    def act_back(at):
        d_mlp = (scale_m * s.dy[0, at, :].astype(F32)).astype(BF16)
        s.dm[0, at, :] = d_mlp
        for b in range(2 * nb):
            s.d_act[b, at, :] = dot_t(d_mlp, s.w2[b * half:(b + 1) * half, :])

    load_dy()
    load_w2()
    act_back(own)
    got_p()
    got_q()
    _, _, hq_o, hkq_o = qry_half(s.ppos, other, low_other)
    project(hkq_o, low_other)
    project_query(hq_o, other)
    got_l()
    _, _, hkl_o = lat_half(other)
    project(hkl_o, other)
    for wait in load_ok:
        wait()

    ok = jnp.concatenate([s.ok[0], s.ok[1]], axis=1) > 0
    lane = lax.broadcasted_iota(jnp.int32, (2 * rows, 2 * HEAD_DIM), 1)
    first = lane < HEAD_DIM

    def stack(pair):
        zero = jnp.zeros_like(pair)
        return jnp.concatenate([jnp.where(first, pair, zero), jnp.where(first, zero, pair)], axis=0)

    def unstack(both):
        return jnp.where(first, both[:2 * rows], both[2 * rows:])

    for pair in range(2 * pairs):
        at = slice(pair * 2 * HEAD_DIM, (pair + 1) * 2 * HEAD_DIM)
        raw = dot_t(stack(s.q[:, at]), s.k[:, at]) * scale
        scores = jnp.where(ok, raw, -1e30)
        peak = jnp.max(scores, axis=-1, keepdims=True)
        weight = jnp.exp(scores - peak)
        prob = weight * (1.0 / jnp.sum(weight, axis=-1, keepdims=True))
        s.prob[pair] = prob
        s.att[:, at] = unstack(dot(prob.astype(BF16), s.v[:, at])).astype(BF16)

    got_dy()
    got_dy_z2 = push(s.dy.at[0, other], s.dy.at[1, other], PZ1)
    load_wo()
    branch = dot(s.att[...], s.wo[...]) + b_out
    resid = s.qin[...] + scale_a * branch
    hat_m, inv_m = normalise(resid)
    h_two = (hat_m * gain_m + shift_m).astype(BF16)

    def blocks(ref, cc, yy):
        return jnp.concatenate(
            [
                ref[pl.ds(pl.multiple_of(((zs[t] * 2 + yy) * 2 + cc) * blk, blk), blk), :]
                for t in Z_ORDER
            ],
            axis=0,
        )

    s.h2_t[...] = h_two.T
    s.h2_g[1, 0] = blocks(s.h2_t, c, 1 - y)
    s.h2_g[1, 1] = blocks(s.h2_t, 1 - c, 1 - y)
    got_h2 = push(s.h2_g.at[1], s.h2_r, PY)
    act_back(other)
    load_w1()

    def hidden(first_block, b, bias):
        at = pl.ds(pl.multiple_of((first_block + b) * half, half), half)
        pre = dot(h_two, s.w1[:, at]) + bias[:, b * half:(b + 1) * half]
        cdf = 0.5 * (1.0 + lax.erf(pre * math.sqrt(0.5)))
        slope = cdf + pre * (jnp.exp(-0.5 * pre * pre) * (1.0 / math.sqrt(2 * math.pi)))
        s.act[first_block + b] = (pre * cdf).astype(BF16)
        s.dp[first_block + b] = (s.d_act[first_block + b] * slope).astype(BF16)

    got_dp = []
    for b in range(nb):
        hidden(x * nb, b, halves_b_fc1[0])
        got_dp.append(push(s.dp.at[x * nb + b], s.dp_r.at[b], PY))

    def turn(zz):
        for k in range(nb // 2):
            s.act_t[zz, k * half:(k + 1) * half, :] = s.act[x * nb + zz * (nb // 2) + k].T

    turn(1 - z_low)
    got_act = push(s.act_t.at[1 - z_low], s.act_r, PZ1)
    turn(z_low)
    s.h2_g[0, 0] = blocks(s.h2_t, c, y)
    s.h2_g[0, 1] = blocks(s.h2_t, 1 - c, y)
    s.hq_t[...] = s.hq[...].T
    s.hk_t[...] = s.hk[...].T
    s.att_t[...] = s.att[...].T

    got_c1, got_z1, got_w1 = [None] * nb, [None] * nb, [None] * nb

    def fc1_product(b):
        if b == 0:
            got_h2()
        got_dp[b]()
        right = jnp.concatenate([s.dp[x * nb + b], s.dp_r[b]], axis=0)
        left = jnp.concatenate([s.h2_g[0], s.h2_r[...]], axis=-1)
        s.fc1_cs[b] = dot(left[1], right).astype(BF16)
        got_c1[b] = push(s.fc1_cs.at[b], s.fc1_cr.at[b], PC)
        s.fc1[b] = dot(left[0], right)

    def fc1_rows(b):
        kept, leaving = ((0, 2), (1, 3)) if b in Z2_FIRST else ((0, 1), (2, 3))
        return [[slice(k * blk, (k + 1) * blk) for k in side] for side in (kept, leaving)]

    def fc1_core(b):
        got_c1[b]()
        s.fc1[b] = s.fc1[b] + s.fc1_cr[b].astype(F32)
        for k, at in enumerate(fc1_rows(b)[1]):
            s.fc1_zs[b, k * blk:(k + 1) * blk, :] = s.fc1[b, at, :].astype(BF16)
        got_z1[b] = push(s.fc1_zs.at[b], s.fc1_zr.at[b], PZ2 if b in Z2_FIRST else PZ1)

    def fc1_z(b):
        got_z1[b]()
        s.fc1_ws[b] = (
            s.fc1[b, fc1_rows(b)[0][1], :] + s.fc1_zr[b, blk:, :].astype(F32)
        ).astype(BF16)
        got_w1[b] = push(s.fc1_ws.at[b], s.fc1_wr.at[b], PZ1 if b in Z2_FIRST else PZ2)

    def fc1_end(b):
        got_w1[b]()
        out_w1[:, b * half:(b + 1) * half] = (
            s.fc1[b, :blk, :] + s.fc1_zr[b, :blk, :].astype(F32) + s.fc1_wr[b].astype(F32)
        )

    live = types.SimpleNamespace()
    hb = fblk // 2
    got_c2, got_x2, got_y2, got_w2 = ([None] * 2 for _ in range(4))

    def fc2_side(cc, k):
        left = jnp.concatenate(
            [
                jnp.concatenate([s.act_t[z_low, at, :], s.act_r[at, :]], axis=-1)
                for at in (
                    pl.ds(pl.multiple_of((yy * 2 + cc) * fblk + k * hb, hb), hb)
                    for yy in (y, 1 - y)
                )
            ],
            axis=0,
        )
        return dot(left, s.dm[...].reshape(4 * rows, width))

    def fc2_product(k):
        if got_c2 == [None, None]:
            for got in (got_dy_z, got_dy_z2, got_act):
                got()
            s.dm[1] = (scale_m * s.dy[1].astype(F32)).astype(BF16)
        s.fc2_cs[k] = fc2_side(1 - c, k).astype(BF16)
        got_c2[k] = push(s.fc2_cs.at[k], s.fc2_cr.at[k], PC)

    def fc2_rest(k):
        s.fc2[k] = fc2_side(c, k)

    def fc2_core(k):
        got_c2[k]()
        s.fc2[k] = s.fc2[k] + s.fc2_cr[k].astype(F32)
        s.fc2_xs[k] = s.fc2[k, :, theirs].astype(BF16)
        got_x2[k] = push(s.fc2_xs.at[k], s.fc2_xr.at[k], PX)
        s.fc2_all[k, x] = s.fc2[k, :, mine]

    def fc2_swap(k):
        got_x2[k]()
        s.fc2_all[k, 1 - x] = s.fc2_xr[k].astype(F32)
        s.fc2_ys[k] = s.fc2_all[k, :, hb:, :].astype(BF16)
        got_y2[k] = push(s.fc2_ys.at[k], s.fc2_yr.at[k], PY)

    def fc2_y(k):
        got_y2[k]()
        s.fc2_ws[k] = (
            s.fc2_all[k, 1 - z_high, :hb, :] + s.fc2_yr[k, 1 - z_high].astype(F32)
        ).astype(BF16)
        got_w2[k] = push(s.fc2_ws.at[k], s.fc2_wr.at[k], PZ2)

    def fc2_end(k):
        got_w2[k]()
        out_w2[k * hb:(k + 1) * hb, :] = (
            s.fc2_all[k, z_high, :hb, :]
            + s.fc2_yr[k, z_high].astype(F32)
            + s.fc2_wr[k].astype(F32)
        )

    yrows, zrows = 4 * blk, 2 * blk
    got_c, got_y, got_yr, got_zsq, got_wsq = ([None] * 4 for _ in range(5))

    def square(i, left_t, right):
        for leave in (1, 0):
            cc = 1 - c if leave else c
            left = jnp.concatenate([blocks(left_t, cc, y), blocks(left_t, cc, 1 - y)], axis=0)
            total = dot(left, right)
            if leave:
                s.sq_cs[i] = total.astype(BF16)
                got_c[i] = push(s.sq_cs.at[i], s.sq_cr.at[i], PC)
            else:
                s.sq[i] = total

    def square_core(i):
        got_c[i]()
        s.sq[i] = s.sq[i] + s.sq_cr[i].astype(F32)
        if i in Z_FIRST:
            for k in range(2):
                s.sq_zs[i, k] = s.sq[i, k * yrows + zrows:(k + 1) * yrows, :].astype(BF16)
            got_zsq[i] = push(s.sq_zs.at[i], s.sq_zr.at[i], PZ1)
        else:
            s.sq_ys[i, 1] = s.sq[i, yrows + zrows:, :].astype(BF16)
            got_y[i] = push(s.sq_ys.at[i, 1], s.sq_yr.at[i, 1], PY)

    def square_core_rest(i):
        s.sq_ys[i, 0] = s.sq[i, yrows:yrows + zrows, :].astype(BF16)
        got_yr[i] = push(s.sq_ys.at[i, 0], s.sq_yr.at[i, 0], PY)

    def square_y(i):
        if i in Z_FIRST:
            got_zsq[i]()
            s.sq_ys[i, 0] = (
                s.sq[i, yrows:yrows + zrows, :] + s.sq_zr[i, 1].astype(F32)
            ).astype(BF16)
            got_yr[i] = push(s.sq_ys.at[i, 0], s.sq_yr.at[i, 0], PY)
        else:
            got_y[i]()
            s.sq_zs[i, 0] = (s.sq[i, zrows:yrows, :] + s.sq_yr[i, 1].astype(F32)).astype(BF16)
            got_zsq[i] = push(s.sq_zs.at[i, 0], s.sq_zr.at[i, 0], PZ1)

    def square_z(i):
        got_yr[i]()
        if i not in Z_FIRST:
            got_zsq[i]()
        s.sq[i, :zrows, :] = (
            s.sq[i, :zrows, :] + s.sq_yr[i, 0].astype(F32) + s.sq_zr[i, 0].astype(F32)
        )
        s.sq_ws[i] = s.sq[i, blk:zrows, :].astype(BF16)
        got_wsq[i] = push(s.sq_ws.at[i], s.sq_wr.at[i], PZ2)

    def square_end(i):
        got_wsq[i]()
        (out_wo, out_wv, out_wk, out_wq)[i][...] = (
            s.sq[i, :blk, :] + s.sq_wr[i].astype(F32)
        )

    def hidden_others():
        for b in range(nb):
            hidden((1 - x) * nb, b, halves_b_fc1[1])
        s.branch[...] = branch
        s.resid[...] = resid

    def d_resid():
        d_h2 = jnp.zeros((width, 2 * rows), F32)
        for b in range(2 * nb):
            d_h2 += dot(s.w1[:, b * half:(b + 1) * half], s.dp[b].T)
        d_h2 = d_h2.T
        s.vec[0, 6:7, :] = col_sum(d_h2 * hat_m)
        s.vec[0, 7:8, :] = col_sum(d_h2)
        d_resid = s.dy[0].astype(F32) + normalise_back(d_h2 * gain_m, hat_m, inv_m)
        s.d_resid[...] = d_resid
        s.dbr[...] = (scale_a * d_resid).astype(BF16)

    def mlp_sums():
        mlp = jnp.zeros((2 * rows, width), F32) + b_fc2
        for b in range(2 * nb):
            mlp += dot(s.act[b], s.w2[b * half:(b + 1) * half, :])
            s.vec[0, b // 2:b // 2 + 1, (b % 2) * half:(b % 2 + 1) * half] = col_sum(
                s.dp[b].astype(F32)
            )
        s.mlp[...] = mlp
        s.vec[0, 4:5, :] = col_sum(s.dm[0].astype(F32))
        s.vec[0, 5:6, :] = col_sum(s.dy[0].astype(F32) * mlp)

    def block_end():
        out_block[0] = (s.resid[own, :] + scale_m * s.mlp[own, :]).astype(BF16)

    def heads_back(xx, cols):
        s.da[:, cols] = dot(s.wo[cols, :], s.dbr[...].T).T.astype(BF16)
        for p in range(pairs):
            pair = xx * pairs + p
            at = pl.ds(pl.multiple_of(pair * 2 * HEAD_DIM, 2 * HEAD_DIM), 2 * HEAD_DIM)
            q2 = stack(s.q[:, at])
            da2 = stack(s.da[:, at])
            prob = s.prob[pair]
            s.dv[:, at] = dot(prob.astype(BF16).T, da2).astype(BF16)
            d_prob = dot_t(da2, s.v[:, at])
            delta = jnp.sum(d_prob * prob, axis=-1, keepdims=True)
            ds = (prob * (d_prob - delta)).astype(BF16)
            s.dq[:, at] = (unstack(dot(ds, s.k[:, at])) * scale).astype(BF16)
            s.dk[:, at] = (dot(ds.T, q2) * scale).astype(BF16)

    def attention_back():
        heads_back(x, mine)

    def attention_back_others():
        heads_back(1 - x, theirs)

    def square_product(i):
        square(
            i,
            (s.att_t, s.hk_t, s.hk_t, s.hq_t)[i],
            (s.dbr, s.dv, s.dk, s.dq)[i][:, mine],
        )

    def norms_back():
        dhk = dot_t(s.dk[...], s.wk[...]) + dot_t(s.dv[...], s.wv[...])
        dhq = dot_t(s.dq[...], s.wq[...])
        s.dx[0] = dhk[:2 * rows] * gain_k
        s.dx[1] = dhk[2 * rows:] * gain_k + dhq * gain_q
        s.vec2[0, 0:1, :] = col_sum(s.dbr[...].astype(F32))
        s.vec2[0, 1:2, :] = col_sum(s.d_resid[...] * s.branch[...])
        s.vec2[0, 2:3, :] = col_sum(s.dq[...].astype(F32))
        s.vec2[0, 3:4, :] = col_sum(s.dv[...].astype(F32))
        s.vec2[0, 4:5, :] = col_sum(dhq * s.hat[2 * rows:, :])
        s.vec2[0, 5:6, :] = col_sum(dhq)
        s.vec2[0, 6:7, :] = col_sum(dhk * s.hat[...])
        s.vec2[0, 7:8, :] = col_sum(dhk)

    def norms_end():
        out_dl[0] = normalise_back(s.dx[0, own, :], hat_l, inv_l)
        out_dq[0] = s.d_resid[own, :] + normalise_back(s.dx[1, own, :], hat_q, inv_q)

    routes = (PZ2, PZ1, PY, PC)
    got_v = [None] * 2

    def vector(g, step):
        if step == 0:
            s.part[g, 0] = (s.vec, s.vec2)[g][0, :, mine]
        else:
            got_v[g]()
            if step < 5:
                s.part[g, step] = s.part[g, step - 1] + s.part_r[g, step - 1]
        at = slice(g * 8, g * 8 + 8)
        if step < 4:
            got_v[g] = push(s.part.at[g, step], s.part_r.at[g, step], routes[step])
        elif step == 4:
            out_vec[at, mine] = s.part[g, 4]
            got_v[g] = push(s.part.at[g, 4], s.part_r.at[g, 4], PX)
        else:
            out_vec[at, theirs] = s.part_r[g, 4]

    pl.semaphore_wait(s.ready, z_links)
    V, K, Q, O = 1, 2, 3, 0
    hidden_others()
    d_resid()
    square_product(O)
    attention_back()
    square_product(V)
    square_core(O)
    fc1_product(0)
    attention_back_others()
    fc1_product(1)
    square_core(V)
    fc1_core(0)
    fc2_product(1)
    mlp_sums()
    fc1_product(2)
    fc2_rest(1)
    vector(0, 0)
    fc2_core(1)
    square_product(K)
    fc1_core(2)
    fc2_product(0)
    square_y(O)
    fc2_rest(0)
    fc1_core(1)
    fc1_product(3)
    square_core(K)
    norms_back()
    square_core_rest(V)
    vector(1, 0)
    fc1_core(3)
    fc2_core(0)
    square_y(V)
    vector(0, 1)
    square_z(O)
    fc1_z(2)
    square_product(Q)
    fc2_swap(1)
    fc1_z(3)
    block_end()
    vector(1, 1)
    square_core(Q)
    fc2_swap(0)
    square_z(V)
    square_core_rest(K)
    norms_end()
    square_y(K)
    fc2_y(1)
    fc2_y(0)
    vector(1, 2)
    square_y(Q)
    fc1_z(0)
    vector(0, 2)
    square_z(K)
    vector(1, 3)
    square_z(Q)
    vector(0, 3)
    vector(1, 4)
    square_end(O)
    fc1_z(1)
    fc1_end(2)
    fc2_end(1)
    vector(0, 4)
    fc1_end(3)
    fc1_end(1)
    square_end(V)
    square_end(K)
    vector(0, 5)
    fc2_end(0)
    vector(1, 5)
    fc1_end(0)
    square_end(Q)
    for copy in sent:
        copy.wait_send()


def fused(share, args):
    (queries, latents, positions, vis_ok, msk_ok, dy, w_query, w_key, w_value, w_out, w_fc1, w_fc2) = args[:12]
    vectors = args[12:]
    _, rows, width = queries.shape
    ff = w_fc1.shape[1]
    half = width // 2
    blk, fblk, hid = width // GROUPS, ff // GROUPS, ff // 2
    nb = hid // half
    pairs = half // (2 * HEAD_DIM)
    vm = pltpu.VMEM
    scratch = dict(
        send=pltpu.SemaphoreType.DMA((96,)),
        recv=pltpu.SemaphoreType.DMA((96,)),
        load=pltpu.SemaphoreType.DMA((32,)),
        ready=pltpu.SemaphoreType.REGULAR,
        rows=vm((12, width), F32),
        b_fc1=vm((ff,), F32),
        ok=vm((2, 1, 2 * rows), jnp.int32),
        pos=vm((1, rows), jnp.int32),
        dy=vm((2, 2 * rows, width), BF16),
        qraw=vm((2 * rows, width), BF16),
        lraw=vm((2 * rows, width), BF16),
        ppos=vm((1, rows), jnp.int32),
        w2=vm((ff, width), BF16),
        w1=vm((width, ff), BF16),
        wo=vm((width, width), BF16),
        wk=vm((width, width), BF16),
        wv=vm((width, width), BF16),
        wq=vm((width, width), BF16),
        qin=vm((2 * rows, width), F32),
        hat=vm((4 * rows, width), F32),
        hq=vm((2 * rows, width), BF16),
        hk=vm((4 * rows, width), BF16),
        hq_t=vm((width, 2 * rows), BF16),
        hk_t=vm((width, 4 * rows), BF16),
        att_t=vm((width, 2 * rows), BF16),
        h2_t=vm((width, 2 * rows), BF16),
        act_t=vm((2, hid // 2, 2 * rows), BF16),
        q=vm((2 * rows, width), BF16),
        k=vm((4 * rows, width), BF16),
        v=vm((4 * rows, width), BF16),
        prob=vm((2 * pairs, 4 * rows, 4 * rows), F32),
        att=vm((2 * rows, width), BF16),
        branch=vm((2 * rows, width), F32),
        resid=vm((2 * rows, width), F32),
        d_resid=vm((2 * rows, width), F32),
        mlp=vm((2 * rows, width), F32),
        d_act=vm((2 * nb, 2 * rows, half), F32),
        dm=vm((2, 2 * rows, width), BF16),
        h2_g=vm((2, 2, 4 * blk, 2 * rows), BF16),
        h2_r=vm((2, 4 * blk, 2 * rows), BF16),
        act=vm((2 * nb, 2 * rows, half), BF16),
        act_r=vm((hid // 2, 2 * rows), BF16),
        dp=vm((2 * nb, 2 * rows, half), BF16),
        dp_r=vm((nb, 2 * rows, half), BF16),
        dbr=vm((2 * rows, width), BF16),
        da=vm((2 * rows, width), BF16),
        dq=vm((2 * rows, width), BF16),
        dk=vm((4 * rows, width), BF16),
        dv=vm((4 * rows, width), BF16),
        dx=vm((2, 2 * rows, width), F32),
        sq=vm((4, 8 * blk, half), F32),
        sq_cs=vm((4, 8 * blk, half), BF16),
        sq_cr=vm((4, 8 * blk, half), BF16),
        sq_ys=vm((4, 2, 2 * blk, half), BF16),
        sq_yr=vm((4, 2, 2 * blk, half), BF16),
        sq_zs=vm((4, 2, 2 * blk, half), BF16),
        sq_zr=vm((4, 2, 2 * blk, half), BF16),
        sq_ws=vm((4, blk, half), BF16),
        sq_wr=vm((4, blk, half), BF16),
        fc2=vm((2, fblk, width), F32),
        fc2_cs=vm((2, fblk, width), BF16),
        fc2_cr=vm((2, fblk, width), BF16),
        fc2_xs=vm((2, fblk, half), BF16),
        fc2_xr=vm((2, fblk, half), BF16),
        fc2_all=vm((2, 2, fblk, half), F32),
        fc2_ys=vm((2, 2, fblk // 2, half), BF16),
        fc2_yr=vm((2, 2, fblk // 2, half), BF16),
        fc2_ws=vm((2, fblk // 2, half), BF16),
        fc2_wr=vm((2, fblk // 2, half), BF16),
        fc1=vm((nb, 4 * blk, half), F32),
        fc1_cs=vm((nb, 4 * blk, half), BF16),
        fc1_cr=vm((nb, 4 * blk, half), BF16),
        fc1_zs=vm((nb, 2 * blk, half), BF16),
        fc1_zr=vm((nb, 2 * blk, half), BF16),
        fc1_ws=vm((nb, blk, half), BF16),
        fc1_wr=vm((nb, blk, half), BF16),
        part=vm((2, 5, 8, half), F32),
        part_r=vm((2, 5, 8, half), F32),
        vec=vm((1, 8, width), F32),
        vec2=vm((1, 8, width), F32),
    )
    ANY = pl.BlockSpec(memory_space=pl.ANY)
    VMEM = pl.BlockSpec(memory_space=pltpu.VMEM)
    sds = jax.ShapeDtypeStruct
    return pl.pallas_call(
        functools.partial(kernel, (rows, width, ff, share)),
        out_shape=(
            vm((1, rows, width), BF16),
            vm((1, rows, width), F32),
            vm((1, rows, width), F32),
            vm((blk, half), F32),
            vm((blk, half), F32),
            vm((blk, half), F32),
            vm((blk, half), F32),
            vm((blk, ff // 2), F32),
            vm((fblk, half), F32),
            vm((16, width), F32),
        ),
        in_specs=[ANY] * 25,
        out_specs=[VMEM] * 10,
        scratch_shapes=[scratch],
        compiler_params=pltpu.CompilerParams(
            collective_id=0, has_side_effects=True, vmem_limit_bytes=60 << 20
        ),
        cost_estimate=pl.CostEstimate(
            flops=6 * 10**9, bytes_accessed=16 * 10**6, transcendentals=10**6
        ),
    )(queries, latents, positions, vis_ok, msk_ok, dy, w_query, w_key, w_value, w_out, w_fc1, w_fc2, *vectors)


def finish_kernel(count, *refs):
    arrays, table = refs[:count], refs[count]
    outs, rows = refs[count + 1:2 * count + 1], refs[2 * count + 1:-1]
    sems = refs[-1]
    copies = [
        pltpu.make_async_copy(src, dst, sems.at[i]) for i, (src, dst) in enumerate(zip(arrays, outs))
    ]
    for copy in copies:
        copy.start()
    width = table.shape[1]
    parts = rows[0].shape[0] // width
    for k in range(parts):
        rows[0][k * width:(k + 1) * width] = table[k, :]
    for k, row in enumerate(rows[1:]):
        row[...] = table[parts + k, :]
    for copy in copies:
        copy.wait()


def finish(arrays, table, ff, share):
    if share == 1:
        arrays = tuple(pltpu.with_memory_space_constraint(a, pltpu.VMEM) for a in arrays)
        table = pltpu.with_memory_space_constraint(table, pltpu.VMEM)
    count, width = len(arrays), table.shape[1]
    sds = jax.ShapeDtypeStruct
    vectors = table.shape[0] - ff // width
    ANY = pl.BlockSpec(memory_space=pl.ANY)
    VMEM = pl.BlockSpec(memory_space=pltpu.VMEM)
    return pl.pallas_call(
        functools.partial(finish_kernel, count),
        out_shape=tuple(sds(a.shape, a.dtype) for a in arrays)
        + (sds((ff,), F32),)
        + (sds((width,), F32),) * vectors,
        in_specs=[VMEM] * (count + 1),
        out_specs=[ANY] * count + [VMEM] * (1 + vectors),
        scratch_shapes=[pltpu.SemaphoreType.DMA((count,))],
    )(*arrays, table)


def per_device(
    queries, latents, positions, visible_valid, masked_valid,
    w_query, b_query, w_key, w_value, b_value, w_out, b_out, w_fc1, b_fc1, w_fc2, b_fc2,
    gain_query, shift_query, gain_keys, shift_keys, gain_mlp, shift_mlp, scale_attn, scale_mlp,
    out_grad,
):
    parts = lax.axis_size("dp")
    share = parts // GROUPS
    out = fused(
        share,
        (
            queries, latents, positions, visible_valid, masked_valid, out_grad,
            w_query, w_key, w_value, w_out, w_fc1, w_fc2,
            b_query, b_value, b_out, b_fc1, b_fc2,
            gain_query, shift_query, gain_keys, shift_keys, gain_mlp, shift_mlp, scale_attn, scale_mlp,
        ),
    )
    block_out, d_queries, d_latents, wq, wk, wv, wo, w1, w2, vec = out
    if share > 1:
        groups = [[n * share + i for i in range(share)] for n in range(GROUPS)]
        wq, wk, wv, wo, w1, w2 = (
            lax.psum_scatter(
                w, "dp", scatter_dimension=0, axis_index_groups=groups, tiled=True
            )
            for w in (wq, wk, wv, wo, w1, w2)
        )
        vec = lax.psum(vec, "dp", axis_index_groups=groups)
    arrays = (block_out, d_queries, d_latents, wq, wk, wv, wo, w1, w2)
    done = finish(arrays, vec, w_fc1.shape[1], share)
    block_out, d_queries, d_latents, wq, wk, wv, wo, w1, w2, b1 = done[:10]
    b2, sm, gm, hm, bo, sa, bq, bv, gq, hq, gk, hk = done[10:]
    return (
        block_out, d_queries, d_latents,
        wq, bq, wk, wv, bv, wo, bo, w1, b1, w2, b2,
        gq, hq, gk, hk, gm, hm, sa, sm,
    )


def solution(mesh):
    rows3 = P("dp", "qry", None)
    split = P("dp", "qry")
    full = P()
    return jax.shard_map(
        per_device,
        mesh=mesh,
        in_specs=(rows3, rows3, split, P("dp", None), P("dp", None)) + (full,) * 19 + (rows3,),
        out_specs=(
            rows3, rows3, rows3,
            split, full, split, split, full, split, full, split, full, split,
        ) + (full,) * 9,
        check_vma=False,
    )
```

```python
import functools
import math
import types

import jax
import jax.numpy as jnp
from jax import lax
from jax.experimental import pallas as pl
from jax.experimental.pallas import tpu as pltpu
from jax.sharding import PartitionSpec as P

HEAD_DIM = 64
MESH = pl.DeviceIdType.MESH
F32 = jnp.float32
BF16 = jnp.bfloat16
GROUPS = 16
Z_ORDER = (0, 2, 1, 3)
Z2_FIRST = (0, 1)
Z_FIRST = (3, 0)


def dot(a, b):
    return lax.dot_general(a, b, (((1,), (0,)), ((), ())), preferred_element_type=F32)


def dot_t(a, b):
    return lax.dot_general(a, b, (((1,), (1,)), ((), ())), preferred_element_type=F32)


def col_sum(a):
    return jnp.sum(a, axis=0, keepdims=True)


def normalise(v):
    centre = v - jnp.mean(v, axis=-1, keepdims=True)
    spread = jnp.mean(centre * centre, axis=-1, keepdims=True)
    inv = lax.rsqrt(spread + 1e-06)
    return centre * inv, inv


def normalise_back(grad_hat, hat, inv):
    m1 = jnp.mean(grad_hat, axis=-1, keepdims=True)
    m2 = jnp.mean(grad_hat * hat, axis=-1, keepdims=True)
    return inv * (grad_hat - m1 - hat * m2)


def sinusoid(places, width):
    index = lax.broadcasted_iota(jnp.int32, (1, width), 1)
    half = index // 2
    freq = jnp.exp(-(2.0 * half.astype(F32) / width) * math.log(10000.0))
    odd = (index - 2 * half).astype(F32)
    angle = places * freq
    turns = jnp.floor(angle * (2.0 / math.pi) + 0.5)
    rest = angle - turns * 1.5703125
    rest = rest - turns * 4.8351287841796875e-4
    rest = rest - turns * 3.1385570764541626e-07
    sq = rest * rest
    sine = rest * (
        1.0 + sq * (-1.0 / 6 + sq * (1.0 / 120 + sq * (-1.0 / 5040 + sq * (1.0 / 362880))))
    )
    cosine = 1.0 + sq * (-0.5 + sq * (1.0 / 24 + sq * (-1.0 / 720 + sq * (1.0 / 40320))))
    quarter = turns + odd
    pairs = jnp.floor(quarter * 0.5)
    parity = quarter - 2.0 * pairs
    flips = pairs - 2.0 * jnp.floor(pairs * 0.5)
    value = jnp.where(parity > 0.5, cosine, sine)
    return jnp.where(flips > 0.5, -value, value)


def kernel(
    shape,
    queries, latents, positions, vis_ok, msk_ok, dy_in,
    w_query, w_key, w_value, w_out, w_fc1, w_fc2,
    b_query, b_value, b_out, b_fc1, b_fc2,
    gain_q, shift_q, gain_k, shift_k, gain_m, shift_m, scale_a, scale_m,
    out_block, out_dq, out_dl, out_wq, out_wk, out_wv, out_wo, out_w1, out_w2, out_vec,
    s,
):
    s = types.SimpleNamespace(**s)
    rows, width, ff, share = shape
    half = width // 2
    pairs = half // (2 * HEAD_DIM)
    blk = width // GROUPS
    fblk = ff // GROUPS
    hid = ff // 2
    nb = hid // half
    scale = 1.0 / math.sqrt(HEAD_DIM)

    x = lax.axis_index("qry")
    place = lax.axis_index("dp")
    n = place // share
    low = place - n * share
    z = n // 4
    y = (n // 2) % 2
    c = n % 2
    zs = (z, z + 1 - 2 * (z % 2), (z + 2) % 4, 3 - z)

    def dev(zz, yy, cc, xx):
        return (((zz * 2 + yy) * 2 + cc) * share + low, xx)

    PX = dev(z, y, c, 1 - x)
    PY = dev(z, 1 - y, c, x)
    PC = dev(z, y, 1 - c, x)
    PZ1 = dev(zs[1], y, c, x)
    PZ2 = dev(zs[2], y, c, x)
    z_low = z % 2
    z_high = z // 2

    counter = [0]
    sent = []

    def push(src, dst, peer, landing=None):
        i = counter[0]
        counter[0] += 1

        def describe(to):
            return pltpu.make_async_remote_copy(
                src_ref=src, dst_ref=to, send_sem=s.send.at[i], recv_sem=s.recv.at[i],
                device_id=peer, device_id_type=MESH,
            )

        copy = describe(dst)
        copy.start()
        sent.append(copy)
        arrival = copy if landing is None else describe(landing)
        return arrival.wait_recv

    barrier = pltpu.get_barrier_semaphore()

    def tell(sem, peer):
        pl.semaphore_signal(sem, inc=1, device_id=peer, device_id_type=MESH)

    def tell_z(sem):
        @pl.when(z > 0)
        def _():
            tell(sem, dev(z - 1, y, c, x))

        @pl.when(z < 3)
        def _():
            tell(sem, dev(z + 1, y, c, x))

    z_links = 2 - (z + 3) // 3 + (z + 1) // 2 - z // 3
    for peer in (PX, PY, PC):
        tell(barrier, peer)
    tell_z(barrier)

    loads = []

    def load(src, dst):
        copy = pltpu.make_async_copy(src, dst, s.load.at[len(loads)])
        copy.start()
        loads.append(copy)
        return copy.wait

    own = pl.ds(pl.multiple_of(x * rows, rows), rows)
    other = pl.ds(pl.multiple_of((1 - x) * rows, rows), rows)
    low_own = pl.ds(pl.multiple_of((2 + x) * rows, rows), rows)
    low_other = pl.ds(pl.multiple_of((3 - x) * rows, rows), rows)
    mine = pl.ds(pl.multiple_of(x * half, half), half)
    theirs = pl.ds(pl.multiple_of((1 - x) * half, half), half)

    def row_of(ref, i):
        wait = load(ref, s.rows.at[i])

        def value():
            wait()
            return s.rows[i].reshape(1, width)

        return value

    load_q = load(queries.at[0], s.qraw.at[own])
    load_p = load(positions, s.pos)
    load_l = load(latents.at[0], s.lraw.at[own])
    gain_q, shift_q, gain_k, shift_k = (
        row_of(ref, i) for i, ref in enumerate((gain_q, shift_q, gain_k, shift_k))
    )
    load_wk = load(w_key, s.wk)
    load_wv = load(w_value, s.wv)
    load_wq = load(w_query, s.wq)
    b_query, b_value, b_out, b_fc2, gain_m, shift_m, scale_a, scale_m = (
        row_of(ref, 4 + i)
        for i, ref in enumerate((b_query, b_value, b_out, b_fc2, gain_m, shift_m, scale_a, scale_m))
    )
    load_b1 = load(b_fc1, s.b_fc1)
    load_ok = [load(vis_ok, s.ok.at[0]), load(msk_ok, s.ok.at[1])]
    load_dy = load(dy_in.at[0], s.dy.at[0, own])
    load_w2 = load(w_fc2, s.w2)
    load_wo = load(w_out, s.wo)
    load_w1 = load(w_fc1, s.w1)

    eye = lax.broadcasted_iota(jnp.int32, (rows, rows), 0) == lax.broadcasted_iota(
        jnp.int32, (rows, rows), 1
    )

    gain_q, shift_q, gain_k, shift_k = gain_q(), shift_q(), gain_k(), shift_k()

    def qry_half(pos_ref, at, low_at):
        row = jnp.broadcast_to(pos_ref[...].astype(F32), (rows, rows))
        places = jnp.sum(jnp.where(eye, row, 0.0), axis=1, keepdims=True)
        qin = s.qraw[at, :].astype(F32) + sinusoid(places, width)
        s.qin[at, :] = qin
        hat, inv = normalise(qin)
        s.hat[low_at, :] = hat
        hq = (hat * gain_q + shift_q).astype(BF16)
        hkq = (hat * gain_k + shift_k).astype(BF16)
        s.hq[at, :] = hq
        s.hk[low_at, :] = hkq
        return hat, inv, hq, hkq

    def lat_half(at):
        hat, inv = normalise(s.lraw[at, :].astype(F32))
        s.hat[at, :] = hat
        hkl = (hat * gain_k + shift_k).astype(BF16)
        s.hk[at, :] = hkl
        return hat, inv, hkl

    def project(hk, at):
        s.k[at, :] = dot(hk, s.wk[...]).astype(BF16)
        s.v[at, :] = (dot(hk, s.wv[...]) + b_value).astype(BF16)

    def project_query(hq, at):
        s.q[at, :] = (dot(hq, s.wq[...]) + b_query).astype(BF16)

    load_q()
    load_p()
    hat_q, inv_q, hq, hkq = qry_half(s.pos, own, low_own)
    load_l()
    hat_l, inv_l, hkl = lat_half(own)

    pl.semaphore_wait(barrier, 3 + z_links)
    got_p = push(positions, s.ppos, PX)
    got_q = push(queries.at[0], s.qraw.at[own], PX, s.qraw.at[other])
    got_l = push(latents.at[0], s.lraw.at[own], PX, s.lraw.at[other])
    got_dy = push(dy_in.at[0], s.dy.at[0, own], PX, s.dy.at[0, other])
    got_dy_z = push(dy_in.at[0], s.dy.at[1, own], PZ1)
    tell_z(s.ready)

    load_wk()
    load_wv()
    load_wq()
    b_query, b_value, b_out, b_fc2, gain_m, shift_m, scale_a, scale_m = (
        value() for value in (b_query, b_value, b_out, b_fc2, gain_m, shift_m, scale_a, scale_m)
    )
    load_b1()
    b_fc1 = s.b_fc1[...].reshape(1, ff)
    halves_b_fc1 = [
        jnp.where(x == k, b_fc1[:, :hid], b_fc1[:, hid:]) for k in range(2)
    ]
    project(hkl, own)
    project(hkq, low_own)
    project_query(hq, own)

    def act_back(at, first_block, blocks):
        for b in range(blocks):
            units = pl.ds(pl.multiple_of((first_block + b) * half, half), half)
            s.d_act[first_block + b, at, :] = dot_t(s.dm[0, at, :], s.w2[units, :])

    def d_mlp(at):
        s.dm[0, at, :] = (scale_m * s.dy[0, at, :].astype(F32)).astype(BF16)

    load_dy()
    load_w2()
    d_mlp(own)
    act_back(own, 0, 2 * nb)
    got_p()
    got_q()
    _, _, hq_o, hkq_o = qry_half(s.ppos, other, low_other)
    project(hkq_o, low_other)
    project_query(hq_o, other)
    got_l()
    _, _, hkl_o = lat_half(other)
    project(hkl_o, other)
    for wait in load_ok:
        wait()

    ok = jnp.concatenate([s.ok[0], s.ok[1]], axis=1) > 0
    lane = lax.broadcasted_iota(jnp.int32, (2 * rows, 2 * HEAD_DIM), 1)
    first = lane < HEAD_DIM

    def stack(pair):
        zero = jnp.zeros_like(pair)
        return jnp.concatenate([jnp.where(first, pair, zero), jnp.where(first, zero, pair)], axis=0)

    def unstack(both):
        return jnp.where(first, both[:2 * rows], both[2 * rows:])

    for pair in range(2 * pairs):
        at = slice(pair * 2 * HEAD_DIM, (pair + 1) * 2 * HEAD_DIM)
        raw = dot_t(stack(s.q[:, at]), s.k[:, at]) * scale
        scores = jnp.where(ok, raw, -1e30)
        peak = jnp.max(scores, axis=-1, keepdims=True)
        weight = jnp.exp(scores - peak)
        prob = weight * (1.0 / jnp.sum(weight, axis=-1, keepdims=True))
        s.prob[pair] = prob
        s.att[:, at] = unstack(dot(prob.astype(BF16), s.v[:, at])).astype(BF16)

    got_dy()
    got_dy_z2 = push(s.dy.at[0, other], s.dy.at[1, other], PZ1)
    load_wo()
    branch = dot(s.att[...], s.wo[...]) + b_out
    resid = s.qin[...] + scale_a * branch
    hat_m, inv_m = normalise(resid)
    h_two = (hat_m * gain_m + shift_m).astype(BF16)

    def blocks(ref, cc, yy):
        return jnp.concatenate(
            [
                ref[pl.ds(pl.multiple_of(((zs[t] * 2 + yy) * 2 + cc) * blk, blk), blk), :]
                for t in Z_ORDER
            ],
            axis=0,
        )

    s.h2_t[...] = h_two.T
    s.h2_g[1, 0] = blocks(s.h2_t, c, 1 - y)
    s.h2_g[1, 1] = blocks(s.h2_t, 1 - c, 1 - y)
    got_h2 = push(s.h2_g.at[1], s.h2_r, PY)
    d_mlp(other)
    act_back(other, x * nb, nb)
    load_w1()

    def hidden(first_block, b, bias):
        at = pl.ds(pl.multiple_of((first_block + b) * half, half), half)
        pre = dot(h_two, s.w1[:, at]) + bias[:, b * half:(b + 1) * half]
        cdf = 0.5 * (1.0 + lax.erf(pre * math.sqrt(0.5)))
        slope = cdf + pre * (jnp.exp(-0.5 * pre * pre) * (1.0 / math.sqrt(2 * math.pi)))
        s.act[first_block + b] = (pre * cdf).astype(BF16)
        s.dp[first_block + b] = (s.d_act[first_block + b] * slope).astype(BF16)

    got_dp = []
    for b in range(nb):
        hidden(x * nb, b, halves_b_fc1[0])
        got_dp.append(push(s.dp.at[x * nb + b], s.dp_r.at[b], PY))

    def turn(zz):
        for k in range(nb // 2):
            s.act_t[zz, k * half:(k + 1) * half, :] = s.act[x * nb + zz * (nb // 2) + k].T

    turn(1 - z_low)
    got_act = push(s.act_t.at[1 - z_low], s.act_r, PZ1)
    turn(z_low)

    got_c1, got_z1, got_w1 = [None] * nb, [None] * nb, [None] * nb

    def fc1_product(b):
        if b == 0:
            got_h2()
            s.h2_g[0, 0] = blocks(s.h2_t, c, y)
            s.h2_g[0, 1] = blocks(s.h2_t, 1 - c, y)
        got_dp[b]()
        right = jnp.concatenate([s.dp[x * nb + b], s.dp_r[b]], axis=0)
        left = jnp.concatenate([s.h2_g[0], s.h2_r[...]], axis=-1)
        s.fc1_cs[b] = dot(left[1], right).astype(BF16)
        got_c1[b] = push(s.fc1_cs.at[b], s.fc1_cr.at[b], PC)
        s.fc1[b] = dot(left[0], right)

    def fc1_rows(b):
        kept, leaving = ((0, 2), (1, 3)) if b in Z2_FIRST else ((0, 1), (2, 3))
        return [[slice(k * blk, (k + 1) * blk) for k in side] for side in (kept, leaving)]

    def fc1_core(b):
        got_c1[b]()
        s.fc1[b] = s.fc1[b] + s.fc1_cr[b].astype(F32)
        for k, at in enumerate(fc1_rows(b)[1]):
            s.fc1_zs[b, k * blk:(k + 1) * blk, :] = s.fc1[b, at, :].astype(BF16)
        got_z1[b] = push(s.fc1_zs.at[b], s.fc1_zr.at[b], PZ2 if b in Z2_FIRST else PZ1)

    def fc1_z(b):
        got_z1[b]()
        s.fc1_ws[b] = (
            s.fc1[b, fc1_rows(b)[0][1], :] + s.fc1_zr[b, blk:, :].astype(F32)
        ).astype(BF16)
        got_w1[b] = push(s.fc1_ws.at[b], s.fc1_wr.at[b], PZ1 if b in Z2_FIRST else PZ2)

    def fc1_end(b):
        got_w1[b]()
        out_w1[:, b * half:(b + 1) * half] = (
            s.fc1[b, :blk, :] + s.fc1_zr[b, :blk, :].astype(F32) + s.fc1_wr[b].astype(F32)
        )

    live = types.SimpleNamespace()
    hb = fblk // 2
    got_c2, got_x2, got_y2, got_w2 = ([None] * 2 for _ in range(4))

    def fc2_side(cc, k):
        left = jnp.concatenate(
            [
                jnp.concatenate([s.act_t[z_low, at, :], s.act_r[at, :]], axis=-1)
                for at in (
                    pl.ds(pl.multiple_of((yy * 2 + cc) * fblk + k * hb, hb), hb)
                    for yy in (y, 1 - y)
                )
            ],
            axis=0,
        )
        return dot(left, s.dm[...].reshape(4 * rows, width))

    def fc2_product(k):
        if got_c2 == [None, None]:
            for got in (got_dy_z, got_dy_z2, got_act):
                got()
            s.dm[1] = (scale_m * s.dy[1].astype(F32)).astype(BF16)
        s.fc2_cs[k] = fc2_side(1 - c, k).astype(BF16)
        got_c2[k] = push(s.fc2_cs.at[k], s.fc2_cr.at[k], PC)

    def fc2_rest(k):
        s.fc2[k] = fc2_side(c, k)

    def fc2_core(k):
        got_c2[k]()
        s.fc2[k] = s.fc2[k] + s.fc2_cr[k].astype(F32)
        s.fc2_xs[k] = s.fc2[k, :, theirs].astype(BF16)
        got_x2[k] = push(s.fc2_xs.at[k], s.fc2_xr.at[k], PX)
        s.fc2_all[k, x] = s.fc2[k, :, mine]

    def fc2_swap(k):
        got_x2[k]()
        s.fc2_all[k, 1 - x] = s.fc2_xr[k].astype(F32)
        s.fc2_ys[k] = s.fc2_all[k, :, hb:, :].astype(BF16)
        got_y2[k] = push(s.fc2_ys.at[k], s.fc2_yr.at[k], PY)

    def fc2_y(k):
        got_y2[k]()
        s.fc2_ws[k] = (
            s.fc2_all[k, 1 - z_high, :hb, :] + s.fc2_yr[k, 1 - z_high].astype(F32)
        ).astype(BF16)
        got_w2[k] = push(s.fc2_ws.at[k], s.fc2_wr.at[k], PZ2)

    def fc2_end(k):
        got_w2[k]()
        out_w2[k * hb:(k + 1) * hb, :] = (
            s.fc2_all[k, z_high, :hb, :]
            + s.fc2_yr[k, z_high].astype(F32)
            + s.fc2_wr[k].astype(F32)
        )

    yrows, zrows = 4 * blk, 2 * blk
    got_c, got_y, got_yr, got_zsq, got_wsq = ([None] * 4 for _ in range(5))

    def square(i, left_t, right):
        for leave in (1, 0):
            cc = 1 - c if leave else c
            left = jnp.concatenate([blocks(left_t, cc, y), blocks(left_t, cc, 1 - y)], axis=0)
            total = dot(left, right)
            if leave:
                s.sq_cs[i] = total.astype(BF16)
                got_c[i] = push(s.sq_cs.at[i], s.sq_cr.at[i], PC)
            else:
                s.sq[i] = total

    def square_core(i):
        got_c[i]()
        s.sq[i] = s.sq[i] + s.sq_cr[i].astype(F32)
        if i in Z_FIRST:
            for k in range(2):
                s.sq_zs[i, k] = s.sq[i, k * yrows + zrows:(k + 1) * yrows, :].astype(BF16)
            got_zsq[i] = push(s.sq_zs.at[i], s.sq_zr.at[i], PZ1)
        else:
            s.sq_ys[i, 1] = s.sq[i, yrows + zrows:, :].astype(BF16)
            got_y[i] = push(s.sq_ys.at[i, 1], s.sq_yr.at[i, 1], PY)

    def square_core_rest(i):
        s.sq_ys[i, 0] = s.sq[i, yrows:yrows + zrows, :].astype(BF16)
        got_yr[i] = push(s.sq_ys.at[i, 0], s.sq_yr.at[i, 0], PY)

    def square_y(i):
        if i in Z_FIRST:
            got_zsq[i]()
            s.sq_ys[i, 0] = (
                s.sq[i, yrows:yrows + zrows, :] + s.sq_zr[i, 1].astype(F32)
            ).astype(BF16)
            got_yr[i] = push(s.sq_ys.at[i, 0], s.sq_yr.at[i, 0], PY)
        else:
            got_y[i]()
            s.sq_zs[i, 0] = (s.sq[i, zrows:yrows, :] + s.sq_yr[i, 1].astype(F32)).astype(BF16)
            got_zsq[i] = push(s.sq_zs.at[i, 0], s.sq_zr.at[i, 0], PZ1)

    def square_z(i):
        got_yr[i]()
        if i not in Z_FIRST:
            got_zsq[i]()
        s.sq[i, :zrows, :] = (
            s.sq[i, :zrows, :] + s.sq_yr[i, 0].astype(F32) + s.sq_zr[i, 0].astype(F32)
        )
        s.sq_ws[i] = s.sq[i, blk:zrows, :].astype(BF16)
        got_wsq[i] = push(s.sq_ws.at[i], s.sq_wr.at[i], PZ2)

    def square_end(i):
        got_wsq[i]()
        (out_wo, out_wv, out_wk, out_wq)[i][...] = (
            s.sq[i, :blk, :] + s.sq_wr[i].astype(F32)
        )

    def hidden_others():
        act_back(other, (1 - x) * nb, nb)
        for b in range(nb):
            hidden((1 - x) * nb, b, halves_b_fc1[1])
        s.branch[...] = branch
        s.resid[...] = resid

    def d_resid():
        d_h2 = jnp.zeros((width, 2 * rows), F32)
        for b in range(2 * nb):
            d_h2 += dot(s.w1[:, b * half:(b + 1) * half], s.dp[b].T)
        d_h2 = d_h2.T
        s.vec[0, 6:7, :] = col_sum(d_h2 * hat_m)
        s.vec[0, 7:8, :] = col_sum(d_h2)
        d_resid = s.dy[0].astype(F32) + normalise_back(d_h2 * gain_m, hat_m, inv_m)
        s.d_resid[...] = d_resid
        s.dbr[...] = (scale_a * d_resid).astype(BF16)

    def mlp_sums():
        mlp = jnp.zeros((2 * rows, width), F32) + b_fc2
        for b in range(2 * nb):
            mlp += dot(s.act[b], s.w2[b * half:(b + 1) * half, :])
            s.vec[0, b // 2:b // 2 + 1, (b % 2) * half:(b % 2 + 1) * half] = col_sum(
                s.dp[b].astype(F32)
            )
        s.mlp[...] = mlp
        s.vec[0, 4:5, :] = col_sum(s.dm[0].astype(F32))
        s.vec[0, 5:6, :] = col_sum(s.dy[0].astype(F32) * mlp)

    def block_end():
        out_block[0] = (s.resid[own, :] + scale_m * s.mlp[own, :]).astype(BF16)

    def heads_back(xx, cols):
        s.da[:, cols] = dot(s.wo[cols, :], s.dbr[...].T).T.astype(BF16)
        for p in range(pairs):
            pair = xx * pairs + p
            at = pl.ds(pl.multiple_of(pair * 2 * HEAD_DIM, 2 * HEAD_DIM), 2 * HEAD_DIM)
            q2 = stack(s.q[:, at])
            da2 = stack(s.da[:, at])
            prob = s.prob[pair]
            s.dv[:, at] = dot(prob.astype(BF16).T, da2).astype(BF16)
            d_prob = dot_t(da2, s.v[:, at])
            delta = jnp.sum(d_prob * prob, axis=-1, keepdims=True)
            ds = (prob * (d_prob - delta)).astype(BF16)
            s.dq[:, at] = (unstack(dot(ds, s.k[:, at])) * scale).astype(BF16)
            s.dk[:, at] = (dot(ds.T, q2) * scale).astype(BF16)

    def attention_back():
        heads_back(x, mine)

    def attention_back_others():
        heads_back(1 - x, theirs)

    turned = set()

    def square_product(i):
        kind = (0, 1, 1, 2)[i]
        if kind not in turned:
            turned.add(kind)
            left, left_t = ((s.att, s.att_t), (s.hk, s.hk_t), (s.hq, s.hq_t))[kind]
            left_t[...] = left[...].T
        square(
            i,
            (s.att_t, s.hk_t, s.hk_t, s.hq_t)[i],
            (s.dbr, s.dv, s.dk, s.dq)[i][:, mine],
        )

    def norms_back():
        dhk = dot_t(s.dk[...], s.wk[...]) + dot_t(s.dv[...], s.wv[...])
        dhq = dot_t(s.dq[...], s.wq[...])
        s.dx[0] = dhk[:2 * rows] * gain_k
        s.dx[1] = dhk[2 * rows:] * gain_k + dhq * gain_q
        s.vec2[0, 0:1, :] = col_sum(s.dbr[...].astype(F32))
        s.vec2[0, 1:2, :] = col_sum(s.d_resid[...] * s.branch[...])
        s.vec2[0, 2:3, :] = col_sum(s.dq[...].astype(F32))
        s.vec2[0, 3:4, :] = col_sum(s.dv[...].astype(F32))
        s.vec2[0, 4:5, :] = col_sum(dhq * s.hat[2 * rows:, :])
        s.vec2[0, 5:6, :] = col_sum(dhq)
        s.vec2[0, 6:7, :] = col_sum(dhk * s.hat[...])
        s.vec2[0, 7:8, :] = col_sum(dhk)

    def norms_end():
        out_dl[0] = normalise_back(s.dx[0, own, :], hat_l, inv_l)
        out_dq[0] = s.d_resid[own, :] + normalise_back(s.dx[1, own, :], hat_q, inv_q)

    routes = (PZ2, PZ1, PY, PC)
    got_v = [None] * 2

    def vector(g, step):
        if step == 0:
            s.part[g, 0] = (s.vec, s.vec2)[g][0, :, mine]
        else:
            got_v[g]()
            if step < 5:
                s.part[g, step] = s.part[g, step - 1] + s.part_r[g, step - 1]
        at = slice(g * 8, g * 8 + 8)
        if step < 4:
            got_v[g] = push(s.part.at[g, step], s.part_r.at[g, step], routes[step])
        elif step == 4:
            out_vec[at, mine] = s.part[g, 4]
            got_v[g] = push(s.part.at[g, 4], s.part_r.at[g, 4], PX)
        else:
            out_vec[at, theirs] = s.part_r[g, 4]

    pl.semaphore_wait(s.ready, z_links)
    V, K, Q, O = 1, 2, 3, 0
    hidden_others()
    d_resid()
    square_product(O)
    attention_back()
    square_product(V)
    square_core(O)
    fc1_product(0)
    attention_back_others()
    fc1_product(1)
    square_core(V)
    fc1_core(0)
    fc2_product(1)
    mlp_sums()
    fc1_product(2)
    fc2_rest(1)
    vector(0, 0)
    fc2_core(1)
    square_product(K)
    fc1_core(2)
    fc2_product(0)
    square_y(O)
    fc2_rest(0)
    fc1_core(1)
    fc1_product(3)
    square_core(K)
    norms_back()
    square_core_rest(V)
    vector(1, 0)
    fc1_core(3)
    fc2_core(0)
    square_y(V)
    vector(0, 1)
    square_z(O)
    fc1_z(2)
    square_product(Q)
    fc2_swap(1)
    fc1_z(3)
    block_end()
    vector(1, 1)
    square_core(Q)
    fc2_swap(0)
    square_z(V)
    square_core_rest(K)
    norms_end()
    square_y(K)
    fc2_y(1)
    fc2_y(0)
    vector(1, 2)
    square_y(Q)
    fc1_z(0)
    vector(0, 2)
    square_z(K)
    vector(1, 3)
    square_z(Q)
    vector(0, 3)
    vector(1, 4)
    square_end(O)
    fc1_z(1)
    fc1_end(2)
    fc2_end(1)
    vector(0, 4)
    fc1_end(3)
    fc1_end(1)
    square_end(V)
    square_end(K)
    vector(0, 5)
    fc2_end(0)
    vector(1, 5)
    fc1_end(0)
    square_end(Q)
    for copy in sent:
        copy.wait_send()


def fused(share, args):
    (queries, latents, positions, vis_ok, msk_ok, dy, w_query, w_key, w_value, w_out, w_fc1, w_fc2) = args[:12]
    vectors = args[12:]
    _, rows, width = queries.shape
    ff = w_fc1.shape[1]
    half = width // 2
    blk, fblk, hid = width // GROUPS, ff // GROUPS, ff // 2
    nb = hid // half
    pairs = half // (2 * HEAD_DIM)
    vm = pltpu.VMEM
    scratch = dict(
        send=pltpu.SemaphoreType.DMA((96,)),
        recv=pltpu.SemaphoreType.DMA((96,)),
        load=pltpu.SemaphoreType.DMA((32,)),
        ready=pltpu.SemaphoreType.REGULAR,
        rows=vm((12, width), F32),
        b_fc1=vm((ff,), F32),
        ok=vm((2, 1, 2 * rows), jnp.int32),
        pos=vm((1, rows), jnp.int32),
        dy=vm((2, 2 * rows, width), BF16),
        qraw=vm((2 * rows, width), BF16),
        lraw=vm((2 * rows, width), BF16),
        ppos=vm((1, rows), jnp.int32),
        w2=vm((ff, width), BF16),
        w1=vm((width, ff), BF16),
        wo=vm((width, width), BF16),
        wk=vm((width, width), BF16),
        wv=vm((width, width), BF16),
        wq=vm((width, width), BF16),
        qin=vm((2 * rows, width), F32),
        hat=vm((4 * rows, width), F32),
        hq=vm((2 * rows, width), BF16),
        hk=vm((4 * rows, width), BF16),
        hq_t=vm((width, 2 * rows), BF16),
        hk_t=vm((width, 4 * rows), BF16),
        att_t=vm((width, 2 * rows), BF16),
        h2_t=vm((width, 2 * rows), BF16),
        act_t=vm((2, hid // 2, 2 * rows), BF16),
        q=vm((2 * rows, width), BF16),
        k=vm((4 * rows, width), BF16),
        v=vm((4 * rows, width), BF16),
        prob=vm((2 * pairs, 4 * rows, 4 * rows), F32),
        att=vm((2 * rows, width), BF16),
        branch=vm((2 * rows, width), F32),
        resid=vm((2 * rows, width), F32),
        d_resid=vm((2 * rows, width), F32),
        mlp=vm((2 * rows, width), F32),
        d_act=vm((2 * nb, 2 * rows, half), F32),
        dm=vm((2, 2 * rows, width), BF16),
        h2_g=vm((2, 2, 4 * blk, 2 * rows), BF16),
        h2_r=vm((2, 4 * blk, 2 * rows), BF16),
        act=vm((2 * nb, 2 * rows, half), BF16),
        act_r=vm((hid // 2, 2 * rows), BF16),
        dp=vm((2 * nb, 2 * rows, half), BF16),
        dp_r=vm((nb, 2 * rows, half), BF16),
        dbr=vm((2 * rows, width), BF16),
        da=vm((2 * rows, width), BF16),
        dq=vm((2 * rows, width), BF16),
        dk=vm((4 * rows, width), BF16),
        dv=vm((4 * rows, width), BF16),
        dx=vm((2, 2 * rows, width), F32),
        sq=vm((4, 8 * blk, half), F32),
        sq_cs=vm((4, 8 * blk, half), BF16),
        sq_cr=vm((4, 8 * blk, half), BF16),
        sq_ys=vm((4, 2, 2 * blk, half), BF16),
        sq_yr=vm((4, 2, 2 * blk, half), BF16),
        sq_zs=vm((4, 2, 2 * blk, half), BF16),
        sq_zr=vm((4, 2, 2 * blk, half), BF16),
        sq_ws=vm((4, blk, half), BF16),
        sq_wr=vm((4, blk, half), BF16),
        fc2=vm((2, fblk, width), F32),
        fc2_cs=vm((2, fblk, width), BF16),
        fc2_cr=vm((2, fblk, width), BF16),
        fc2_xs=vm((2, fblk, half), BF16),
        fc2_xr=vm((2, fblk, half), BF16),
        fc2_all=vm((2, 2, fblk, half), F32),
        fc2_ys=vm((2, 2, fblk // 2, half), BF16),
        fc2_yr=vm((2, 2, fblk // 2, half), BF16),
        fc2_ws=vm((2, fblk // 2, half), BF16),
        fc2_wr=vm((2, fblk // 2, half), BF16),
        fc1=vm((nb, 4 * blk, half), F32),
        fc1_cs=vm((nb, 4 * blk, half), BF16),
        fc1_cr=vm((nb, 4 * blk, half), BF16),
        fc1_zs=vm((nb, 2 * blk, half), BF16),
        fc1_zr=vm((nb, 2 * blk, half), BF16),
        fc1_ws=vm((nb, blk, half), BF16),
        fc1_wr=vm((nb, blk, half), BF16),
        part=vm((2, 5, 8, half), F32),
        part_r=vm((2, 5, 8, half), F32),
        vec=vm((1, 8, width), F32),
        vec2=vm((1, 8, width), F32),
    )
    ANY = pl.BlockSpec(memory_space=pl.ANY)
    VMEM = pl.BlockSpec(memory_space=pltpu.VMEM)
    sds = jax.ShapeDtypeStruct
    return pl.pallas_call(
        functools.partial(kernel, (rows, width, ff, share)),
        out_shape=(
            vm((1, rows, width), BF16),
            vm((1, rows, width), F32),
            vm((1, rows, width), F32),
            vm((blk, half), F32),
            vm((blk, half), F32),
            vm((blk, half), F32),
            vm((blk, half), F32),
            vm((blk, ff // 2), F32),
            vm((fblk, half), F32),
            vm((16, width), F32),
        ),
        in_specs=[ANY] * 25,
        out_specs=[VMEM] * 10,
        scratch_shapes=[scratch],
        compiler_params=pltpu.CompilerParams(
            collective_id=0, has_side_effects=True, vmem_limit_bytes=60 << 20
        ),
        cost_estimate=pl.CostEstimate(
            flops=6 * 10**9, bytes_accessed=16 * 10**6, transcendentals=10**6
        ),
    )(queries, latents, positions, vis_ok, msk_ok, dy, w_query, w_key, w_value, w_out, w_fc1, w_fc2, *vectors)


def finish_kernel(count, *refs):
    arrays, table = refs[:count], refs[count]
    outs, rows = refs[count + 1:2 * count + 1], refs[2 * count + 1:-1]
    sems = refs[-1]
    copies = [
        pltpu.make_async_copy(src, dst, sems.at[i]) for i, (src, dst) in enumerate(zip(arrays, outs))
    ]
    for copy in copies:
        copy.start()
    width = table.shape[1]
    parts = rows[0].shape[0] // width
    for k in range(parts):
        rows[0][k * width:(k + 1) * width] = table[k, :]
    for k, row in enumerate(rows[1:]):
        row[...] = table[parts + k, :]
    for copy in copies:
        copy.wait()


def finish(arrays, table, ff, share):
    if share == 1:
        arrays = tuple(pltpu.with_memory_space_constraint(a, pltpu.VMEM) for a in arrays)
        table = pltpu.with_memory_space_constraint(table, pltpu.VMEM)
    count, width = len(arrays), table.shape[1]
    sds = jax.ShapeDtypeStruct
    vectors = table.shape[0] - ff // width
    ANY = pl.BlockSpec(memory_space=pl.ANY)
    VMEM = pl.BlockSpec(memory_space=pltpu.VMEM)
    return pl.pallas_call(
        functools.partial(finish_kernel, count),
        out_shape=tuple(sds(a.shape, a.dtype) for a in arrays)
        + (sds((ff,), F32),)
        + (sds((width,), F32),) * vectors,
        in_specs=[VMEM] * (count + 1),
        out_specs=[ANY] * count + [VMEM] * (1 + vectors),
        scratch_shapes=[pltpu.SemaphoreType.DMA((count,))],
    )(*arrays, table)


def per_device(
    queries, latents, positions, visible_valid, masked_valid,
    w_query, b_query, w_key, w_value, b_value, w_out, b_out, w_fc1, b_fc1, w_fc2, b_fc2,
    gain_query, shift_query, gain_keys, shift_keys, gain_mlp, shift_mlp, scale_attn, scale_mlp,
    out_grad,
):
    parts = lax.axis_size("dp")
    share = parts // GROUPS
    out = fused(
        share,
        (
            queries, latents, positions, visible_valid, masked_valid, out_grad,
            w_query, w_key, w_value, w_out, w_fc1, w_fc2,
            b_query, b_value, b_out, b_fc1, b_fc2,
            gain_query, shift_query, gain_keys, shift_keys, gain_mlp, shift_mlp, scale_attn, scale_mlp,
        ),
    )
    block_out, d_queries, d_latents, wq, wk, wv, wo, w1, w2, vec = out
    if share > 1:
        groups = [[n * share + i for i in range(share)] for n in range(GROUPS)]
        wq, wk, wv, wo, w1, w2 = (
            lax.psum_scatter(
                w, "dp", scatter_dimension=0, axis_index_groups=groups, tiled=True
            )
            for w in (wq, wk, wv, wo, w1, w2)
        )
        vec = lax.psum(vec, "dp", axis_index_groups=groups)
    arrays = (block_out, d_queries, d_latents, wq, wk, wv, wo, w1, w2)
    done = finish(arrays, vec, w_fc1.shape[1], share)
    block_out, d_queries, d_latents, wq, wk, wv, wo, w1, w2, b1 = done[:10]
    b2, sm, gm, hm, bo, sa, bq, bv, gq, hq, gk, hk = done[10:]
    return (
        block_out, d_queries, d_latents,
        wq, bq, wk, wv, bv, wo, bo, w1, b1, w2, b2,
        gq, hq, gk, hk, gm, hm, sa, sm,
    )


def solution(mesh):
    rows3 = P("dp", "qry", None)
    split = P("dp", "qry")
    full = P()
    return jax.shard_map(
        per_device,
        mesh=mesh,
        in_specs=(rows3, rows3, split, P("dp", None), P("dp", None)) + (full,) * 19 + (rows3,),
        out_specs=(
            rows3, rows3, rows3,
            split, full, split, split, full, split, full, split, full, split,
        ) + (full,) * 9,
        check_vma=False,
    )
```

```python
import functools
import math
import types

import jax
import jax.numpy as jnp
from jax import lax
from jax.experimental import pallas as pl
from jax.experimental.pallas import tpu as pltpu
from jax.sharding import PartitionSpec as P

HEAD_DIM = 64
MESH = pl.DeviceIdType.MESH
F32 = jnp.float32
BF16 = jnp.bfloat16
GROUPS = 16
Z_ORDER = (0, 2, 1, 3)
Z2_FIRST = (0, 1)
Z_FIRST = (3, 0)


def dot(a, b):
    return lax.dot_general(a, b, (((1,), (0,)), ((), ())), preferred_element_type=F32)


def dot_t(a, b):
    return lax.dot_general(a, b, (((1,), (1,)), ((), ())), preferred_element_type=F32)


def col_sum(a):
    return jnp.sum(a, axis=0, keepdims=True)


def normalise(v):
    centre = v - jnp.mean(v, axis=-1, keepdims=True)
    spread = jnp.mean(centre * centre, axis=-1, keepdims=True)
    inv = lax.rsqrt(spread + 1e-06)
    return centre * inv, inv


def normalise_back(grad_hat, hat, inv):
    m1 = jnp.mean(grad_hat, axis=-1, keepdims=True)
    m2 = jnp.mean(grad_hat * hat, axis=-1, keepdims=True)
    return inv * (grad_hat - m1 - hat * m2)


def sinusoid(places, width):
    index = lax.broadcasted_iota(jnp.int32, (1, width), 1)
    half = index // 2
    freq = jnp.exp(-(2.0 * half.astype(F32) / width) * math.log(10000.0))
    odd = (index - 2 * half).astype(F32)
    angle = places * freq
    turns = jnp.floor(angle * (2.0 / math.pi) + 0.5)
    rest = angle - turns * 1.5703125
    rest = rest - turns * 4.8351287841796875e-4
    rest = rest - turns * 3.1385570764541626e-07
    sq = rest * rest
    sine = rest * (
        1.0 + sq * (-1.0 / 6 + sq * (1.0 / 120 + sq * (-1.0 / 5040 + sq * (1.0 / 362880))))
    )
    cosine = 1.0 + sq * (-0.5 + sq * (1.0 / 24 + sq * (-1.0 / 720 + sq * (1.0 / 40320))))
    quarter = turns + odd
    pairs = jnp.floor(quarter * 0.5)
    parity = quarter - 2.0 * pairs
    flips = pairs - 2.0 * jnp.floor(pairs * 0.5)
    value = jnp.where(parity > 0.5, cosine, sine)
    return jnp.where(flips > 0.5, -value, value)


def kernel(
    shape,
    queries, latents, positions, vis_ok, msk_ok, dy_in,
    w_query, w_key, w_value, w_out, w_fc1, w_fc2,
    b_query, b_value, b_out, b_fc1, b_fc2,
    gain_q, shift_q, gain_k, shift_k, gain_m, shift_m, scale_a, scale_m,
    out_block, out_dq, out_dl, out_wq, out_wk, out_wv, out_wo, out_w1, out_w2, out_vec,
    s,
):
    s = types.SimpleNamespace(**s)
    rows, width, ff, share = shape
    half = width // 2
    pairs = half // (2 * HEAD_DIM)
    blk = width // GROUPS
    fblk = ff // GROUPS
    hid = ff // 2
    nb = hid // half
    scale = 1.0 / math.sqrt(HEAD_DIM)

    x = lax.axis_index("qry")
    place = lax.axis_index("dp")
    n = place // share
    low = place - n * share
    z = n // 4
    y = (n // 2) % 2
    c = n % 2
    zs = (z, z + 1 - 2 * (z % 2), (z + 2) % 4, 3 - z)

    def dev(zz, yy, cc, xx):
        return (((zz * 2 + yy) * 2 + cc) * share + low, xx)

    PX = dev(z, y, c, 1 - x)
    PY = dev(z, 1 - y, c, x)
    PC = dev(z, y, 1 - c, x)
    PZ1 = dev(zs[1], y, c, x)
    PZ2 = dev(zs[2], y, c, x)
    z_low = z % 2
    z_high = z // 2

    counter = [0]
    sent = []

    def push(src, dst, peer, landing=None):
        i = counter[0]
        counter[0] += 1

        def describe(to):
            return pltpu.make_async_remote_copy(
                src_ref=src, dst_ref=to, send_sem=s.send.at[i], recv_sem=s.recv.at[i],
                device_id=peer, device_id_type=MESH,
            )

        copy = describe(dst)
        copy.start()
        sent.append(copy)
        arrival = copy if landing is None else describe(landing)
        return arrival.wait_recv

    barrier = pltpu.get_barrier_semaphore()

    def tell(sem, peer):
        pl.semaphore_signal(sem, inc=1, device_id=peer, device_id_type=MESH)

    def tell_z(sem):
        @pl.when(z > 0)
        def _():
            tell(sem, dev(z - 1, y, c, x))

        @pl.when(z < 3)
        def _():
            tell(sem, dev(z + 1, y, c, x))

    z_links = 2 - (z + 3) // 3 + (z + 1) // 2 - z // 3
    for peer in (PX, PY, PC):
        tell(barrier, peer)
    tell_z(barrier)

    loads = []

    def load(src, dst):
        copy = pltpu.make_async_copy(src, dst, s.load.at[len(loads)])
        copy.start()
        loads.append(copy)
        return copy.wait

    own = pl.ds(pl.multiple_of(x * rows, rows), rows)
    other = pl.ds(pl.multiple_of((1 - x) * rows, rows), rows)
    low_own = pl.ds(pl.multiple_of((2 + x) * rows, rows), rows)
    low_other = pl.ds(pl.multiple_of((3 - x) * rows, rows), rows)
    mine = pl.ds(pl.multiple_of(x * half, half), half)
    theirs = pl.ds(pl.multiple_of((1 - x) * half, half), half)

    def row_of(ref, i):
        wait = load(ref, s.rows.at[i])

        def value():
            wait()
            return s.rows[i].reshape(1, width)

        return value

    load_q = load(queries.at[0], s.qraw.at[own])
    load_p = load(positions, s.pos)
    load_l = load(latents.at[0], s.lraw.at[own])
    gain_q, shift_q, gain_k, shift_k = (
        row_of(ref, i) for i, ref in enumerate((gain_q, shift_q, gain_k, shift_k))
    )
    load_wk = load(w_key, s.wk)
    load_wv = load(w_value, s.wv)
    load_wq = load(w_query, s.wq)
    b_query, b_value, b_out, b_fc2, gain_m, shift_m, scale_a, scale_m = (
        row_of(ref, 4 + i)
        for i, ref in enumerate((b_query, b_value, b_out, b_fc2, gain_m, shift_m, scale_a, scale_m))
    )
    load_b1 = load(b_fc1, s.b_fc1)
    load_ok = [load(vis_ok, s.ok.at[0]), load(msk_ok, s.ok.at[1])]
    load_dy = load(dy_in.at[0], s.dy.at[0, own])
    load_w2 = load(w_fc2, s.w2)
    load_wo = load(w_out, s.wo)
    load_w1 = load(w_fc1, s.w1)

    eye = lax.broadcasted_iota(jnp.int32, (rows, rows), 0) == lax.broadcasted_iota(
        jnp.int32, (rows, rows), 1
    )

    gain_q, shift_q, gain_k, shift_k = gain_q(), shift_q(), gain_k(), shift_k()

    def qry_half(pos_ref, at, low_at):
        row = jnp.broadcast_to(pos_ref[...].astype(F32), (rows, rows))
        places = jnp.sum(jnp.where(eye, row, 0.0), axis=1, keepdims=True)
        qin = s.qraw[at, :].astype(F32) + sinusoid(places, width)
        s.qin[at, :] = qin
        hat, inv = normalise(qin)
        s.hat[low_at, :] = hat
        hq = (hat * gain_q + shift_q).astype(BF16)
        hkq = (hat * gain_k + shift_k).astype(BF16)
        s.hq[at, :] = hq
        s.hk[low_at, :] = hkq
        return hat, inv, hq, hkq

    def lat_half(at):
        hat, inv = normalise(s.lraw[at, :].astype(F32))
        s.hat[at, :] = hat
        hkl = (hat * gain_k + shift_k).astype(BF16)
        s.hk[at, :] = hkl
        return hat, inv, hkl

    def project(hk, at):
        s.k[at, :] = dot(hk, s.wk[...]).astype(BF16)
        s.v[at, :] = (dot(hk, s.wv[...]) + b_value).astype(BF16)

    def project_query(hq, at):
        s.q[at, :] = (dot(hq, s.wq[...]) + b_query).astype(BF16)

    load_q()
    load_p()
    hat_q, inv_q, hq, hkq = qry_half(s.pos, own, low_own)
    load_l()
    hat_l, inv_l, hkl = lat_half(own)

    pl.semaphore_wait(barrier, 3 + z_links)
    got_p = push(positions, s.ppos, PX)
    got_q = push(queries.at[0], s.qraw.at[own], PX, s.qraw.at[other])
    got_l = push(latents.at[0], s.lraw.at[own], PX, s.lraw.at[other])
    got_dy = push(dy_in.at[0], s.dy.at[0, own], PX, s.dy.at[0, other])
    got_dy_z = push(dy_in.at[0], s.dy.at[1, own], PZ1)
    tell_z(s.ready)

    load_wk()
    load_wv()
    load_wq()
    b_query, b_value, b_out, b_fc2, gain_m, shift_m, scale_a, scale_m = (
        value() for value in (b_query, b_value, b_out, b_fc2, gain_m, shift_m, scale_a, scale_m)
    )
    load_b1()
    b_fc1 = s.b_fc1[...].reshape(1, ff)
    halves_b_fc1 = [
        jnp.where(x == k, b_fc1[:, :hid], b_fc1[:, hid:]) for k in range(2)
    ]
    project(hkl, own)
    project(hkq, low_own)
    project_query(hq, own)

    def act_back(at, first_block, blocks):
        for b in range(blocks):
            units = pl.ds(pl.multiple_of((first_block + b) * half, half), half)
            s.d_act[first_block + b, at, :] = dot_t(s.dm[0, at, :], s.w2[units, :])

    def d_mlp(at):
        s.dm[0, at, :] = (scale_m * s.dy[0, at, :].astype(F32)).astype(BF16)

    load_dy()
    load_w2()
    d_mlp(own)
    act_back(own, 0, 2 * nb)
    got_p()
    got_q()
    _, _, hq_o, hkq_o = qry_half(s.ppos, other, low_other)
    project(hkq_o, low_other)
    project_query(hq_o, other)
    got_l()
    _, _, hkl_o = lat_half(other)
    project(hkl_o, other)
    for wait in load_ok:
        wait()

    ok = jnp.concatenate([s.ok[0], s.ok[1]], axis=1) > 0
    lane = lax.broadcasted_iota(jnp.int32, (2 * rows, 2 * HEAD_DIM), 1)
    first = lane < HEAD_DIM

    def stack(pair):
        zero = jnp.zeros_like(pair)
        return jnp.concatenate([jnp.where(first, pair, zero), jnp.where(first, zero, pair)], axis=0)

    def unstack(both):
        return jnp.where(first, both[:2 * rows], both[2 * rows:])

    for pair in range(2 * pairs):
        at = slice(pair * 2 * HEAD_DIM, (pair + 1) * 2 * HEAD_DIM)
        raw = dot_t(stack(s.q[:, at] * scale), s.k[:, at])
        scores = jnp.where(ok, raw, -1e30)
        peak = jnp.max(scores, axis=-1, keepdims=True)
        weight = jnp.exp(scores - peak)
        prob = weight * (1.0 / jnp.sum(weight, axis=-1, keepdims=True))
        s.prob[pair] = prob
        s.att[:, at] = unstack(dot(prob.astype(BF16), s.v[:, at])).astype(BF16)

    got_dy()
    got_dy_z2 = push(s.dy.at[0, other], s.dy.at[1, other], PZ1)
    load_wo()
    branch = dot(s.att[...], s.wo[...]) + b_out
    resid = s.qin[...] + scale_a * branch
    hat_m, inv_m = normalise(resid)
    h_two = (hat_m * gain_m + shift_m).astype(BF16)

    def blocks(ref, cc, yy):
        return jnp.concatenate(
            [
                ref[pl.ds(pl.multiple_of(((zs[t] * 2 + yy) * 2 + cc) * blk, blk), blk), :]
                for t in Z_ORDER
            ],
            axis=0,
        )

    s.h2_t[...] = h_two.T
    s.h2_g[1, 0] = blocks(s.h2_t, c, 1 - y)
    s.h2_g[1, 1] = blocks(s.h2_t, 1 - c, 1 - y)
    got_h2 = push(s.h2_g.at[1], s.h2_r, PY)
    d_mlp(other)
    act_back(other, x * nb, nb)
    load_w1()

    def hidden(first_block, b, bias):
        at = pl.ds(pl.multiple_of((first_block + b) * half, half), half)
        pre = dot(h_two, s.w1[:, at]) + bias[:, b * half:(b + 1) * half]
        cdf = 0.5 * (1.0 + lax.erf(pre * math.sqrt(0.5)))
        slope = cdf + pre * (jnp.exp(-0.5 * pre * pre) * (1.0 / math.sqrt(2 * math.pi)))
        s.act[first_block + b] = (pre * cdf).astype(BF16)
        s.dp[first_block + b] = (s.d_act[first_block + b] * slope).astype(BF16)

    got_dp = []
    for b in range(nb):
        hidden(x * nb, b, halves_b_fc1[0])
        got_dp.append(push(s.dp.at[x * nb + b], s.dp_r.at[b], PY))

    def turn(zz):
        for k in range(nb // 2):
            s.act_t[zz, k * half:(k + 1) * half, :] = s.act[x * nb + zz * (nb // 2) + k].T

    turn(1 - z_low)
    got_act = push(s.act_t.at[1 - z_low], s.act_r, PZ1)
    turn(z_low)

    got_c1, got_z1, got_w1 = [None] * nb, [None] * nb, [None] * nb

    def fc1_product(b):
        if b == 0:
            got_h2()
            s.h2_g[0, 0] = blocks(s.h2_t, c, y)
            s.h2_g[0, 1] = blocks(s.h2_t, 1 - c, y)
        got_dp[b]()
        right = jnp.concatenate([s.dp[x * nb + b], s.dp_r[b]], axis=0)
        left = jnp.concatenate([s.h2_g[0], s.h2_r[...]], axis=-1)
        s.fc1_cs[b] = dot(left[1], right).astype(BF16)
        got_c1[b] = push(s.fc1_cs.at[b], s.fc1_cr.at[b], PC)
        s.fc1[b] = dot(left[0], right)

    def fc1_rows(b):
        kept, leaving = ((0, 2), (1, 3)) if b in Z2_FIRST else ((0, 1), (2, 3))
        return [[slice(k * blk, (k + 1) * blk) for k in side] for side in (kept, leaving)]

    def fc1_core(b):
        got_c1[b]()
        s.fc1[b] = s.fc1[b] + s.fc1_cr[b].astype(F32)
        for k, at in enumerate(fc1_rows(b)[1]):
            s.fc1_zs[b, k * blk:(k + 1) * blk, :] = s.fc1[b, at, :].astype(BF16)
        got_z1[b] = push(s.fc1_zs.at[b], s.fc1_zr.at[b], PZ2 if b in Z2_FIRST else PZ1)

    def fc1_z(b):
        got_z1[b]()
        s.fc1_ws[b] = (
            s.fc1[b, fc1_rows(b)[0][1], :] + s.fc1_zr[b, blk:, :].astype(F32)
        ).astype(BF16)
        got_w1[b] = push(s.fc1_ws.at[b], s.fc1_wr.at[b], PZ1 if b in Z2_FIRST else PZ2)

    def fc1_end(b):
        got_w1[b]()
        out_w1[:, b * half:(b + 1) * half] = (
            s.fc1[b, :blk, :] + s.fc1_zr[b, :blk, :].astype(F32) + s.fc1_wr[b].astype(F32)
        )

    live = types.SimpleNamespace()
    hb = fblk // 2
    got_c2, got_x2, got_y2, got_w2 = ([None] * 2 for _ in range(4))

    def fc2_side(cc, k):
        left = jnp.concatenate(
            [
                jnp.concatenate([s.act_t[z_low, at, :], s.act_r[at, :]], axis=-1)
                for at in (
                    pl.ds(pl.multiple_of((yy * 2 + cc) * fblk + k * hb, hb), hb)
                    for yy in (y, 1 - y)
                )
            ],
            axis=0,
        )
        return dot(left, s.dm[...].reshape(4 * rows, width))

    def fc2_product(k):
        if got_c2 == [None, None]:
            for got in (got_dy_z, got_dy_z2, got_act):
                got()
            s.dm[1] = (scale_m * s.dy[1].astype(F32)).astype(BF16)
        s.fc2_cs[k] = fc2_side(1 - c, k).astype(BF16)
        got_c2[k] = push(s.fc2_cs.at[k], s.fc2_cr.at[k], PC)

    def fc2_rest(k):
        s.fc2[k] = fc2_side(c, k)

    def fc2_core(k):
        got_c2[k]()
        s.fc2[k] = s.fc2[k] + s.fc2_cr[k].astype(F32)
        s.fc2_xs[k] = s.fc2[k, :, theirs].astype(BF16)
        got_x2[k] = push(s.fc2_xs.at[k], s.fc2_xr.at[k], PX)
        s.fc2_all[k, x] = s.fc2[k, :, mine]

    def fc2_swap(k):
        got_x2[k]()
        s.fc2_all[k, 1 - x] = s.fc2_xr[k].astype(F32)
        s.fc2_ys[k] = s.fc2_all[k, :, hb:, :].astype(BF16)
        got_y2[k] = push(s.fc2_ys.at[k], s.fc2_yr.at[k], PY)

    def fc2_y(k):
        got_y2[k]()
        s.fc2_ws[k] = (
            s.fc2_all[k, 1 - z_high, :hb, :] + s.fc2_yr[k, 1 - z_high].astype(F32)
        ).astype(BF16)
        got_w2[k] = push(s.fc2_ws.at[k], s.fc2_wr.at[k], PZ2)

    def fc2_end(k):
        got_w2[k]()
        out_w2[k * hb:(k + 1) * hb, :] = (
            s.fc2_all[k, z_high, :hb, :]
            + s.fc2_yr[k, z_high].astype(F32)
            + s.fc2_wr[k].astype(F32)
        )

    yrows, zrows = 4 * blk, 2 * blk
    got_c, got_y, got_yr, got_zsq, got_wsq = ([None] * 4 for _ in range(5))

    def square(i, left_t, right):
        for leave in (1, 0):
            cc = 1 - c if leave else c
            left = jnp.concatenate([blocks(left_t, cc, y), blocks(left_t, cc, 1 - y)], axis=0)
            total = dot(left, right)
            if leave:
                s.sq_cs[i] = total.astype(BF16)
                got_c[i] = push(s.sq_cs.at[i], s.sq_cr.at[i], PC)
            else:
                s.sq[i] = total

    def square_core(i):
        got_c[i]()
        s.sq[i] = s.sq[i] + s.sq_cr[i].astype(F32)
        if i in Z_FIRST:
            for k in range(2):
                s.sq_zs[i, k] = s.sq[i, k * yrows + zrows:(k + 1) * yrows, :].astype(BF16)
            got_zsq[i] = push(s.sq_zs.at[i], s.sq_zr.at[i], PZ1)
        else:
            s.sq_ys[i, 1] = s.sq[i, yrows + zrows:, :].astype(BF16)
            got_y[i] = push(s.sq_ys.at[i, 1], s.sq_yr.at[i, 1], PY)

    def square_core_rest(i):
        s.sq_ys[i, 0] = s.sq[i, yrows:yrows + zrows, :].astype(BF16)
        got_yr[i] = push(s.sq_ys.at[i, 0], s.sq_yr.at[i, 0], PY)

    def square_y(i):
        if i in Z_FIRST:
            got_zsq[i]()
            s.sq_ys[i, 0] = (
                s.sq[i, yrows:yrows + zrows, :] + s.sq_zr[i, 1].astype(F32)
            ).astype(BF16)
            got_yr[i] = push(s.sq_ys.at[i, 0], s.sq_yr.at[i, 0], PY)
        else:
            got_y[i]()
            s.sq_zs[i, 0] = (s.sq[i, zrows:yrows, :] + s.sq_yr[i, 1].astype(F32)).astype(BF16)
            got_zsq[i] = push(s.sq_zs.at[i, 0], s.sq_zr.at[i, 0], PZ1)

    def square_z(i):
        got_yr[i]()
        if i not in Z_FIRST:
            got_zsq[i]()
        s.sq[i, :zrows, :] = (
            s.sq[i, :zrows, :] + s.sq_yr[i, 0].astype(F32) + s.sq_zr[i, 0].astype(F32)
        )
        s.sq_ws[i] = s.sq[i, blk:zrows, :].astype(BF16)
        got_wsq[i] = push(s.sq_ws.at[i], s.sq_wr.at[i], PZ2)

    def square_end(i):
        got_wsq[i]()
        (out_wo, out_wv, out_wk, out_wq)[i][...] = (
            s.sq[i, :blk, :] + s.sq_wr[i].astype(F32)
        )

    def hidden_others():
        act_back(other, (1 - x) * nb, nb)
        for b in range(nb):
            hidden((1 - x) * nb, b, halves_b_fc1[1])
        s.branch[...] = branch
        s.resid[...] = resid

    def d_resid():
        d_h2 = jnp.zeros((width, 2 * rows), F32)
        for b in range(2 * nb):
            d_h2 += dot(s.w1[:, b * half:(b + 1) * half], s.dp[b].T)
        d_h2 = d_h2.T
        s.vec[0, 6:7, :] = col_sum(d_h2 * hat_m)
        s.vec[0, 7:8, :] = col_sum(d_h2)
        d_resid = s.dy[0].astype(F32) + normalise_back(d_h2 * gain_m, hat_m, inv_m)
        s.d_resid[...] = d_resid
        s.dbr[...] = (scale_a * d_resid).astype(BF16)

    def mlp_sums():
        mlp = jnp.zeros((2 * rows, width), F32) + b_fc2
        for b in range(2 * nb):
            mlp += dot(s.act[b], s.w2[b * half:(b + 1) * half, :])
            s.vec[0, b // 2:b // 2 + 1, (b % 2) * half:(b % 2 + 1) * half] = col_sum(
                s.dp[b].astype(F32)
            )
        s.mlp[...] = mlp
        s.vec[0, 4:5, :] = col_sum(s.dm[0].astype(F32))
        s.vec[0, 5:6, :] = col_sum(s.dy[0].astype(F32) * mlp)

    def block_end():
        out_block[0] = (s.resid[own, :] + scale_m * s.mlp[own, :]).astype(BF16)

    def heads_back(xx, cols):
        s.da[:, cols] = dot(s.wo[cols, :], s.dbr[...].T).T.astype(BF16)
        for p in range(pairs):
            pair = xx * pairs + p
            at = pl.ds(pl.multiple_of(pair * 2 * HEAD_DIM, 2 * HEAD_DIM), 2 * HEAD_DIM)
            q2 = stack(s.q[:, at])
            da2 = stack(s.da[:, at])
            prob = s.prob[pair]
            s.dv[:, at] = dot(prob.astype(BF16).T, da2).astype(BF16)
            d_prob = dot_t(da2, s.v[:, at])
            delta = jnp.sum(d_prob * prob, axis=-1, keepdims=True)
            ds = (prob * (d_prob - delta)).astype(BF16)
            s.dq[:, at] = (unstack(dot(ds, s.k[:, at])) * scale).astype(BF16)
            s.dk[:, at] = (dot(ds.T, q2) * scale).astype(BF16)

    def attention_back():
        heads_back(x, mine)

    def attention_back_others():
        heads_back(1 - x, theirs)

    turned = set()

    def square_product(i):
        kind = (0, 1, 1, 2)[i]
        if kind not in turned:
            turned.add(kind)
            left, left_t = ((s.att, s.att_t), (s.hk, s.hk_t), (s.hq, s.hq_t))[kind]
            left_t[...] = left[...].T
        square(
            i,
            (s.att_t, s.hk_t, s.hk_t, s.hq_t)[i],
            (s.dbr, s.dv, s.dk, s.dq)[i][:, mine],
        )

    def norms_back():
        dhk = dot_t(s.dk[...], s.wk[...]) + dot_t(s.dv[...], s.wv[...])
        dhq = dot_t(s.dq[...], s.wq[...])
        s.dx[0] = dhk[:2 * rows] * gain_k
        s.dx[1] = dhk[2 * rows:] * gain_k + dhq * gain_q
        s.vec2[0, 0:1, :] = col_sum(s.dbr[...].astype(F32))
        s.vec2[0, 1:2, :] = col_sum(s.d_resid[...] * s.branch[...])
        s.vec2[0, 2:3, :] = col_sum(s.dq[...].astype(F32))
        s.vec2[0, 3:4, :] = col_sum(s.dv[...].astype(F32))
        s.vec2[0, 4:5, :] = col_sum(dhq * s.hat[2 * rows:, :])
        s.vec2[0, 5:6, :] = col_sum(dhq)
        s.vec2[0, 6:7, :] = col_sum(dhk * s.hat[...])
        s.vec2[0, 7:8, :] = col_sum(dhk)

    def norms_end():
        out_dl[0] = normalise_back(s.dx[0, own, :], hat_l, inv_l)
        out_dq[0] = s.d_resid[own, :] + normalise_back(s.dx[1, own, :], hat_q, inv_q)

    routes = (PZ2, PZ1, PY, PC)
    got_v = [None] * 2

    def vector(g, step):
        if step == 0:
            s.part[g, 0] = (s.vec, s.vec2)[g][0, :, mine]
        else:
            got_v[g]()
            if step < 5:
                s.part[g, step] = s.part[g, step - 1] + s.part_r[g, step - 1]
        at = slice(g * 8, g * 8 + 8)
        if step < 4:
            got_v[g] = push(s.part.at[g, step], s.part_r.at[g, step], routes[step])
        elif step == 4:
            out_vec[at, mine] = s.part[g, 4]
            got_v[g] = push(s.part.at[g, 4], s.part_r.at[g, 4], PX)
        else:
            out_vec[at, theirs] = s.part_r[g, 4]

    pl.semaphore_wait(s.ready, z_links)
    V, K, Q, O = 1, 2, 3, 0
    hidden_others()
    d_resid()
    square_product(O)
    attention_back()
    square_product(V)
    square_core(O)
    fc1_product(0)
    attention_back_others()
    square_core(V)
    fc1_core(0)
    fc2_product(1)
    mlp_sums()
    fc1_product(1)
    fc1_product(2)
    fc2_rest(1)
    vector(0, 0)
    fc2_core(1)
    square_product(K)
    fc1_core(2)
    fc2_product(0)
    square_y(O)
    fc2_rest(0)
    fc1_core(1)
    fc1_product(3)
    square_core(K)
    norms_back()
    square_core_rest(V)
    vector(1, 0)
    fc2_core(0)
    fc1_core(3)
    square_y(V)
    vector(0, 1)
    square_z(O)
    fc1_z(2)
    square_product(Q)
    fc2_swap(1)
    fc1_z(3)
    block_end()
    vector(1, 1)
    square_core(Q)
    fc2_swap(0)
    square_z(V)
    square_core_rest(K)
    norms_end()
    square_y(K)
    fc2_y(1)
    fc2_y(0)
    vector(1, 2)
    square_y(Q)
    fc1_z(0)
    vector(0, 2)
    square_z(K)
    vector(1, 3)
    square_z(Q)
    vector(1, 4)
    square_end(O)
    fc1_z(1)
    fc1_end(2)
    fc2_end(1)
    vector(0, 3)
    vector(0, 4)
    fc1_end(3)
    fc1_end(1)
    square_end(V)
    square_end(K)
    vector(0, 5)
    fc2_end(0)
    vector(1, 5)
    fc1_end(0)
    square_end(Q)
    for copy in sent:
        copy.wait_send()


def fused(share, args):
    (queries, latents, positions, vis_ok, msk_ok, dy, w_query, w_key, w_value, w_out, w_fc1, w_fc2) = args[:12]
    vectors = args[12:]
    _, rows, width = queries.shape
    ff = w_fc1.shape[1]
    half = width // 2
    blk, fblk, hid = width // GROUPS, ff // GROUPS, ff // 2
    nb = hid // half
    pairs = half // (2 * HEAD_DIM)
    vm = pltpu.VMEM
    scratch = dict(
        send=pltpu.SemaphoreType.DMA((96,)),
        recv=pltpu.SemaphoreType.DMA((96,)),
        load=pltpu.SemaphoreType.DMA((32,)),
        ready=pltpu.SemaphoreType.REGULAR,
        rows=vm((12, width), F32),
        b_fc1=vm((ff,), F32),
        ok=vm((2, 1, 2 * rows), jnp.int32),
        pos=vm((1, rows), jnp.int32),
        dy=vm((2, 2 * rows, width), BF16),
        qraw=vm((2 * rows, width), BF16),
        lraw=vm((2 * rows, width), BF16),
        ppos=vm((1, rows), jnp.int32),
        w2=vm((ff, width), BF16),
        w1=vm((width, ff), BF16),
        wo=vm((width, width), BF16),
        wk=vm((width, width), BF16),
        wv=vm((width, width), BF16),
        wq=vm((width, width), BF16),
        qin=vm((2 * rows, width), F32),
        hat=vm((4 * rows, width), F32),
        hq=vm((2 * rows, width), BF16),
        hk=vm((4 * rows, width), BF16),
        hq_t=vm((width, 2 * rows), BF16),
        hk_t=vm((width, 4 * rows), BF16),
        att_t=vm((width, 2 * rows), BF16),
        h2_t=vm((width, 2 * rows), BF16),
        act_t=vm((2, hid // 2, 2 * rows), BF16),
        q=vm((2 * rows, width), BF16),
        k=vm((4 * rows, width), BF16),
        v=vm((4 * rows, width), BF16),
        prob=vm((2 * pairs, 4 * rows, 4 * rows), F32),
        att=vm((2 * rows, width), BF16),
        branch=vm((2 * rows, width), F32),
        resid=vm((2 * rows, width), F32),
        d_resid=vm((2 * rows, width), F32),
        mlp=vm((2 * rows, width), F32),
        d_act=vm((2 * nb, 2 * rows, half), F32),
        dm=vm((2, 2 * rows, width), BF16),
        h2_g=vm((2, 2, 4 * blk, 2 * rows), BF16),
        h2_r=vm((2, 4 * blk, 2 * rows), BF16),
        act=vm((2 * nb, 2 * rows, half), BF16),
        act_r=vm((hid // 2, 2 * rows), BF16),
        dp=vm((2 * nb, 2 * rows, half), BF16),
        dp_r=vm((nb, 2 * rows, half), BF16),
        dbr=vm((2 * rows, width), BF16),
        da=vm((2 * rows, width), BF16),
        dq=vm((2 * rows, width), BF16),
        dk=vm((4 * rows, width), BF16),
        dv=vm((4 * rows, width), BF16),
        dx=vm((2, 2 * rows, width), F32),
        sq=vm((4, 8 * blk, half), F32),
        sq_cs=vm((4, 8 * blk, half), BF16),
        sq_cr=vm((4, 8 * blk, half), BF16),
        sq_ys=vm((4, 2, 2 * blk, half), BF16),
        sq_yr=vm((4, 2, 2 * blk, half), BF16),
        sq_zs=vm((4, 2, 2 * blk, half), BF16),
        sq_zr=vm((4, 2, 2 * blk, half), BF16),
        sq_ws=vm((4, blk, half), BF16),
        sq_wr=vm((4, blk, half), BF16),
        fc2=vm((2, fblk, width), F32),
        fc2_cs=vm((2, fblk, width), BF16),
        fc2_cr=vm((2, fblk, width), BF16),
        fc2_xs=vm((2, fblk, half), BF16),
        fc2_xr=vm((2, fblk, half), BF16),
        fc2_all=vm((2, 2, fblk, half), F32),
        fc2_ys=vm((2, 2, fblk // 2, half), BF16),
        fc2_yr=vm((2, 2, fblk // 2, half), BF16),
        fc2_ws=vm((2, fblk // 2, half), BF16),
        fc2_wr=vm((2, fblk // 2, half), BF16),
        fc1=vm((nb, 4 * blk, half), F32),
        fc1_cs=vm((nb, 4 * blk, half), BF16),
        fc1_cr=vm((nb, 4 * blk, half), BF16),
        fc1_zs=vm((nb, 2 * blk, half), BF16),
        fc1_zr=vm((nb, 2 * blk, half), BF16),
        fc1_ws=vm((nb, blk, half), BF16),
        fc1_wr=vm((nb, blk, half), BF16),
        part=vm((2, 5, 8, half), F32),
        part_r=vm((2, 5, 8, half), F32),
        vec=vm((1, 8, width), F32),
        vec2=vm((1, 8, width), F32),
    )
    ANY = pl.BlockSpec(memory_space=pl.ANY)
    VMEM = pl.BlockSpec(memory_space=pltpu.VMEM)
    sds = jax.ShapeDtypeStruct
    return pl.pallas_call(
        functools.partial(kernel, (rows, width, ff, share)),
        out_shape=(
            vm((1, rows, width), BF16),
            vm((1, rows, width), F32),
            vm((1, rows, width), F32),
            vm((blk, half), F32),
            vm((blk, half), F32),
            vm((blk, half), F32),
            vm((blk, half), F32),
            vm((blk, ff // 2), F32),
            vm((fblk, half), F32),
            vm((16, width), F32),
        ),
        in_specs=[ANY] * 25,
        out_specs=[VMEM] * 10,
        scratch_shapes=[scratch],
        compiler_params=pltpu.CompilerParams(
            collective_id=0, has_side_effects=True, vmem_limit_bytes=60 << 20
        ),
        cost_estimate=pl.CostEstimate(
            flops=6 * 10**9, bytes_accessed=16 * 10**6, transcendentals=10**6
        ),
    )(queries, latents, positions, vis_ok, msk_ok, dy, w_query, w_key, w_value, w_out, w_fc1, w_fc2, *vectors)


def finish_kernel(count, *refs):
    arrays, table = refs[:count], refs[count]
    outs, rows = refs[count + 1:2 * count + 1], refs[2 * count + 1:-1]
    sems = refs[-1]
    copies = [
        pltpu.make_async_copy(src, dst, sems.at[i]) for i, (src, dst) in enumerate(zip(arrays, outs))
    ]
    for copy in copies:
        copy.start()
    width = table.shape[1]
    parts = rows[0].shape[0] // width
    for k in range(parts):
        rows[0][k * width:(k + 1) * width] = table[k, :]
    for k, row in enumerate(rows[1:]):
        row[...] = table[parts + k, :]
    for copy in copies:
        copy.wait()


def finish(arrays, table, ff, share):
    if share == 1:
        arrays = tuple(pltpu.with_memory_space_constraint(a, pltpu.VMEM) for a in arrays)
        table = pltpu.with_memory_space_constraint(table, pltpu.VMEM)
    count, width = len(arrays), table.shape[1]
    sds = jax.ShapeDtypeStruct
    vectors = table.shape[0] - ff // width
    ANY = pl.BlockSpec(memory_space=pl.ANY)
    VMEM = pl.BlockSpec(memory_space=pltpu.VMEM)
    return pl.pallas_call(
        functools.partial(finish_kernel, count),
        out_shape=tuple(sds(a.shape, a.dtype) for a in arrays)
        + (sds((ff,), F32),)
        + (sds((width,), F32),) * vectors,
        in_specs=[VMEM] * (count + 1),
        out_specs=[ANY] * count + [VMEM] * (1 + vectors),
        scratch_shapes=[pltpu.SemaphoreType.DMA((count,))],
    )(*arrays, table)


def per_device(
    queries, latents, positions, visible_valid, masked_valid,
    w_query, b_query, w_key, w_value, b_value, w_out, b_out, w_fc1, b_fc1, w_fc2, b_fc2,
    gain_query, shift_query, gain_keys, shift_keys, gain_mlp, shift_mlp, scale_attn, scale_mlp,
    out_grad,
):
    parts = lax.axis_size("dp")
    share = parts // GROUPS
    out = fused(
        share,
        (
            queries, latents, positions, visible_valid, masked_valid, out_grad,
            w_query, w_key, w_value, w_out, w_fc1, w_fc2,
            b_query, b_value, b_out, b_fc1, b_fc2,
            gain_query, shift_query, gain_keys, shift_keys, gain_mlp, shift_mlp, scale_attn, scale_mlp,
        ),
    )
    block_out, d_queries, d_latents, wq, wk, wv, wo, w1, w2, vec = out
    if share > 1:
        groups = [[n * share + i for i in range(share)] for n in range(GROUPS)]
        wq, wk, wv, wo, w1, w2 = (
            lax.psum_scatter(
                w, "dp", scatter_dimension=0, axis_index_groups=groups, tiled=True
            )
            for w in (wq, wk, wv, wo, w1, w2)
        )
        vec = lax.psum(vec, "dp", axis_index_groups=groups)
    arrays = (block_out, d_queries, d_latents, wq, wk, wv, wo, w1, w2)
    done = finish(arrays, vec, w_fc1.shape[1], share)
    block_out, d_queries, d_latents, wq, wk, wv, wo, w1, w2, b1 = done[:10]
    b2, sm, gm, hm, bo, sa, bq, bv, gq, hq, gk, hk = done[10:]
    return (
        block_out, d_queries, d_latents,
        wq, bq, wk, wv, bv, wo, bo, w1, b1, w2, b2,
        gq, hq, gk, hk, gm, hm, sa, sm,
    )


def solution(mesh):
    rows3 = P("dp", "qry", None)
    split = P("dp", "qry")
    full = P()
    return jax.shard_map(
        per_device,
        mesh=mesh,
        in_specs=(rows3, rows3, split, P("dp", None), P("dp", None)) + (full,) * 19 + (rows3,),
        out_specs=(
            rows3, rows3, rows3,
            split, full, split, split, full, split, full, split, full, split,
        ) + (full,) * 9,
        check_vma=False,
    )
```
